32 devices in a mesh: row: 4 (over y, x), seq: 8 (over z, core).
Axes of the slice: x: 2, y: 2, z: 4, core: 2. Of those that a mesh axis runs over, the one named last changes fastest.
Arguments:
- hidden: bfloat16 [4, 1536, 2048], P('row', 'seq'), may hold values from -6 to 6
- cotangent: bfloat16 [4, 1536, 2048], P('row', 'seq'), may hold values from -6 to 6
- lengths: int32 [4, 4], P('row'), may hold values from 0 to 1536, as said below
- attn_gain: bfloat16 [2048], P(('row', 'seq')), may hold values from 0.25 to 1.75
- query_down: bfloat16 [2048, 1024], P(('row', 'seq')), may hold values from -0.125 to 0.125
- latent_gain: bfloat16 [1024], P(('row', 'seq')), may hold values from 0.25 to 1.75
- query_up: bfloat16 [1024, 4096], P(('row', 'seq')), may hold values from -0.1875 to 0.1875
- key_proj: bfloat16 [2048, 256], P(('row', 'seq')), may hold values from -0.125 to 0.125
- value_proj: bfloat16 [2048, 256], P(('row', 'seq')), may hold values from -0.125 to 0.125
- out_proj: bfloat16 [4096, 2048], P(('row', 'seq')), may hold values from -0.75 to 0.75
- ffn_gain: bfloat16 [2048], P(('row', 'seq')), may hold values from 0.25 to 1.75
- gate_proj: bfloat16 [2048, 5632], P(('row', 'seq')), may hold values from -0.125 to 0.125
- up_proj: bfloat16 [2048, 5632], P(('row', 'seq')), may hold values from -0.125 to 0.125
- down_proj: bfloat16 [5632, 2048], P(('row', 'seq')), may hold values from -0.078125 to 0.078125
Outputs:
- layer_out: bfloat16 [4, 1536, 2048], P('row', 'seq')
- hidden_grad: float32 [4, 1536, 2048], P('row', 'seq')
- attn_gain_grad: float32 [2048], P(('row', 'seq'))
- query_down_grad: float32 [2048, 1024], P(('row', 'seq'))
- latent_gain_grad: float32 [1024], P(('row', 'seq'))
- query_up_grad: float32 [1024, 4096], P(('row', 'seq'))
- key_grad: float32 [2048, 256], P(('row', 'seq'))
- value_grad: float32 [2048, 256], P(('row', 'seq'))
- out_grad: float32 [4096, 2048], P(('row', 'seq'))
- ffn_gain_grad: float32 [2048], P(('row', 'seq'))
- gate_grad: float32 [2048, 5632], P(('row', 'seq'))
- up_grad: float32 [2048, 5632], P(('row', 'seq'))
- down_grad: float32 [5632, 2048], P(('row', 'seq'))
The draws below stay inside these ranges and needn't reach their ends.
Inputs may be any that keep to these rules, and one draw needn't show every extreme that they name: In each row the nonzero lengths come first, each is at least 256, and together they are at most 1536; the slots after them are padding and the remaining entries are 0. In one row, drawn from the seed, a single document fills all 1536 slots.
All inputs are finite; a program needn't handle non-finite values.
Results may differ from the reference program's by a relative error of at most 0.02.
Values may be sent and summed in bfloat16 or wider, within the bound.
A program may use at most 384 MiB of HBM per device.

```python
import math
import jax
import jax.numpy as jnp
from jax import lax

D = 2048
QLAT = 1024
HEADS = 16
HEAD_DIM = 256
FF = 5632
TOK_DEV = 192
DOCS = 4
ROWS = 4
SLOTS = 1536
N_SEQ = 8


def draw_lengths(key, part):
    key = jax.random.fold_in(key, 7)
    key_count, key_share, key_pad, key_full = jax.random.split(key, 4)
    shortest = SLOTS // 6
    doc_total = jax.random.randint(key_count, (ROWS, 1), 1, DOCS + 1)
    powers = jax.random.randint(key_share, (ROWS, DOCS), 0, 6)
    columns = jnp.arange(DOCS, dtype=jnp.int32)[None, :]
    active = columns < doc_total
    shares = jnp.where(active, jnp.left_shift(jnp.ones_like(powers), powers), 0)
    padding = jax.random.randint(key_pad, (ROWS, 1), 0, TOK_DEV + 1)
    spare = SLOTS - padding - doc_total * shortest
    extra = spare * shares // jnp.sum(shares, axis=1, keepdims=True)
    packed = jnp.where(active, shortest + extra, 0)
    full_row = jax.random.randint(key_full, (), 0, ROWS)
    row_ids = jnp.arange(ROWS, dtype=jnp.int32)[:, None]
    single = jnp.where(columns == 0, SLOTS, 0)
    result = jnp.where(row_ids == full_row, single, packed)
    return result.astype(jnp.int32)


def shard_levels(rng, dims, cuts, low, largest):
    def one(axis_at, shards_of):
        draws = jax.random.uniform(jax.random.fold_in(jax.random.fold_in(rng, 6), axis_at), (shards_of,), jnp.float32, low / len(cuts), largest / len(cuts))
        return jnp.repeat(jnp.exp(draws), dims[axis_at] // shards_of).reshape((-1,) + (1,) * (len(dims) - axis_at - 1))

    level = one(*cuts[0])
    for cut in cuts[1:]:
        level = level * one(*cut)
    return level


def normal_values(own_key, extent, width, reach, cuts=(), held_as=jnp.bfloat16):
    loudness = shard_levels(own_key, extent, cuts, -0.22, 0.18) if cuts else 1.0
    values = jax.random.normal(own_key, extent, jnp.float32) * width * loudness
    return jnp.minimum(jnp.maximum(values, -reach), reach).astype(held_as)


def setup_inputs(seed: int = 0) -> dict:
    arg_keys = jax.random.split(jax.random.key(seed), 15)
    hidden = normal_values(arg_keys[0], (ROWS, SLOTS, D), 1.0, 6.0, ((0, 4), (1, 8)))
    cotangent = normal_values(arg_keys[1], (ROWS, SLOTS, D), 1.0, 6.0, ((0, 4), (1, 8)))
    lengths = draw_lengths(jax.random.fold_in(arg_keys[14], 71), 0)
    attn_gain = jnp.clip(1.0 + 0.15 * jax.random.normal(arg_keys[3], (D,), jnp.float32), 0.25, 1.75).astype(jnp.bfloat16)
    query_down = normal_values(arg_keys[4], (D, QLAT), D ** -0.5, 0.125, ((0, 32),))
    latent_gain = jnp.clip(1.0 + 0.15 * jax.random.normal(arg_keys[5], (QLAT,), jnp.float32), 0.25, 1.75).astype(jnp.bfloat16)
    query_up = normal_values(arg_keys[6], (QLAT, HEADS * HEAD_DIM), QLAT ** -0.5, 0.1875, ((0, 32),))
    key_proj = normal_values(arg_keys[7], (D, HEAD_DIM), D ** -0.5, 0.125, ((0, 32),))
    value_proj = normal_values(arg_keys[8], (D, HEAD_DIM), D ** -0.5, 0.125, ((0, 32),))
    out_proj = normal_values(arg_keys[9], (HEADS * HEAD_DIM, D), (HEADS * HEAD_DIM // 64) ** -0.5, 0.75, ((0, 32),))
    ffn_gain = jnp.clip(1.0 + 0.15 * jax.random.normal(arg_keys[10], (D,), jnp.float32), 0.25, 1.75).astype(jnp.bfloat16)
    gate_proj = normal_values(arg_keys[11], (D, FF), D ** -0.5, 0.125, ((0, 32),))
    up_proj = normal_values(arg_keys[12], (D, FF), D ** -0.5, 0.125, ((0, 32),))
    down_proj = normal_values(arg_keys[13], (FF, D), FF ** -0.5, 0.078125, ((0, 32),))
    return dict(hidden=hidden, cotangent=cotangent, lengths=lengths, attn_gain=attn_gain, query_down=query_down, latent_gain=latent_gain, query_up=query_up, key_proj=key_proj, value_proj=value_proj, out_proj=out_proj, ffn_gain=ffn_gain, gate_proj=gate_proj, up_proj=up_proj, down_proj=down_proj)


epsilon = 1e-06
masked_value = -1e+30

@jax.custom_vjp
def low(v):
    return lax.optimization_barrier(v.astype(jnp.bfloat16)).astype(jnp.float32)

@jax.custom_vjp
def low_back(v):
    return v

def low_keep(v):
    return (low(v), None)

def low_pass(kept, grad):
    return (grad,)

def back_keep(v):
    return (v, None)

def back_low(kept, grad):
    return (low(grad),)
low.defvjp(low_keep, low_pass)
low_back.defvjp(back_keep, back_low)

def matmul(left, right):
    return jnp.dot(left, right, precision=lax.Precision.HIGHEST, preferred_element_type=jnp.float32)

def rms_norm(values, gain):
    return values * lax.rsqrt(lax.optimization_barrier(jnp.mean(values * values, axis=-1, keepdims=True)) + epsilon) * gain

def documents(doc_lens, slot_count):
    doc_ends = jnp.cumsum(doc_lens).astype(jnp.int32)
    slot_all = jnp.arange(slot_count, dtype=jnp.int32)
    is_past = slot_all[:, None] >= doc_ends[None, :]
    segment_all = lax.optimization_barrier(jnp.sum(is_past.astype(jnp.int32), axis=1)).astype(jnp.int32)
    begin_all = lax.optimization_barrier(jnp.sum(jnp.where(is_past, doc_lens[None, :], 0), axis=1)).astype(jnp.int32)
    return (segment_all, slot_all - begin_all)

def rope_tables(position, head_size):
    half_dim = head_size // 2
    frequency = jnp.exp(jnp.arange(half_dim, dtype=jnp.float32) * (-2.0 * math.log(10000.0) / head_size))
    angles = position.astype(jnp.float32)[:, None] * frequency[None, :]
    return (jnp.cos(angles), jnp.sin(angles))

def rotate(values, cosine, sine_table):
    half_dim = values.shape[-1] // 2
    front = values[..., :half_dim]
    behind = values[..., half_dim:]
    return jnp.concatenate([front * cosine - behind * sine_table, behind * cosine + front * sine_table], axis=-1)

def layer_row(residual, doc_lens, weights):
    attn_gain, query_down, latent_gain, query_up, key_proj, value_proj, out_proj, ffn_gain, gate_proj, up_proj, down_proj = weights
    slot_count = residual.shape[0]
    segment_all, position = documents(doc_lens, slot_count)
    cosine, sine_table = rope_tables(position, HEAD_DIM)
    first_low = low(rms_norm(residual, attn_gain))
    latent = low_back(matmul(first_low, query_down))
    latent_low = low(rms_norm(latent, latent_gain))
    queries = low_back(matmul(latent_low, query_up)).reshape(slot_count, HEADS, HEAD_DIM)
    queries = low(rotate(queries, cosine[:, None, :], sine_table[:, None, :]))
    key_rows = low(rotate(low_back(matmul(first_low, key_proj)), cosine, sine_table))
    value_rows = low(low_back(matmul(first_low, value_proj)))
    score_scale = HEAD_DIM ** (-0.5)
    slot_all = jnp.arange(slot_count, dtype=jnp.int32)

    def attend_block(block_pair):
        query_block, query_slots = block_pair
        query_seg = segment_all[query_slots]
        score = low_back(score_scale * jnp.einsum('thd,kd->thk', query_block, key_rows, precision=lax.Precision.HIGHEST))
        allowed = (query_seg[:, None] == segment_all[None, :]) & (slot_all[None, :] <= query_slots[:, None]) & (segment_all[None, :] < DOCS) | (slot_all[None, :] == query_slots[:, None])
        allowed = allowed[:, None, :]
        row_max = lax.optimization_barrier(jnp.max(jnp.where(allowed, score, masked_value), axis=-1, keepdims=True))
        weight = jnp.exp(jnp.where(allowed, score - row_max, masked_value))
        row_total = lax.optimization_barrier(jnp.sum(weight, axis=-1, keepdims=True))
        weighted = low_back(jnp.einsum('thk,kd->thd', low(weight), value_rows, precision=lax.Precision.HIGHEST))
        return weighted / row_total
    query_blocks = queries.reshape(N_SEQ, TOK_DEV, HEADS, HEAD_DIM)
    slot_blocks = slot_all.reshape(N_SEQ, TOK_DEV)
    attend = lax.map(jax.checkpoint(attend_block), (query_blocks, slot_blocks)).reshape(slot_count, HEADS * HEAD_DIM)
    branch = low_back(matmul(low(attend), out_proj))
    middle = residual + branch
    second_low = low(rms_norm(middle, ffn_gain))
    gate_pre = low_back(matmul(second_low, gate_proj))
    upward = low_back(matmul(second_low, up_proj))
    act_low = low(jax.nn.silu(gate_pre) * upward)
    return middle + matmul(act_low, down_proj)

def reference(hidden, cotangent, lengths, attn_gain, query_down, latent_gain, query_up, key_proj, value_proj, out_proj, ffn_gain, gate_proj, up_proj, down_proj):
    params = tuple((member.astype(jnp.float32) for member in (attn_gain, query_down, latent_gain, query_up, key_proj, value_proj, out_proj, ffn_gain, gate_proj, up_proj, down_proj)))

    def forward(residual_all, weights):

        def one_row(row_pair):
            return layer_row(row_pair[0], row_pair[1], weights)
        return lax.map(jax.checkpoint(one_row), (residual_all, lengths))
    result, pullback = jax.vjp(forward, hidden.astype(jnp.float32), params)
    grad_hidden, weight_grads = pullback(cotangent.astype(jnp.float32))
    return (result.astype(jnp.bfloat16), grad_hidden, weight_grads[0], weight_grads[1], weight_grads[2], weight_grads[3], weight_grads[4], weight_grads[5], weight_grads[6], weight_grads[7], weight_grads[8], weight_grads[9], weight_grads[10])
```

```python
import functools
import math

import jax
import jax.numpy as jnp
from jax import lax
from jax.experimental import pallas as pl
from jax.experimental.pallas import tpu as pltpu
from jax.sharding import PartitionSpec as P

epsilon = 1e-06
masked_value = -1e30
BF = jnp.bfloat16
F32 = jnp.float32
VMEM_BYTES = 60 * 1024 * 1024


def rms_forward(values, gain):
    inv_rms = lax.rsqrt(jnp.mean(values * values, axis=-1, keepdims=True) + epsilon)
    normed = values * inv_rms
    return (normed * gain, normed, inv_rms)


def rms_backward(incoming, normed, inv_rms, gain):
    grad_normed = incoming * gain
    inner = jnp.mean(grad_normed * normed, axis=-1, keepdims=True)
    return inv_rms * (grad_normed - normed * inner)


def document_positions(lengths, slots):
    ends = jnp.cumsum(lengths, axis=1)
    is_past = slots[None, :, None] >= ends[:, None, :]
    begin = jnp.sum(jnp.where(is_past, lengths[:, None, :], 0), axis=2)
    return slots[None, :] - begin


def rope_tables(position, head_size):
    half_dim = head_size // 2
    frequency = jnp.exp(jnp.arange(half_dim, dtype=F32) * (-2.0 * math.log(10000.0) / head_size))
    angles = position.astype(F32)[..., None] * frequency
    return (jnp.cos(angles), jnp.sin(angles))


def rotate(values, cosine, sine_table):
    half = values.shape[-1] // 2
    front, behind = values[..., :half], values[..., half:]
    return jnp.concatenate(
        [front * cosine - behind * sine_table, behind * cosine + front * sine_table], axis=-1
    )


def rotate_back(grads, cosine, sine_table):
    half = grads.shape[-1] // 2
    front, behind = grads[..., :half], grads[..., half:]
    return jnp.concatenate(
        [front * cosine + behind * sine_table, behind * cosine - front * sine_table], axis=-1
    )


def dot(a, b, dims):
    return lax.dot_general(a, b, (dims, ((), ())), preferred_element_type=F32)


def mm(a, b):
    return dot(a, b, ((1,), (0,)))


def mm_nt(a, b):
    return dot(a, b, ((1,), (1,)))


def mm_tn(a, b):
    return dot(a, b, ((0,), (0,)))


KEYS = 256


def visible(lens_ref, row, first_slot, tok):
    slot = first_slot + lax.broadcasted_iota(jnp.int32, (tok, 1), 0)
    low = jnp.zeros((tok, 1), jnp.int32)
    first_low = jnp.int32(0)
    end = jnp.int32(0)
    docs = lens_ref.shape[1]
    for doc in range(docs):
        end = end + lens_ref[row, doc]
        if doc < docs - 1:
            low = jnp.where(slot >= end, end, low)
            first_low = jnp.where(first_slot >= end, end, first_low)
        else:
            low = jnp.where(slot >= end, slot, low)
            first_low = jnp.where(first_slot >= end, first_slot, first_low)
    first_step = first_low // KEYS
    last_step = (first_slot + tok + KEYS - 1) // KEYS
    return (slot, low, first_step, last_step)


def stack_heads(ref_or_value, heads, head):
    return jnp.concatenate(
        [ref_or_value[:, h * head : (h + 1) * head] for h in range(heads)], axis=0
    )


def attend_kernel(
    heads, scale, lens_ref, lat_ref, qup_ref, cos_ref, sin_ref, kv_ref, q_ref, out_ref, low_ref, stats_ref, score_ref
):
    row = pl.program_id(0)
    tok = lat_ref.shape[1]
    head = kv_ref.shape[2] // 2
    first_slot = lax.axis_index("seq") * tok
    slot, low, first_step, last_step = visible(lens_ref, row, first_slot, tok)
    slot = jnp.concatenate([slot] * heads, axis=0)
    low = jnp.concatenate([low] * heads, axis=0)
    queries = mm(lat_ref[0], qup_ref[...])
    cosine, sine = cos_ref[0], sin_ref[0]
    for h in range(heads):
        q_ref[0, :, h * head : (h + 1) * head] = rotate(
            queries[:, h * head : (h + 1) * head], cosine, sine
        ).astype(BF)
    query = stack_heads(q_ref[0], heads, head)

    def keys_of(step):
        return pl.ds(pl.multiple_of(step * KEYS, KEYS), KEYS)

    def score_step(step, row_max):
        score = mm_nt(query, kv_ref[0, keys_of(step), :head]) * scale
        key_slot = step * KEYS + lax.broadcasted_iota(jnp.int32, (1, KEYS), 1)
        score = jnp.where((key_slot >= low) & (key_slot <= slot), score, masked_value)
        score_ref[step] = score
        return jnp.maximum(row_max, jnp.max(score, axis=1, keepdims=True))

    row_max = lax.fori_loop(
        first_step, last_step, score_step, jnp.full((heads * tok, 1), masked_value, F32)
    )

    def value_step(step, carry):
        row_total, weighted = carry
        weight = jnp.exp(score_ref[step] - row_max)
        row_total = row_total + jnp.sum(weight, axis=1, keepdims=True)
        weighted = weighted + mm(weight.astype(BF), kv_ref[0, keys_of(step), head:])
        return (row_total, weighted)

    row_total, weighted = lax.fori_loop(
        first_step,
        last_step,
        value_step,
        (jnp.zeros((heads * tok, 1), F32), jnp.zeros((heads * tok, head), F32)),
    )
    attend = weighted / row_total
    lane = lax.broadcasted_iota(jnp.int32, (tok, 128), 1)
    stats = jnp.zeros((tok, 128), F32)
    for h in range(heads):
        rows = slice(h * tok, (h + 1) * tok)
        out_ref[0, :, h * head : (h + 1) * head] = attend[rows]
        low_ref[0, :, h * head : (h + 1) * head] = attend[rows].astype(BF)
        stats = jnp.where(lane == h, row_max[rows], stats)
        stats = jnp.where(lane == heads + h, row_total[rows], stats)
    stats_ref[0] = stats


def attend_back_kernel(
    heads, scale, lens_ref, q_ref, kv_ref, grad_ref, out_ref, stats_ref, cos_ref, sin_ref, dq_ref, dkv_ref
):
    row = pl.program_id(0)
    tok = q_ref.shape[1]
    head = kv_ref.shape[2] // 2
    first_slot = lax.axis_index("seq") * tok
    slot, low, first_step, last_step = visible(lens_ref, row, first_slot, tok)
    slot = jnp.concatenate([slot] * heads, axis=0)
    low = jnp.concatenate([low] * heads, axis=0)
    query = stack_heads(q_ref[0], heads, head)
    grad = stack_heads(grad_ref[0], heads, head)
    attend = stack_heads(out_ref[0], heads, head)
    stats = stats_ref[0]
    row_max = jnp.concatenate([stats[:, h : h + 1] for h in range(heads)], axis=0)
    row_total = jnp.concatenate(
        [stats[:, heads + h : heads + h + 1] for h in range(heads)], axis=0
    )
    grad_weighted = (grad / row_total).astype(BF)
    delta = jnp.sum(grad * attend, axis=1, keepdims=True) / row_total
    dkv_ref[...] = jnp.zeros_like(dkv_ref)

    def step_back(step, grad_query):
        keys = pl.ds(pl.multiple_of(step * KEYS, KEYS), KEYS)
        key, value = kv_ref[0, keys, :head], kv_ref[0, keys, head:]
        score = mm_nt(query, key) * scale
        key_slot = step * KEYS + lax.broadcasted_iota(jnp.int32, (1, KEYS), 1)
        allowed = (key_slot >= low) & (key_slot <= slot)
        weight = jnp.exp(jnp.where(allowed, score - row_max, masked_value))
        grad_weight = mm_nt(grad_weighted, value)
        grad_score = (weight * (grad_weight - delta)).astype(BF)
        dkv_ref[0, keys, :head] = (mm_tn(grad_score, query) * scale).astype(BF)
        dkv_ref[0, keys, head:] = mm_tn(weight.astype(BF), grad_weighted).astype(BF)
        return grad_query + mm(grad_score, key)

    grad_query = lax.fori_loop(
        first_step, last_step, step_back, jnp.zeros((heads * tok, head), F32)
    )
    cosine, sine = cos_ref[0], sin_ref[0]
    for h in range(heads):
        dq_ref[0, :, h * head : (h + 1) * head] = rotate_back(
            grad_query[h * tok : (h + 1) * tok] * scale, cosine, sine
        ).astype(BF)


def row_block(shape):
    return pl.BlockSpec((1,) + shape[1:], lambda i: (i, 0, 0))


def whole_block(shape):
    return pl.BlockSpec(shape, lambda i: (0,) * len(shape))


def kernel_params():
    return pltpu.CompilerParams(
        dimension_semantics=("arbitrary",), vmem_limit_bytes=VMEM_BYTES
    )


def attend_forward(heads, scale, lens, lat, qup, cosine, sine, kv):
    rows, tok, _ = lat.shape
    slots = kv.shape[1]
    wide = (rows, tok, qup.shape[1])
    flops = rows * tok * (2 * lat.shape[2] * qup.shape[1] + 4 * slots * qup.shape[1])
    return pl.pallas_call(
        functools.partial(attend_kernel, heads, scale),
        grid=(rows,),
        in_specs=[pl.BlockSpec(memory_space=pltpu.SMEM)]
        + [row_block(lat.shape), whole_block(qup.shape)]
        + [row_block(cosine.shape), row_block(sine.shape), row_block(kv.shape)],
        out_specs=[row_block(wide), row_block(wide), row_block(wide), row_block((rows, tok, 128))],
        out_shape=[
            jax.ShapeDtypeStruct(wide, BF),
            jax.ShapeDtypeStruct(wide, F32),
            jax.ShapeDtypeStruct(wide, BF),
            jax.ShapeDtypeStruct((rows, tok, 128), F32),
        ],
        scratch_shapes=[pltpu.VMEM((slots // KEYS, heads * tok, KEYS), F32)],
        compiler_params=kernel_params(),
        cost_estimate=pl.CostEstimate(
            flops=flops, bytes_accessed=16 * 1024 * 1024, transcendentals=rows * tok * heads * slots
        ),
        name="attend_forward",
    )(lens, lat, qup, cosine, sine, kv)


def attend_backward(heads, scale, lens, query, kv, grad, attend, stats, cosine, sine):
    rows, tok, width = query.shape
    slots = kv.shape[1]
    return pl.pallas_call(
        functools.partial(attend_back_kernel, heads, scale),
        grid=(rows,),
        in_specs=[pl.BlockSpec(memory_space=pltpu.SMEM)]
        + [row_block(v.shape) for v in (query, kv, grad, attend, stats, cosine, sine)],
        out_specs=[row_block(query.shape), row_block(kv.shape)],
        out_shape=[
            jax.ShapeDtypeStruct(query.shape, BF),
            jax.ShapeDtypeStruct(kv.shape, BF),
        ],
        compiler_params=kernel_params(),
        cost_estimate=pl.CostEstimate(
            flops=rows * tok * 10 * slots * width,
            bytes_accessed=24 * 1024 * 1024,
            transcendentals=rows * tok * heads * slots,
        ),
        name="attend_backward",
    )(lens, query, kv, grad, attend, stats, cosine, sine)


def move_row(value, k, rows):
    return lax.ppermute(value, "row", [(i, i ^ k) for i in range(rows)])


def gather_row(value):
    rows = lax.axis_size("row")
    return jnp.stack([value] + [move_row(value, k, rows) for k in range(1, rows)])


def scatter_row(parts):
    rows = lax.axis_size("row")
    total = parts[0].astype(F32)
    for k in range(1, rows):
        total = total + move_row(parts[k].astype(BF), k, rows).astype(F32)
    return total


def scatter_seq(v, axis=0):
    return lax.psum_scatter(v.astype(BF), "seq", scatter_dimension=axis, tiled=True)


def in_row_order(pieces):
    rows, me = lax.axis_size("row"), lax.axis_index("row")
    return jnp.stack(
        [lax.select_n(me, *[pieces[j ^ i] for i in range(rows)]) for j in range(rows)]
    )


def column_slices(weight, shared=None):
    rows, me = lax.axis_size("row"), lax.axis_index("row")
    width = weight.shape[1] // rows
    pieces = []
    for k in range(rows):
        piece = lax.dynamic_slice_in_dim(weight, (me ^ k) * width, width, axis=1)
        if shared is not None:
            piece = jnp.concatenate([piece, shared], axis=1)
        pieces.append(move_row(piece, k, rows) if k else piece)
    return in_row_order(pieces)


def swap_row(blocks):
    rows, me = lax.axis_size("row"), lax.axis_index("row")
    pieces = []
    for k in range(rows):
        piece = lax.dynamic_index_in_dim(blocks, me ^ k, 0, keepdims=False)
        pieces.append(move_row(piece, k, rows) if k else piece)
    return in_row_order(pieces)


def join_columns(blocks):
    rows, n, width = blocks.shape
    return blocks.transpose(1, 0, 2).reshape(n, rows * width)


def swap_core(value):
    spread = lax.axis_size("seq")
    return lax.ppermute(value, "seq", [(i, i ^ 1) for i in range(spread)])


def pick(pair, core):
    return jnp.where(core == 0, pair[0], pair[1])


def gather_keys(key_value):
    rows, spread = lax.axis_size("row"), lax.axis_size("seq")
    core = lax.axis_index("seq") % 2
    tok, width = key_value.shape
    mine = lax.all_gather(key_value, "seq", axis=0, tiled=True).reshape(spread // 2, 2, tok, width)
    half = pick((mine[:, 0], mine[:, 1]), core)
    others = jnp.stack([move_row(half, k, rows) for k in range(1, rows)])
    theirs = swap_core(others)
    both = jnp.where(
        core == 0, jnp.stack([others, theirs], axis=2), jnp.stack([theirs, others], axis=2)
    )
    return jnp.concatenate([mine[None], both], axis=0).reshape(rows, spread * tok, width)


def scatter_keys(parts):
    rows, spread = lax.axis_size("row"), lax.axis_size("seq")
    seq_index = lax.axis_index("seq")
    core = seq_index % 2
    width = parts.shape[2]
    parts = parts.reshape(rows, spread // 2, 2, -1, width)
    even, odd = parts[:, :, 0], parts[:, :, 1]
    half = pick((even, odd), core).astype(F32) + swap_core(pick((odd, even), core)).astype(F32)
    half = scatter_row(half).astype(BF)
    chip = seq_index // 2
    total = lax.dynamic_index_in_dim(half, chip, 0, keepdims=False).astype(F32)
    chips = spread // 2
    for step in range(1, chips):
        block = lax.dynamic_index_in_dim(half, (chip + step) % chips, 0, keepdims=False)
        perm = [(i, (i + 2 * step) % spread) for i in range(spread)]
        total = total + lax.ppermute(block, "seq", perm).astype(F32)
    return total


def on_device(
    hidden,
    cotangent,
    lengths,
    attn_gain,
    query_down,
    latent_gain,
    query_up,
    key_proj,
    value_proj,
    out_proj,
    ffn_gain,
    gate_proj,
    up_proj,
    down_proj,
):
    tok = hidden.shape[1]
    model = hidden.shape[2]
    rows = lax.axis_size("row")
    spread = lax.axis_size("seq")
    row_index = lax.axis_index("row")
    seq_index = lax.axis_index("seq")
    first_slot = seq_index * tok
    head = key_proj.shape[1]
    lat = query_down.shape[1]
    heads = query_up.shape[1] // head // rows
    units = down_proj.shape[0] * spread
    scale = head ** (-0.5)
    own = query_down.shape[0]
    lat_own = latent_gain.shape[0]

    hidden_all = gather_row(hidden[0])
    lens = gather_row(lengths[0])
    first_own = jnp.concatenate([query_down, key_proj, value_proj], axis=1)
    first_width = first_own.shape[1] // rows
    gain_own = jnp.stack([attn_gain, ffn_gain, jnp.pad(latent_gain, (0, own - lat_own))], axis=1)
    first_cut = column_slices(first_own, jnp.pad(gain_own, ((0, 0), (0, 125))))
    first_set = lax.all_gather(first_cut, "seq", axis=1, tiled=True).reshape(model, -1)
    full_first = first_set[:, :first_width]
    full_gains = first_set[:, first_width:].astype(F32)
    full_again = full_gains[:, 0]
    full_fgain = full_gains[:, 1]
    full_lgain = full_gains[:, 2].reshape(rows * spread, own)[:, :lat_own].reshape(lat)
    qup_cut = column_slices(query_up)
    full_qup = lax.all_gather(qup_cut, "seq", axis=1, tiled=True).reshape(lat, -1)
    full_out = lax.all_gather(out_proj, "seq", axis=0, tiled=True)
    gate_cut = column_slices(gate_proj)
    up_cut = column_slices(up_proj)
    full_gate = lax.all_gather(gate_cut, "seq", axis=1, tiled=True).reshape(model, units)
    full_upw = lax.all_gather(up_cut, "seq", axis=1, tiled=True).reshape(model, units)
    full_down = lax.all_gather(down_proj, "seq", axis=0, tiled=True)

    position = document_positions(lens, first_slot + jnp.arange(tok, dtype=jnp.int32))
    cosine, sine = rope_tables(position, head)

    residual_all = hidden_all.astype(F32)
    normed_in, unit_in, inv_in = rms_forward(residual_all, full_again)
    first_low = normed_in.astype(BF).reshape(rows * tok, model)
    first_part = mm(first_low, full_first).reshape(rows, tok, first_width)
    grad_own, first_part = lax.optimization_barrier((cotangent[0], first_part))
    grad_all = gather_row(grad_own).reshape(rows * tok, model)
    first_out = join_columns(
        in_row_order([move_row(first_part[k], k, rows) if k else first_part[0] for k in range(rows)])
    )
    latent_normed, unit_latent, inv_latent = rms_forward(first_out[:, :lat], full_lgain)
    key_low = rotate(first_out[:, lat : lat + head], cosine[0], sine[0]).astype(BF)
    value_low = first_out[:, lat + head :].astype(BF)
    key_value = gather_keys(jnp.concatenate([key_low, value_low], axis=1))
    latent_all = gather_row(latent_normed.astype(BF))

    query_low, attend, attend_low, stats = attend_forward(
        heads, scale, lens, latent_all, full_qup, cosine, sine, key_value
    )
    latent_flat = latent_all.reshape(rows * tok, lat)
    attend_flat = attend_low.reshape(rows * tok, heads * head)
    middle = residual_all[0] + scatter_row(mm(attend_flat, full_out).reshape(rows, tok, model))

    normed_mid, unit_mid, inv_mid = rms_forward(middle, full_fgain)
    second_all = gather_row(normed_mid.astype(BF)).reshape(rows * tok, model)
    gate_pre = mm(second_all, full_gate)
    upward = mm(second_all, full_upw)
    gate_sig = jax.nn.sigmoid(gate_pre)
    gate_act = gate_pre * gate_sig
    act_low = (gate_act * upward).astype(BF)
    layer_sum = middle + scatter_row(mm(act_low, full_down).reshape(rows, tok, model))
    layer_out = layer_sum.astype(BF)[None]

    down_grad = scatter_seq(mm_tn(act_low, grad_all))
    grad_act = mm_nt(grad_all, full_down)
    slope = gate_sig * (1.0 + gate_pre * (1.0 - gate_sig))
    grad_gate = (grad_act * upward * slope).astype(BF)
    grad_upward = (grad_act * gate_act).astype(BF)
    grad_second = scatter_row(
        (mm_nt(grad_gate, full_gate) + mm_nt(grad_upward, full_upw)).reshape(rows, tok, model)
    )
    gate_part = scatter_seq(mm_tn(second_all, grad_gate).reshape(rows, model // rows, -1), 1)
    up_part = scatter_seq(mm_tn(second_all, grad_upward).reshape(rows, model // rows, -1), 1)

    ffn_gain_part = jnp.sum(grad_second * unit_mid, axis=0)
    grad_middle = cotangent[0].astype(F32) + rms_backward(
        grad_second, unit_mid, inv_mid, full_fgain
    )
    branch_all = gather_row(grad_middle.astype(BF)).reshape(rows * tok, model)
    branch_all, down_grad = lax.optimization_barrier((branch_all, down_grad))
    out_grad = scatter_seq(mm_tn(attend_flat, branch_all)).astype(F32)
    grad_attend = mm_nt(branch_all, full_out).reshape(rows, tok, heads * head)
    grad_query, kv_part = attend_backward(
        heads, scale, lens, query_low, key_value, grad_attend, attend, stats, cosine, sine
    )
    kv_sum = scatter_keys(kv_part)
    kv_sum, gate_part = lax.optimization_barrier((kv_sum, gate_part))
    grad_query = grad_query.reshape(rows * tok, heads * head)
    grad_latent_norm = scatter_row(mm_nt(grad_query, full_qup).reshape(rows, tok, lat))
    qup_part = scatter_seq(mm_tn(latent_flat, grad_query).reshape(rows, lat // rows, -1), 1)

    latent_gain_part = jnp.sum(grad_latent_norm * unit_latent, axis=0)
    grad_latent = rms_backward(grad_latent_norm, unit_latent, inv_latent, full_lgain)
    grad_key = rotate_back(kv_sum[:, :head], cosine[0], sine[0])
    grad_first_out = jnp.concatenate([grad_latent, grad_key, kv_sum[:, head:]], axis=1).astype(BF)
    pieces = []
    for k in range(rows):
        piece = lax.dynamic_slice_in_dim(
            grad_first_out, (row_index ^ k) * first_width, first_width, axis=1
        )
        pieces.append(move_row(piece, k, rows) if k else piece)
    grad_first_all = jnp.concatenate(pieces, axis=0)
    grad_first_all, up_part = lax.optimization_barrier((grad_first_all, up_part))
    grad_first_part = mm_nt(grad_first_all, full_first).reshape(rows, tok, model)
    grad_first = scatter_row(grad_first_part)
    attn_gain_part = jnp.sum(grad_first_part * unit_in, axis=(0, 1))
    hidden_grad = grad_middle + rms_backward(grad_first, unit_in[0], inv_in[0], full_again)

    lgain_part = jnp.pad(
        latent_gain_part.reshape(rows * spread, lat_own), ((0, 0), (0, own - lat_own))
    ).reshape(model)
    gain_parts = jnp.stack([attn_gain_part, ffn_gain_part, lgain_part], axis=1)
    first_term = jnp.concatenate(
        [mm_tn(first_low, grad_first_all), jnp.pad(gain_parts, ((0, 0), (0, 125)))], axis=1
    ).astype(BF)
    first_term = first_term.reshape(rows, spread, own, -1).transpose(1, 0, 2, 3)
    first_term = scatter_seq(first_term.reshape(model, -1)).reshape(rows, own, -1)
    first_back = swap_row(first_term).astype(F32)
    first_grad = join_columns(first_back[:, :, :first_width])
    gain_grad = jnp.sum(first_back[:, :, first_width:], axis=0)
    gate_grad = join_columns(swap_row(gate_part)).astype(F32)
    up_grad = join_columns(swap_row(up_part)).astype(F32)
    query_up_grad = join_columns(swap_row(qup_part)).astype(F32)
    return (
        layer_out,
        hidden_grad[None],
        gain_grad[:, 0],
        first_grad[:, :lat],
        gain_grad[:lat_own, 2],
        query_up_grad,
        first_grad[:, lat : lat + head],
        first_grad[:, lat + head :],
        out_grad,
        gain_grad[:, 1],
        gate_grad,
        up_grad,
        down_grad.astype(F32),
    )


def solution(mesh):
    token = P("row", "seq", None)
    vector = P(("row", "seq"))
    matrix = P(("row", "seq"), None)
    return jax.shard_map(
        on_device,
        mesh=mesh,
        in_specs=(token, token, P("row", None), vector, matrix, vector)
        + (matrix,) * 4
        + (vector,)
        + (matrix,) * 3,
        out_specs=(token, token, vector, matrix, vector)
        + (matrix,) * 4
        + (vector,)
        + (matrix,) * 3,
        check_vma=False,
    )
```

```python
import functools
import math

import jax
import jax.numpy as jnp
from jax import lax
from jax.experimental import pallas as pl
from jax.experimental.pallas import tpu as pltpu
from jax.sharding import PartitionSpec as P

epsilon = 1e-06
masked_value = -1e30
BF = jnp.bfloat16
F32 = jnp.float32
VMEM_BYTES = 60 * 1024 * 1024


def rms_forward(values, gain):
    inv_rms = lax.rsqrt(jnp.mean(values * values, axis=-1, keepdims=True) + epsilon)
    normed = values * inv_rms
    return (normed * gain, normed, inv_rms)


def rms_backward(incoming, normed, inv_rms, gain):
    grad_normed = incoming * gain
    inner = jnp.mean(grad_normed * normed, axis=-1, keepdims=True)
    return inv_rms * (grad_normed - normed * inner)


def document_positions(lengths, slots):
    ends = jnp.cumsum(lengths, axis=1)
    is_past = slots[None, :, None] >= ends[:, None, :]
    begin = jnp.sum(jnp.where(is_past, lengths[:, None, :], 0), axis=2)
    return slots[None, :] - begin


def rope_tables(position, head_size):
    half_dim = head_size // 2
    frequency = jnp.exp(jnp.arange(half_dim, dtype=F32) * (-2.0 * math.log(10000.0) / head_size))
    angles = position.astype(F32)[..., None] * frequency
    return (jnp.cos(angles), jnp.sin(angles))


def rotate(values, cosine, sine_table):
    half = values.shape[-1] // 2
    front, behind = values[..., :half], values[..., half:]
    return jnp.concatenate(
        [front * cosine - behind * sine_table, behind * cosine + front * sine_table], axis=-1
    )


def rotate_back(grads, cosine, sine_table):
    half = grads.shape[-1] // 2
    front, behind = grads[..., :half], grads[..., half:]
    return jnp.concatenate(
        [front * cosine + behind * sine_table, behind * cosine - front * sine_table], axis=-1
    )


def dot(a, b, dims):
    return lax.dot_general(a, b, (dims, ((), ())), preferred_element_type=F32)


def mm(a, b):
    return dot(a, b, ((1,), (0,)))


def mm_nt(a, b):
    return dot(a, b, ((1,), (1,)))


def mm_tn(a, b):
    return dot(a, b, ((0,), (0,)))


KEYS = 256


def visible(lens_ref, row, first_slot, tok):
    slot = first_slot + lax.broadcasted_iota(jnp.int32, (tok, 1), 0)
    low = jnp.zeros((tok, 1), jnp.int32)
    first_low = jnp.int32(0)
    end = jnp.int32(0)
    docs = lens_ref.shape[1]
    for doc in range(docs):
        end = end + lens_ref[row, doc]
        if doc < docs - 1:
            low = jnp.where(slot >= end, end, low)
            first_low = jnp.where(first_slot >= end, end, first_low)
        else:
            low = jnp.where(slot >= end, slot, low)
            first_low = jnp.where(first_slot >= end, first_slot, first_low)
    first_step = first_low // KEYS
    last_step = (first_slot + tok + KEYS - 1) // KEYS
    return (slot, low, first_step, last_step)


def stack_heads(ref_or_value, heads, head):
    return jnp.concatenate(
        [ref_or_value[:, h * head : (h + 1) * head] for h in range(heads)], axis=0
    )


def attend_kernel(
    heads, scale, lens_ref, lat_ref, qup_ref, cos_ref, sin_ref, kv_ref, q_ref, out_ref, low_ref, stats_ref, score_ref
):
    row = pl.program_id(0)
    tok = lat_ref.shape[1]
    head = kv_ref.shape[2] // 2
    first_slot = lax.axis_index("seq") * tok
    slot, low, first_step, last_step = visible(lens_ref, row, first_slot, tok)
    slot = jnp.concatenate([slot] * heads, axis=0)
    low = jnp.concatenate([low] * heads, axis=0)
    queries = mm(lat_ref[0], qup_ref[...])
    cosine, sine = cos_ref[0], sin_ref[0]
    for h in range(heads):
        q_ref[0, :, h * head : (h + 1) * head] = rotate(
            queries[:, h * head : (h + 1) * head], cosine, sine
        ).astype(BF)
    query = stack_heads(q_ref[0], heads, head)

    def keys_of(step):
        return pl.ds(pl.multiple_of(step * KEYS, KEYS), KEYS)

    def score_step(step, row_max):
        score = mm_nt(query, kv_ref[0, keys_of(step), :head]) * scale
        key_slot = step * KEYS + lax.broadcasted_iota(jnp.int32, (1, KEYS), 1)
        score = jnp.where((key_slot >= low) & (key_slot <= slot), score, masked_value)
        score_ref[step] = score
        return jnp.maximum(row_max, jnp.max(score, axis=1, keepdims=True))

    row_max = lax.fori_loop(
        first_step, last_step, score_step, jnp.full((heads * tok, 1), masked_value, F32)
    )

    def value_step(step, carry):
        row_total, weighted = carry
        weight = jnp.exp(score_ref[step] - row_max)
        row_total = row_total + jnp.sum(weight, axis=1, keepdims=True)
        weighted = weighted + mm(weight.astype(BF), kv_ref[0, keys_of(step), head:])
        return (row_total, weighted)

    row_total, weighted = lax.fori_loop(
        first_step,
        last_step,
        value_step,
        (jnp.zeros((heads * tok, 1), F32), jnp.zeros((heads * tok, head), F32)),
    )
    attend = weighted / row_total
    lane = lax.broadcasted_iota(jnp.int32, (tok, 128), 1)
    stats = jnp.zeros((tok, 128), F32)
    for h in range(heads):
        rows = slice(h * tok, (h + 1) * tok)
        out_ref[0, :, h * head : (h + 1) * head] = attend[rows]
        low_ref[0, :, h * head : (h + 1) * head] = attend[rows].astype(BF)
        stats = jnp.where(lane == h, row_max[rows], stats)
        stats = jnp.where(lane == heads + h, row_total[rows], stats)
    stats_ref[0] = stats


def attend_back_kernel(
    heads, scale, lens_ref, q_ref, kv_ref, branch_ref, proj_ref, out_ref, stats_ref, cos_ref, sin_ref, dq_ref, dkv_ref
):
    row = pl.program_id(0)
    tok = q_ref.shape[1]
    head = kv_ref.shape[2] // 2
    first_slot = lax.axis_index("seq") * tok
    slot, low, first_step, last_step = visible(lens_ref, row, first_slot, tok)
    slot = jnp.concatenate([slot] * heads, axis=0)
    low = jnp.concatenate([low] * heads, axis=0)
    query = stack_heads(q_ref[0], heads, head)
    branch = branch_ref[0]
    grad = jnp.concatenate(
        [mm_nt(branch, proj_ref[h * head : (h + 1) * head, :]) for h in range(heads)], axis=0
    )
    attend = stack_heads(out_ref[0], heads, head)
    stats = stats_ref[0]
    row_max = jnp.concatenate([stats[:, h : h + 1] for h in range(heads)], axis=0)
    row_total = jnp.concatenate(
        [stats[:, heads + h : heads + h + 1] for h in range(heads)], axis=0
    )
    grad_weighted = (grad / row_total).astype(BF)
    delta = jnp.sum(grad * attend, axis=1, keepdims=True) / row_total
    dkv_ref[...] = jnp.zeros_like(dkv_ref)

    def step_back(step, grad_query):
        keys = pl.ds(pl.multiple_of(step * KEYS, KEYS), KEYS)
        key, value = kv_ref[0, keys, :head], kv_ref[0, keys, head:]
        score = mm_nt(query, key) * scale
        key_slot = step * KEYS + lax.broadcasted_iota(jnp.int32, (1, KEYS), 1)
        allowed = (key_slot >= low) & (key_slot <= slot)
        weight = jnp.exp(jnp.where(allowed, score - row_max, masked_value))
        grad_weight = mm_nt(grad_weighted, value)
        grad_score = (weight * (grad_weight - delta)).astype(BF)
        dkv_ref[0, keys, :head] = (mm_tn(grad_score, query) * scale).astype(BF)
        dkv_ref[0, keys, head:] = mm_tn(weight.astype(BF), grad_weighted).astype(BF)
        return grad_query + mm(grad_score, key)

    grad_query = lax.fori_loop(
        first_step, last_step, step_back, jnp.zeros((heads * tok, head), F32)
    )
    cosine, sine = cos_ref[0], sin_ref[0]
    for h in range(heads):
        dq_ref[0, :, h * head : (h + 1) * head] = rotate_back(
            grad_query[h * tok : (h + 1) * tok] * scale, cosine, sine
        ).astype(BF)


def row_block(shape):
    return pl.BlockSpec((1,) + shape[1:], lambda i: (i, 0, 0))


def whole_block(shape):
    return pl.BlockSpec(shape, lambda i: (0,) * len(shape))


def kernel_params():
    return pltpu.CompilerParams(
        dimension_semantics=("arbitrary",), vmem_limit_bytes=VMEM_BYTES
    )


def attend_forward(heads, scale, lens, lat, qup, cosine, sine, kv):
    rows, tok, _ = lat.shape
    slots = kv.shape[1]
    wide = (rows, tok, qup.shape[1])
    flops = rows * tok * (2 * lat.shape[2] * qup.shape[1] + 4 * slots * qup.shape[1])
    return pl.pallas_call(
        functools.partial(attend_kernel, heads, scale),
        grid=(rows,),
        in_specs=[pl.BlockSpec(memory_space=pltpu.SMEM)]
        + [row_block(lat.shape), whole_block(qup.shape)]
        + [row_block(cosine.shape), row_block(sine.shape), row_block(kv.shape)],
        out_specs=[row_block(wide), row_block(wide), row_block(wide), row_block((rows, tok, 128))],
        out_shape=[
            jax.ShapeDtypeStruct(wide, BF),
            jax.ShapeDtypeStruct(wide, F32),
            jax.ShapeDtypeStruct(wide, BF),
            jax.ShapeDtypeStruct((rows, tok, 128), F32),
        ],
        scratch_shapes=[pltpu.VMEM((slots // KEYS, heads * tok, KEYS), F32)],
        compiler_params=kernel_params(),
        cost_estimate=pl.CostEstimate(
            flops=flops, bytes_accessed=16 * 1024 * 1024, transcendentals=rows * tok * heads * slots
        ),
        name="attend_forward",
    )(lens, lat, qup, cosine, sine, kv)


def attend_backward(heads, scale, lens, query, kv, branch, proj, attend, stats, cosine, sine):
    rows, tok, width = query.shape
    slots = kv.shape[1]
    return pl.pallas_call(
        functools.partial(attend_back_kernel, heads, scale),
        grid=(rows,),
        in_specs=[pl.BlockSpec(memory_space=pltpu.SMEM)]
        + [row_block(v.shape) for v in (query, kv, branch)]
        + [whole_block(proj.shape)]
        + [row_block(v.shape) for v in (attend, stats, cosine, sine)],
        out_specs=[row_block(query.shape), row_block(kv.shape)],
        out_shape=[
            jax.ShapeDtypeStruct(query.shape, BF),
            jax.ShapeDtypeStruct(kv.shape, BF),
        ],
        compiler_params=kernel_params(),
        cost_estimate=pl.CostEstimate(
            flops=rows * tok * 10 * slots * width,
            bytes_accessed=24 * 1024 * 1024,
            transcendentals=rows * tok * heads * slots,
        ),
        name="attend_backward",
    )(lens, query, kv, branch, proj, attend, stats, cosine, sine)


MESH = pl.DeviceIdType.MESH


def partners():
    row, seq = lax.axis_index("row"), lax.axis_index("seq")
    return {1: (row + 1 - 2 * (row % 2), seq), 2: ((row + 2) % 4, seq), 3: (3 - row, seq)}


def chip_partners(chips):
    row, seq = lax.axis_index("row"), lax.axis_index("seq")
    later = [(row, (seq + 2 * i) % (2 * chips)) for i in range(1, chips)]
    return later, (row, seq + 1 - 2 * (seq % 2))


def greet(devices):
    barrier = pltpu.get_barrier_semaphore()
    for device in devices:
        pl.semaphore_signal(barrier, inc=1, device_id=device, device_id_type=MESH)
    pl.semaphore_wait(barrier, len(devices))


def send(source, target, sems, at, device):
    copy = pltpu.make_async_remote_copy(
        src_ref=source,
        dst_ref=target,
        send_sem=sems[0].at[at],
        recv_sem=sems[1].at[at],
        device_id=device,
        device_id_type=MESH,
    )
    copy.start()
    return copy


TILE = 512


def reduce_rows(product, near, parts, kept, landed, sems):
    half = parts.shape[2]
    tiles = half // TILE

    def compute(k, side, store):
        def tile(t, carry):
            local = pl.ds(pl.multiple_of(t * TILE, TILE), TILE)
            columns = pl.ds(pl.multiple_of(side * half + t * TILE, TILE), TILE)
            store(local, columns, product(k, columns))
            return carry

        lax.fori_loop(0, tiles, tile, 0)

    def into_parts(at):
        def store(local, columns, value):
            parts[at, :, local] = value.astype(BF)

        return store

    def into_kept(at):
        def store(local, columns, value):
            kept[at, :, columns] = value

        return store

    copies = []

    def begin():
        for at, (k, side, to) in enumerate([(3, 0, 1), (3, 1, 2), (1, 0, 1), (2, 1, 2)]):
            compute(k, side, into_parts(at))
            copies.append(send(parts.at[at], landed.at[at], sems, at, near[to]))
        compute(2, 0, into_kept(1))
        compute(1, 1, into_kept(1))

    def pass_on():
        copies[0].wait_recv()
        parts[4] = (kept[1, :, :half] + landed[0].astype(F32)).astype(BF)
        copies.append(send(parts.at[4], landed.at[4], sems, 4, near[2]))
        copies[1].wait_recv()
        parts[5] = (kept[1, :, half:] + landed[1].astype(F32)).astype(BF)
        copies.append(send(parts.at[5], landed.at[5], sems, 5, near[1]))

    def finish():
        compute(0, 0, into_kept(0))
        compute(0, 1, into_kept(0))
        copies[2].wait_recv()
        copies[3].wait_recv()
        kept[0, :, :half] = kept[0, :, :half] + landed[2].astype(F32)
        kept[0, :, half:] = kept[0, :, half:] + landed[3].astype(F32)
        copies[4].wait_recv()
        copies[5].wait_recv()
        kept[0, :, :half] = kept[0, :, :half] + landed[4].astype(F32)
        kept[0, :, half:] = kept[0, :, half:] + landed[5].astype(F32)
        for copy in copies:
            copy.wait_send()

    return begin, pass_on, finish


def gather_rows(mine, out, near, sems, local_sem, meanwhile=None):
    tok = mine.shape[0]
    low, high = pl.ds(0, tok // 2), pl.ds(tok // 2, tok // 2)
    own = pltpu.make_async_copy(mine, out.at[0], local_sem)
    own.start()
    first = send(mine.at[low], out.at[1, low], sems, 0, near[1])
    second = send(mine.at[high], out.at[2, high], sems, 1, near[2])
    third = send(mine.at[high], out.at[1, high], sems, 2, near[1])
    fourth = send(mine.at[low], out.at[2, low], sems, 3, near[2])
    if meanwhile is not None:
        meanwhile()
    first.wait_recv()
    fifth = send(out.at[1, low], out.at[3, low], sems, 4, near[2])
    second.wait_recv()
    sixth = send(out.at[2, high], out.at[3, high], sems, 5, near[1])
    for copy in (third, fourth, fifth, sixth):
        copy.wait_recv()
    for copy in (first, second, third, fourth, fifth, sixth):
        copy.wait_send()
    own.wait()


def exchange_scratch(tok, model):
    return [
        pltpu.VMEM((6, tok, model // 2), BF),
        pltpu.VMEM((6, tok, model // 2), BF),
        pltpu.VMEM((2, tok, model), F32),
        pltpu.VMEM((tok, model), BF),
        pltpu.SemaphoreType.DMA((6,)),
        pltpu.SemaphoreType.DMA((6,)),
        pltpu.SemaphoreType.DMA((6,)),
        pltpu.SemaphoreType.DMA((6,)),
        pltpu.SemaphoreType.DMA(()),
    ]


def branch_kernel(
    attend_ref, out_proj_ref, hidden_ref, gain_ref, middle_ref, second_ref, parts, landed, kept, mine, s1, r1, s2, r2, own
):
    near = partners()
    greet([near[1], near[2]])

    def product(k, columns):
        return mm(attend_ref[k], out_proj_ref[:, columns])

    for phase in reduce_rows(product, near, parts, kept, landed, (s1, r1)):
        phase()
    middle = hidden_ref[...].astype(F32) + kept[0]
    middle_ref[...] = middle
    mine[...] = rms_forward(middle, gain_ref[...])[0].astype(BF)
    gather_rows(mine, second_ref, near, (s2, r2), own)


def second_back_kernel(
    both_ref, ffn_ref, middle_ref, cot_ref, gain_ref, grad_ref, gain_grad_ref, branch_ref, parts, landed, kept, mine, s1, r1, s2, r2, own
):
    near = partners()
    greet([near[1], near[2]])

    def product(k, columns):
        return mm_nt(both_ref[k], ffn_ref[columns, :])

    for phase in reduce_rows(product, near, parts, kept, landed, (s1, r1)):
        phase()
    grad_second = kept[0]
    gain = gain_ref[...]
    _, unit, inv = rms_forward(middle_ref[...], gain)
    gain_grad_ref[...] = jnp.sum(grad_second * unit, axis=0, keepdims=True)
    grad_middle = cot_ref[...].astype(F32) + rms_backward(grad_second, unit, inv, gain)
    grad_ref[...] = grad_middle
    mine[...] = grad_middle.astype(BF)
    gather_rows(mine, branch_ref, near, (s2, r2), own)


VMEM_SPEC = pl.BlockSpec(memory_space=pltpu.VMEM)
ANY_SPEC = pl.BlockSpec(memory_space=pl.ANY)


def remote_params(collective_id):
    return pltpu.CompilerParams(
        collective_id=collective_id, has_side_effects=True, vmem_limit_bytes=VMEM_BYTES
    )


def branch_exchange(attend, out_proj, hidden, gain):
    rows, tok, width = attend.shape
    model = out_proj.shape[1]
    return pl.pallas_call(
        branch_kernel,
        in_specs=[VMEM_SPEC] * 4,
        out_specs=[VMEM_SPEC, ANY_SPEC],
        out_shape=[
            jax.ShapeDtypeStruct((tok, model), F32),
            jax.ShapeDtypeStruct((rows, tok, model), BF),
        ],
        scratch_shapes=exchange_scratch(tok, model),
        compiler_params=remote_params(1),
        cost_estimate=pl.CostEstimate(
            flops=2 * rows * tok * width * model, bytes_accessed=190_000_000, transcendentals=0
        ),
        name="branch_exchange",
    )(attend, out_proj, hidden, gain)


def second_exchange(both, ffn, middle, cotangent, gain):
    rows, tok, units = both.shape
    model = ffn.shape[0]
    return pl.pallas_call(
        second_back_kernel,
        in_specs=[VMEM_SPEC] * 5,
        out_specs=[VMEM_SPEC, VMEM_SPEC, ANY_SPEC],
        out_shape=[
            jax.ShapeDtypeStruct((tok, model), F32),
            jax.ShapeDtypeStruct((1, model), F32),
            jax.ShapeDtypeStruct((rows, tok, model), BF),
        ],
        scratch_shapes=exchange_scratch(tok, model),
        compiler_params=remote_params(2),
        cost_estimate=pl.CostEstimate(
            flops=2 * rows * tok * units * model, bytes_accessed=190_000_000, transcendentals=0
        ),
        name="second_exchange",
    )(both, ffn, middle, cotangent, gain)


def tail_kernel(
    dq_ref, qup_ref, dkv_ref, latent_ref, lgain_ref, cos_ref, sin_ref, first_ref, hidden_ref, again_ref, layer_ref, grads_ref, lgain_part_ref, again_part_ref, layer_landed, ours, theirs, kv_landed, z_landed, parts, landed, kept, pieces, grads, sc, rc, sk, rk, sz, rz, sl, rl, sg, rg, sy, ry, own_sem
):
    rows, chips, tok, wide = ours.shape
    head = wide // 2
    lat = latent_ref.shape[1]
    width = pieces.shape[2]
    row, seq = lax.axis_index("row"), lax.axis_index("seq")
    core, chip = seq % 2, seq // 2
    near = partners()
    later, twin = chip_partners(chips)
    greet([near[1], near[2], near[3]] + later + [twin])

    swap = send(dkv_ref.at[:, :, 1 - core], theirs, (sc, rc), 0, twin)
    load = pltpu.make_async_copy(dkv_ref.at[:, :, core], ours, own_sem)
    load.start()
    left, right = slice(0, head), slice(head, wide)

    def latent_product(k, columns):
        return mm_nt(dq_ref[k], qup_ref[columns, :])

    begin, pass_on, finish = reduce_rows(latent_product, near, parts, kept, landed, (sl, rl))
    load.wait()
    swap.wait_recv()

    def add(at, side, other):
        ours[at, :, :, side] = (ours[at, :, :, side].astype(F32) + other.astype(F32)).astype(BF)

    copies = []
    for at, (k, side, to) in enumerate([(3, left, 1), (3, right, 2), (1, left, 1), (2, right, 2)]):
        add(k, side, theirs[k, :, :, side])
        copies.append(send(ours.at[k, :, :, side], kv_landed.at[at], (sk, rk), at, near[to]))
    add(2, left, theirs[2, :, :, left])
    add(1, right, theirs[1, :, :, right])
    add(0, left, theirs[0, :, :, left])
    add(0, right, theirs[0, :, :, right])
    begin()
    copies[0].wait_recv()
    add(2, left, kv_landed[0])
    copies.append(send(ours.at[2, :, :, left], kv_landed.at[4], (sk, rk), 4, near[2]))
    copies[1].wait_recv()
    add(1, right, kv_landed[1])
    copies.append(send(ours.at[1, :, :, right], kv_landed.at[5], (sk, rk), 5, near[1]))
    pass_on()
    for at, side in ((2, left), (3, right), (4, left), (5, right)):
        copies[at].wait_recv()
        add(0, side, kv_landed[at])
    along = [
        send(ours.at[0, (chip + i) % chips], z_landed.at[i - 1], (sz, rz), i - 1, later[i - 1])
        for i in range(1, chips)
    ]
    layer = [
        send(layer_ref.at[k], layer_landed.at[k - 1], (sy, ry), k - 1, near[k])
        for k in range(1, rows)
    ]
    finish()
    grad_latent_norm = kept[0]
    lgain = lgain_ref[...]
    _, unit, inv = rms_forward(latent_ref[...], lgain)
    lgain_part_ref[...] = jnp.sum(grad_latent_norm * unit, axis=0, keepdims=True)
    grad_latent = rms_backward(grad_latent_norm, unit, inv, lgain)
    total = ours[0, chip].astype(F32)
    for i in range(1, chips):
        along[i - 1].wait_recv()
        total = total + z_landed[i - 1].astype(F32)
    grad_key = rotate_back(total[:, :head], cos_ref[...], sin_ref[...])
    joined = jnp.concatenate([grad_latent, grad_key, total[:, head:]], axis=1).astype(BF)
    for j in range(rows):
        pieces[j] = joined[:, j * width : (j + 1) * width]
    last = [
        send(pieces.at[near[k][0]], grads.at[k], (sg, rg), k - 1, near[k]) for k in range(1, rows)
    ]
    grads[0] = pieces[row]
    tiles = again_ref.shape[1] // TILE
    again_part_ref[...] = jnp.zeros_like(again_part_ref)
    for k in range(rows):
        if k:
            last[k - 1].wait_recv()
        grads_ref[k] = grads[k]
        values = hidden_ref[k].astype(F32)
        scale = lax.rsqrt(jnp.mean(values * values, axis=-1, keepdims=True) + epsilon)

        def tile(t, carry):
            columns = pl.ds(pl.multiple_of(t * TILE, TILE), TILE)
            part = mm_nt(grads[k], first_ref[columns, :width])
            part = part * (hidden_ref[k, :, columns].astype(F32) * scale)
            again_part_ref[:, columns] = again_part_ref[:, columns] + jnp.sum(
                part, axis=0, keepdims=True
            )
            return carry

        lax.fori_loop(0, tiles, tile, 0)
    for copy in layer:
        copy.wait_recv()
    for copy in [swap] + copies + along + last + layer:
        copy.wait_send()


def tail_exchange(
    dq, qup, dkv, latent, lgain, cosine, sine, first_set, hidden_all, again, layer, width
):
    rows, chips, _, tok, wide = dkv.shape
    lat = latent.shape[1]
    model = again.shape[1]
    dma = pltpu.SemaphoreType.DMA
    return pl.pallas_call(
        tail_kernel,
        in_specs=[VMEM_SPEC] * 2 + [ANY_SPEC] + [VMEM_SPEC] * 7 + [ANY_SPEC],
        out_specs=[VMEM_SPEC] * 3 + [ANY_SPEC],
        out_shape=[
            jax.ShapeDtypeStruct((rows, tok, width), BF),
            jax.ShapeDtypeStruct((1, lat), F32),
            jax.ShapeDtypeStruct((1, model), F32),
            jax.ShapeDtypeStruct((rows - 1, tok, model), BF),
        ],
        scratch_shapes=[
            pltpu.VMEM((rows, chips, tok, wide), BF),
            pltpu.VMEM((rows, chips, tok, wide), BF),
            pltpu.VMEM((6, chips, tok, wide // 2), BF),
            pltpu.VMEM((chips - 1, tok, wide), BF),
            pltpu.VMEM((6, tok, lat // 2), BF),
            pltpu.VMEM((6, tok, lat // 2), BF),
            pltpu.VMEM((2, tok, lat), F32),
            pltpu.VMEM((rows, tok, width), BF),
            pltpu.VMEM((rows, tok, width), BF),
        ]
        + [dma((n,)) for n in (1, 6, chips - 1, 6, 3, 3) for _ in range(2)]
        + [dma(())],
        compiler_params=remote_params(4),
        cost_estimate=pl.CostEstimate(
            flops=2 * rows * tok * lat * qup.shape[1] + 2 * rows * tok * width * model,
            bytes_accessed=230_000_000,
            transcendentals=0,
        ),
        name="tail_exchange",
    )(dq, qup, dkv, latent, lgain, cosine, sine, first_set, hidden_all, again, layer)


def hidden_back_kernel(
    grads_ref, first_ref, hidden_ref, again_ref, middle_ref, out_ref, parts, landed, kept, s1, r1
):
    near = partners()
    greet([near[1], near[2]])
    width = grads_ref.shape[2]

    def product(k, columns):
        return mm_nt(grads_ref[k], first_ref[columns, :width])

    for phase in reduce_rows(product, near, parts, kept, landed, (s1, r1)):
        phase()
    again = again_ref[...]
    _, unit, inv = rms_forward(hidden_ref[...].astype(F32), again)
    out_ref[...] = middle_ref[...] + rms_backward(kept[0], unit, inv, again)


def hidden_exchange(grads, first_set, hidden, again, grad_middle):
    rows, tok, width = grads.shape
    model = again.shape[1]
    scratch = exchange_scratch(tok, model)
    return pl.pallas_call(
        hidden_back_kernel,
        in_specs=[VMEM_SPEC] * 5,
        out_specs=VMEM_SPEC,
        out_shape=jax.ShapeDtypeStruct((tok, model), F32),
        scratch_shapes=scratch[:3] + scratch[4:6],
        compiler_params=remote_params(5),
        cost_estimate=pl.CostEstimate(
            flops=2 * rows * tok * width * model, bytes_accessed=110_000_000, transcendentals=0
        ),
        name="hidden_exchange",
    )(grads, first_set, hidden, again, grad_middle)


def start_kernel(hidden_ref, gate_ref, up_ref, all_ref, ffn_ref, s1, r1, sg, rg, own, own_ffn):
    row = lax.axis_index("row")
    rows = all_ref.shape[0]
    units = ffn_ref.shape[2] // 2
    near = partners()
    greet([near[1], near[2], near[3]])
    cut = []

    def slices():
        for at, source_ref in ((0, gate_ref), (1, up_ref)):
            for k in range(rows):
                to = row if k == 0 else near[k][0]
                source = source_ref.at[:, pl.ds(pl.multiple_of(to * units, 128), units)]
                target = ffn_ref.at[row, :, pl.ds(at * units, units)]
                if k == 0:
                    copy = pltpu.make_async_copy(source, target, own_ffn.at[at])
                    copy.start()
                else:
                    copy = send(source, target, (sg, rg), 3 * at + k - 1, near[k])
                cut.append(copy)

    gather_rows(hidden_ref, all_ref, near, (s1, r1), own, slices)
    for copy in cut:
        copy.wait()


def start_exchange(hidden, gate, up, rows):
    dma = pltpu.SemaphoreType.DMA
    return pl.pallas_call(
        start_kernel,
        in_specs=[ANY_SPEC] * 3,
        out_specs=[ANY_SPEC] * 2,
        out_shape=[
            jax.ShapeDtypeStruct((rows,) + hidden.shape, BF),
            jax.ShapeDtypeStruct((rows, gate.shape[0], 2 * gate.shape[1] // rows), BF),
        ],
        scratch_shapes=[dma((6,))] * 4 + [dma(()), dma((2,))],
        compiler_params=remote_params(6),
        cost_estimate=pl.CostEstimate(flops=0, bytes_accessed=120_000_000, transcendentals=0),
        name="start_exchange",
    )(hidden, gate, up)


def front_kernel(
    hidden_ref, first_ref, again_ref, lgain_ref, cos_ref, sin_ref, latent_ref, lat_all_ref, kv_ref, first_low, pieces, landed, lat_mine, kv_mine, sa, ra, sl, rl, sz, rz, sr, rr, sf, rf, sc, rc, own_sem
):
    rows, tok, model = hidden_ref.shape
    chips = kv_ref.shape[1]
    width = pieces.shape[2]
    lat = latent_ref.shape[1]
    head = kv_ref.shape[4] // 2
    row, seq = lax.axis_index("row"), lax.axis_index("seq")
    core, chip = seq % 2, seq // 2
    near = partners()
    later, twin = chip_partners(chips)
    greet([near[1], near[2], near[3]] + later + [twin])

    again = again_ref[...]
    copies = []
    for k in (3, 2, 1, 0):
        first_low[...] = rms_forward(hidden_ref[k].astype(F32), again)[0].astype(BF)
        piece = mm(first_low[...], first_ref[:, :width]).astype(BF)
        if k:
            pieces[k] = piece
            copies.append(send(pieces.at[k], landed.at[row], (sa, ra), k - 1, near[k]))
        else:
            landed[row] = piece
    for copy in copies:
        copy.wait_recv()
    joined = jnp.concatenate([landed[j] for j in range(rows)], axis=1)
    key = rotate(joined[:, lat : lat + head].astype(F32), cos_ref[...], sin_ref[...])
    kv_mine[:, :head] = key.astype(BF)
    kv_mine[:, head:] = joined[:, lat + head :]

    own = pltpu.make_async_copy(kv_mine, kv_ref.at[0, chip, core], own_sem.at[0])
    own.start()
    along = [
        send(kv_mine, kv_ref.at[0, chip, core], (sz, rz), i - 1, later[i - 1])
        for i in range(1, chips)
    ]
    low, high = pl.ds(0, tok // 2), pl.ds(tok // 2, tok // 2)
    across, passed = [], []

    def block(i):
        return (chip + chips - i) % chips

    def spread(i):
        source = kv_mine if i == 0 else kv_ref.at[0, block(i), core]
        for k in (1, 2):
            across.append(
                send(source, kv_ref.at[k, block(i), core], (sr, rr), 2 * i + k - 1, near[k])
            )

    def pass_on(i):
        across[2 * i].wait_recv()
        source = kv_ref.at[1, block(i), core, low]
        passed.append(send(source, kv_ref.at[3, block(i), core, low], (sf, rf), 2 * i, near[2]))
        across[2 * i + 1].wait_recv()
        source = kv_ref.at[2, block(i), core, high]
        passed.append(
            send(source, kv_ref.at[3, block(i), core, high], (sf, rf), 2 * i + 1, near[1])
        )

    spread(0)
    latent = joined[:, :lat].astype(F32)
    latent_ref[...] = latent
    lat_mine[...] = rms_forward(latent, lgain_ref[...])[0].astype(BF)
    lat_own = pltpu.make_async_copy(lat_mine, lat_all_ref.at[0], own_sem.at[1])
    lat_own.start()
    lat_copies = [
        send(lat_mine, lat_all_ref.at[k], (sl, rl), k - 1, near[k]) for k in range(1, rows)
    ]
    for i in range(1, chips):
        along[i - 1].wait_recv()
        spread(i)
        pass_on(i - 1)
    own.wait()
    shared = [send(kv_ref.at[0, :, core], kv_ref.at[0, :, core], (sc, rc), 0, twin)]
    pass_on(chips - 1)
    for k in (1, 2):
        shared.append(send(kv_ref.at[k, :, core], kv_ref.at[k, :, core], (sc, rc), k, twin))
    for copy in passed:
        copy.wait_recv()
    shared.append(send(kv_ref.at[3, :, core], kv_ref.at[3, :, core], (sc, rc), 3, twin))
    for copy in lat_copies + shared:
        copy.wait_recv()
    for copy in copies + along + across + passed + lat_copies + shared:
        copy.wait_send()
    lat_own.wait()


def front_exchange(hidden_all, first_set, again, lgain, cosine, sine, chips, width, head):
    rows, tok, model = hidden_all.shape
    lat = lgain.shape[1]
    dma = pltpu.SemaphoreType.DMA
    pairs = [3, 3, chips - 1, 2 * chips, 2 * chips, 4]
    return pl.pallas_call(
        front_kernel,
        in_specs=[VMEM_SPEC] * 6,
        out_specs=[VMEM_SPEC, ANY_SPEC, ANY_SPEC],
        out_shape=[
            jax.ShapeDtypeStruct((tok, lat), F32),
            jax.ShapeDtypeStruct((rows, tok, lat), BF),
            jax.ShapeDtypeStruct((rows, chips, 2, tok, 2 * head), BF),
        ],
        scratch_shapes=[
            pltpu.VMEM((tok, model), BF),
            pltpu.VMEM((rows, tok, width), BF),
            pltpu.VMEM((rows, tok, width), BF),
            pltpu.VMEM((tok, lat), BF),
            pltpu.VMEM((tok, 2 * head), BF),
        ]
        + [dma((n,)) for n in pairs for _ in range(2)]
        + [dma((2,))],
        compiler_params=remote_params(3),
        cost_estimate=pl.CostEstimate(
            flops=2 * rows * tok * model * width, bytes_accessed=230_000_000, transcendentals=0
        ),
        name="front_exchange",
    )(hidden_all, first_set, again, lgain, cosine, sine)


def move_row(value, k, rows):
    return lax.ppermute(value, "row", [(i, i ^ k) for i in range(rows)])


def gather_row(value):
    rows = lax.axis_size("row")
    return jnp.stack([value] + [move_row(value, k, rows) for k in range(1, rows)])


def scatter_row(parts):
    rows = lax.axis_size("row")
    total = parts[0].astype(F32)
    for k in range(1, rows):
        total = total + move_row(parts[k].astype(BF), k, rows).astype(F32)
    return total


def scatter_seq(v, axis=0):
    return lax.psum_scatter(v.astype(BF), "seq", scatter_dimension=axis, tiled=True)


def in_row_order(pieces):
    rows, me = lax.axis_size("row"), lax.axis_index("row")
    return jnp.stack(
        [lax.select_n(me, *[pieces[j ^ i] for i in range(rows)]) for j in range(rows)]
    )


def column_slices(weight, shared=None):
    rows, me = lax.axis_size("row"), lax.axis_index("row")
    width = weight.shape[1] // rows
    pieces = []
    for k in range(rows):
        piece = lax.dynamic_slice_in_dim(weight, (me ^ k) * width, width, axis=1)
        if shared is not None:
            piece = jnp.concatenate([piece, shared], axis=1)
        pieces.append(move_row(piece, k, rows) if k else piece)
    return in_row_order(pieces)


def swap_row(blocks):
    rows, me = lax.axis_size("row"), lax.axis_index("row")
    pieces = []
    for k in range(rows):
        piece = lax.dynamic_index_in_dim(blocks, me ^ k, 0, keepdims=False)
        pieces.append(move_row(piece, k, rows) if k else piece)
    return in_row_order(pieces)


def join_columns(blocks):
    rows, n, width = blocks.shape
    return blocks.transpose(1, 0, 2).reshape(n, rows * width)


def on_device(
    hidden,
    cotangent,
    lengths,
    attn_gain,
    query_down,
    latent_gain,
    query_up,
    key_proj,
    value_proj,
    out_proj,
    ffn_gain,
    gate_proj,
    up_proj,
    down_proj,
):
    tok = hidden.shape[1]
    model = hidden.shape[2]
    rows = lax.axis_size("row")
    spread = lax.axis_size("seq")
    row_index = lax.axis_index("row")
    seq_index = lax.axis_index("seq")
    first_slot = seq_index * tok
    head = key_proj.shape[1]
    lat = query_down.shape[1]
    heads = query_up.shape[1] // head // rows
    units = down_proj.shape[0] * spread
    scale = head ** (-0.5)
    own = query_down.shape[0]
    lat_own = latent_gain.shape[0]

    hidden_all, ffn_cut = start_exchange(hidden[0], gate_proj, up_proj, rows)
    full_ffn = lax.all_gather(ffn_cut, "seq", axis=1, tiled=True).reshape(model, -1)
    full_down = lax.all_gather(down_proj, "seq", axis=0, tiled=True)
    lens = gather_row(lengths[0])
    first_own = jnp.concatenate([query_down, key_proj, value_proj], axis=1)
    first_width = first_own.shape[1] // rows
    gain_own = jnp.stack([attn_gain, ffn_gain, jnp.pad(latent_gain, (0, own - lat_own))], axis=1)
    first_cut = column_slices(first_own, jnp.pad(gain_own, ((0, 0), (0, 125))))
    first_set = lax.all_gather(first_cut, "seq", axis=1, tiled=True).reshape(model, -1)
    full_first = first_set[:, :first_width]
    full_gains = first_set[:, first_width:].astype(F32)
    full_again = full_gains[:, 0]
    full_fgain = full_gains[:, 1]
    full_lgain = full_gains[:, 2].reshape(rows * spread, own)[:, :lat_own].reshape(lat)
    qup_cut = column_slices(query_up).reshape(out_proj.shape[0], -1)
    full_oq = lax.all_gather(
        jnp.concatenate([out_proj, qup_cut], axis=1), "seq", axis=0, tiled=True
    )
    full_out = full_oq[:, :model]
    full_qup = full_oq[:, model:].reshape(spread, rows, lat_own, -1).transpose(1, 0, 2, 3)
    full_qup = full_qup.reshape(lat, heads * head)
    position = document_positions(lens, first_slot + jnp.arange(tok, dtype=jnp.int32))
    cosine, sine = rope_tables(position, head)

    residual_all = hidden_all.astype(F32)
    first_low = rms_forward(residual_all, full_again)[0].astype(BF).reshape(rows * tok, model)
    latent, latent_all, key_value = front_exchange(
        hidden_all,
        first_set,
        full_again[None],
        full_lgain[None],
        cosine[0],
        sine[0],
        spread // 2,
        first_width,
        head,
    )
    key_value = key_value.reshape(rows, spread * tok, 2 * head)
    query_low, attend, attend_low, stats = attend_forward(
        heads, scale, lens, latent_all, full_qup, cosine, sine, key_value
    )
    latent_flat = latent_all.reshape(rows * tok, lat)
    attend_flat = attend_low.reshape(rows * tok, heads * head)
    middle, second_all = branch_exchange(attend_low, full_out, hidden[0], full_fgain[None])
    grad_own, second_all = lax.optimization_barrier((cotangent[0], second_all))
    grad_all = gather_row(grad_own).reshape(rows * tok, model)
    second_all = second_all.reshape(rows * tok, model)
    both = mm(second_all, full_ffn)
    gate_pre, upward = both[:, :units], both[:, units:]
    gate_sig = jax.nn.sigmoid(gate_pre)
    gate_act = gate_pre * gate_sig
    act_low = (gate_act * upward).astype(BF)
    down_part = mm_tn(act_low, grad_all).astype(BF)
    down_part, full_down = lax.optimization_barrier((down_part, full_down))
    down_grad = scatter_seq(down_part)
    layer_part = mm(act_low, full_down)
    grad_act = mm_nt(grad_all, full_down)
    slope = gate_sig * (1.0 + gate_pre * (1.0 - gate_sig))
    grad_both = jnp.concatenate([grad_act * upward * slope, grad_act * gate_act], axis=1).astype(BF)
    ffn_part = scatter_seq(mm_tn(second_all, grad_both).reshape(rows, model // rows, -1), 1)

    grad_both, layer_part = lax.optimization_barrier((grad_both, layer_part.astype(BF)))
    grad_middle, ffn_gain_part, branch_all = second_exchange(
        grad_both.reshape(rows, tok, 2 * units), full_ffn, middle, cotangent[0], full_fgain[None]
    )
    ffn_gain_part = ffn_gain_part[0]
    out_part = mm_tn(attend_flat, branch_all.reshape(rows * tok, model)).astype(BF)
    grad_query, kv_part = attend_backward(
        heads, scale, lens, query_low, key_value, branch_all, full_out, attend, stats, cosine, sine
    )
    grad_query, out_part = lax.optimization_barrier((grad_query, out_part))
    qup_part = mm_tn(latent_flat, grad_query.reshape(rows * tok, heads * head)).astype(BF)
    qup_part = qup_part.reshape(rows, spread, lat_own, -1).transpose(1, 0, 2, 3)
    oq_part = jnp.concatenate([out_part, qup_part.reshape(lat, -1)], axis=1)
    grad_query, oq_part, down_grad = lax.optimization_barrier((grad_query, oq_part, down_grad))
    oq_part = scatter_seq(oq_part)
    layer_part = layer_part.reshape(rows, tok, model)
    grad_first_all, latent_gain_part, attn_gain_part, layer_more = tail_exchange(
        grad_query,
        full_qup,
        kv_part.reshape(rows, spread // 2, 2, tok, 2 * head),
        latent,
        full_lgain[None],
        cosine[0],
        sine[0],
        first_set,
        hidden_all,
        full_again[None],
        layer_part,
        first_width,
    )
    layer_sum = middle + layer_part[0].astype(F32) + jnp.sum(layer_more.astype(F32), axis=0)
    layer_out = layer_sum.astype(BF)
    lgain_part = jnp.pad(
        latent_gain_part.reshape(rows * spread, lat_own), ((0, 0), (0, own - lat_own))
    ).reshape(model)
    gain_parts = jnp.stack([attn_gain_part[0], ffn_gain_part, lgain_part], axis=1)
    first_term = mm_tn(first_low, grad_first_all.reshape(rows * tok, first_width))
    first_term = jnp.concatenate(
        [first_term, jnp.pad(gain_parts, ((0, 0), (0, 125)))], axis=1
    ).astype(BF)
    first_term = first_term.reshape(rows, spread, own, -1).transpose(1, 0, 2, 3)
    first_term = first_term.reshape(model, -1)
    grad_first_all, first_term, ffn_part, oq_part = lax.optimization_barrier(
        (grad_first_all, first_term, ffn_part, oq_part)
    )
    hidden_grad = hidden_exchange(
        grad_first_all, first_set, hidden[0], full_again[None], grad_middle
    )
    first_back = swap_row(scatter_seq(first_term).reshape(rows, own, -1)).astype(F32)
    first_grad = join_columns(first_back[:, :, :first_width])
    gain_grad = jnp.sum(first_back[:, :, first_width:], axis=0)
    ffn_back = swap_row(ffn_part).astype(F32)
    gate_grad = join_columns(ffn_back[:, :, :units])
    up_grad = join_columns(ffn_back[:, :, units:])
    out_grad = oq_part[:, :model].astype(F32)
    query_up_grad = join_columns(
        swap_row(oq_part[:, model:].reshape(rows, lat_own, -1))
    ).astype(F32)
    return (
        layer_out[None],
        hidden_grad[None],
        gain_grad[:, 0],
        first_grad[:, :lat],
        gain_grad[:lat_own, 2],
        query_up_grad,
        first_grad[:, lat : lat + head],
        first_grad[:, lat + head :],
        out_grad,
        gain_grad[:, 1],
        gate_grad,
        up_grad,
        down_grad.astype(F32),
    )


def solution(mesh):
    token = P("row", "seq", None)
    vector = P(("row", "seq"))
    matrix = P(("row", "seq"), None)
    return jax.shard_map(
        on_device,
        mesh=mesh,
        in_specs=(token, token, P("row", None), vector, matrix, vector)
        + (matrix,) * 4
        + (vector,)
        + (matrix,) * 3,
        out_specs=(token, token, vector, matrix, vector)
        + (matrix,) * 4
        + (vector,)
        + (matrix,) * 3,
        check_vma=False,
    )
```

```python
import functools
import math

import jax
import jax.numpy as jnp
from jax import lax
from jax.experimental import pallas as pl
from jax.experimental.pallas import tpu as pltpu
from jax.sharding import PartitionSpec as P

epsilon = 1e-06
masked_value = -1e30
BF = jnp.bfloat16
F32 = jnp.float32
VMEM_BYTES = 60 * 1024 * 1024


def rms_forward(values, gain):
    inv_rms = lax.rsqrt(jnp.mean(values * values, axis=-1, keepdims=True) + epsilon)
    normed = values * inv_rms
    return (normed * gain, normed, inv_rms)


def rms_backward(incoming, normed, inv_rms, gain):
    grad_normed = incoming * gain
    inner = jnp.mean(grad_normed * normed, axis=-1, keepdims=True)
    return inv_rms * (grad_normed - normed * inner)


def document_positions(lengths, slots):
    ends = jnp.cumsum(lengths, axis=1)
    is_past = slots[None, :, None] >= ends[:, None, :]
    begin = jnp.sum(jnp.where(is_past, lengths[:, None, :], 0), axis=2)
    return slots[None, :] - begin


def rope_tables(position, head_size):
    half_dim = head_size // 2
    frequency = jnp.exp(jnp.arange(half_dim, dtype=F32) * (-2.0 * math.log(10000.0) / head_size))
    angles = position.astype(F32)[..., None] * frequency
    return (jnp.cos(angles), jnp.sin(angles))


def rotate(values, cosine, sine_table):
    half = values.shape[-1] // 2
    front, behind = values[..., :half], values[..., half:]
    return jnp.concatenate(
        [front * cosine - behind * sine_table, behind * cosine + front * sine_table], axis=-1
    )


def rotate_back(grads, cosine, sine_table):
    half = grads.shape[-1] // 2
    front, behind = grads[..., :half], grads[..., half:]
    return jnp.concatenate(
        [front * cosine + behind * sine_table, behind * cosine - front * sine_table], axis=-1
    )


def dot(a, b, dims):
    return lax.dot_general(a, b, (dims, ((), ())), preferred_element_type=F32)


def mm(a, b):
    return dot(a, b, ((1,), (0,)))


def mm_nt(a, b):
    return dot(a, b, ((1,), (1,)))


def mm_tn(a, b):
    return dot(a, b, ((0,), (0,)))


KEYS = 256


def visible(lens_ref, row, first_slot, tok):
    slot = first_slot + lax.broadcasted_iota(jnp.int32, (tok, 1), 0)
    low = jnp.zeros((tok, 1), jnp.int32)
    first_low = jnp.int32(0)
    end = jnp.int32(0)
    docs = lens_ref.shape[1]
    for doc in range(docs):
        end = end + lens_ref[row, doc]
        if doc < docs - 1:
            low = jnp.where(slot >= end, end, low)
            first_low = jnp.where(first_slot >= end, end, first_low)
        else:
            low = jnp.where(slot >= end, slot, low)
            first_low = jnp.where(first_slot >= end, first_slot, first_low)
    first_step = first_low // KEYS
    last_step = (first_slot + tok + KEYS - 1) // KEYS
    return (slot, low, first_step, last_step)


def stack_heads(ref_or_value, heads, head):
    return jnp.concatenate(
        [ref_or_value[:, h * head : (h + 1) * head] for h in range(heads)], axis=0
    )


def attend_kernel(
    heads, scale, lens_ref, lat_ref, qup_ref, cos_ref, sin_ref, kv_ref, q_ref, out_ref, low_ref, stats_ref, score_ref
):
    row = pl.program_id(0)
    tok = lat_ref.shape[1]
    head = kv_ref.shape[2] // 2
    first_slot = lax.axis_index("seq") * tok
    slot, low, first_step, last_step = visible(lens_ref, row, first_slot, tok)
    slot = jnp.concatenate([slot] * heads, axis=0)
    low = jnp.concatenate([low] * heads, axis=0)
    queries = mm(lat_ref[0], qup_ref[...])
    cosine, sine = cos_ref[0], sin_ref[0]
    for h in range(heads):
        q_ref[0, :, h * head : (h + 1) * head] = rotate(
            queries[:, h * head : (h + 1) * head], cosine, sine
        ).astype(BF)
    query = stack_heads(q_ref[0], heads, head)

    def keys_of(step):
        return pl.ds(pl.multiple_of(step * KEYS, KEYS), KEYS)

    def score_step(step, row_max):
        score = mm_nt(query, kv_ref[0, keys_of(step), :head]) * scale
        key_slot = step * KEYS + lax.broadcasted_iota(jnp.int32, (1, KEYS), 1)
        score = jnp.where((key_slot >= low) & (key_slot <= slot), score, masked_value)
        score_ref[step] = score
        return jnp.maximum(row_max, jnp.max(score, axis=1, keepdims=True))

    row_max = lax.fori_loop(
        first_step, last_step, score_step, jnp.full((heads * tok, 1), masked_value, F32)
    )

    def value_step(step, carry):
        row_total, weighted = carry
        weight = jnp.exp(score_ref[step] - row_max)
        row_total = row_total + jnp.sum(weight, axis=1, keepdims=True)
        weighted = weighted + mm(weight.astype(BF), kv_ref[0, keys_of(step), head:])
        return (row_total, weighted)

    row_total, weighted = lax.fori_loop(
        first_step,
        last_step,
        value_step,
        (jnp.zeros((heads * tok, 1), F32), jnp.zeros((heads * tok, head), F32)),
    )
    attend = weighted / row_total
    lane = lax.broadcasted_iota(jnp.int32, (tok, 128), 1)
    stats = jnp.zeros((tok, 128), F32)
    for h in range(heads):
        rows = slice(h * tok, (h + 1) * tok)
        out_ref[0, :, h * head : (h + 1) * head] = attend[rows]
        low_ref[0, :, h * head : (h + 1) * head] = attend[rows].astype(BF)
        stats = jnp.where(lane == h, row_max[rows], stats)
        stats = jnp.where(lane == heads + h, row_total[rows], stats)
    stats_ref[0] = stats


def attend_back_kernel(
    heads, scale, lens_ref, q_ref, kv_ref, branch_ref, proj_ref, branch_all_ref, low_ref, lat_ref, out_ref, stats_ref, cos_ref, sin_ref, dq_ref, dkv_ref, oq_ref, dq_all
):
    row = pl.program_id(0)
    tok = q_ref.shape[1]
    head = kv_ref.shape[2] // 2
    first_slot = lax.axis_index("seq") * tok
    slot, low, first_step, last_step = visible(lens_ref, row, first_slot, tok)
    slot = jnp.concatenate([slot] * heads, axis=0)
    low = jnp.concatenate([low] * heads, axis=0)
    query = stack_heads(q_ref[0], heads, head)
    branch = branch_ref[0]
    grad = jnp.concatenate(
        [mm_nt(branch, proj_ref[h * head : (h + 1) * head, :]) for h in range(heads)], axis=0
    )
    attend = stack_heads(out_ref[0], heads, head)
    stats = stats_ref[0]
    row_max = jnp.concatenate([stats[:, h : h + 1] for h in range(heads)], axis=0)
    row_total = jnp.concatenate(
        [stats[:, heads + h : heads + h + 1] for h in range(heads)], axis=0
    )
    grad_weighted = (grad / row_total).astype(BF)
    delta = jnp.sum(grad * attend, axis=1, keepdims=True) / row_total
    dkv_ref[...] = jnp.zeros_like(dkv_ref)

    def step_back(step, grad_query):
        keys = pl.ds(pl.multiple_of(step * KEYS, KEYS), KEYS)
        key, value = kv_ref[0, keys, :head], kv_ref[0, keys, head:]
        score = mm_nt(query, key) * scale
        key_slot = step * KEYS + lax.broadcasted_iota(jnp.int32, (1, KEYS), 1)
        allowed = (key_slot >= low) & (key_slot <= slot)
        weight = jnp.exp(jnp.where(allowed, score - row_max, masked_value))
        grad_weight = mm_nt(grad_weighted, value)
        grad_score = (weight * (grad_weight - delta)).astype(BF)
        dkv_ref[0, keys, :head] = (mm_tn(grad_score, query) * scale).astype(BF)
        dkv_ref[0, keys, head:] = mm_tn(weight.astype(BF), grad_weighted).astype(BF)
        return grad_query + mm(grad_score, key)

    grad_query = lax.fori_loop(
        first_step, last_step, step_back, jnp.zeros((heads * tok, head), F32)
    )
    cosine, sine = cos_ref[0], sin_ref[0]
    for h in range(heads):
        dq_ref[0, :, h * head : (h + 1) * head] = rotate_back(
            grad_query[h * tok : (h + 1) * tok] * scale, cosine, sine
        ).astype(BF)
        dq_all[row, :, h * head : (h + 1) * head] = dq_ref[0, :, h * head : (h + 1) * head]

    @pl.when(row == pl.num_programs(0) - 1)
    def _():
        weight_grads(low_ref, branch_all_ref, lat_ref, dq_all, oq_ref)


def weight_grads(low_ref, branch_ref, lat_ref, dq_ref, oq_ref):
    model, width = branch_ref.shape[2], dq_ref.shape[2]
    lat = lat_ref.shape[2]
    rows, spread = lax.axis_size("row"), lax.axis_size("seq")
    own = lat // rows // spread
    right = branch_ref[...].reshape(-1, model)
    tile = 256

    def out_tile(t, carry):
        at = pl.ds(pl.multiple_of(t * tile, tile), tile)
        left = low_ref[:, :, at].reshape(-1, tile)
        oq_ref[at, :model] = mm_tn(left, right).astype(BF)
        return carry

    lax.fori_loop(0, low_ref.shape[2] // tile, out_tile, 0)
    right_lat = dq_ref[...].reshape(-1, width)
    block = lat // rows
    if own % 16 == 0:
        for r in range(rows):
            left = lat_ref[:, :, r * block : (r + 1) * block].reshape(-1, block)
            product = mm_tn(left, right_lat).astype(BF)
            for seq in range(spread):
                at = (seq * rows + r) * own
                oq_ref[at : at + own, model:] = product[seq * own : (seq + 1) * own]
    else:
        product = mm_tn(lat_ref[...].reshape(-1, lat), right_lat)
        for seq in range(spread):
            pieces = [
                product[(r * spread + seq) * own : (r * spread + seq + 1) * own] for r in range(rows)
            ]
            oq_ref[seq * rows * own : (seq + 1) * rows * own, model:] = jnp.concatenate(
                pieces, axis=0
            ).astype(BF)


def row_block(shape):
    return pl.BlockSpec((1,) + shape[1:], lambda i: (i, 0, 0))


def whole_block(shape):
    return pl.BlockSpec(shape, lambda i: (0,) * len(shape))


def kernel_params():
    return pltpu.CompilerParams(
        dimension_semantics=("arbitrary",), vmem_limit_bytes=VMEM_BYTES
    )


def attend_forward(heads, scale, lens, lat, qup, cosine, sine, kv):
    rows, tok, _ = lat.shape
    slots = kv.shape[1]
    wide = (rows, tok, qup.shape[1])
    flops = rows * tok * (2 * lat.shape[2] * qup.shape[1] + 4 * slots * qup.shape[1])
    return pl.pallas_call(
        functools.partial(attend_kernel, heads, scale),
        grid=(rows,),
        in_specs=[pl.BlockSpec(memory_space=pltpu.SMEM)]
        + [row_block(lat.shape), whole_block(qup.shape)]
        + [row_block(cosine.shape), row_block(sine.shape), row_block(kv.shape)],
        out_specs=[row_block(wide), row_block(wide), row_block(wide), row_block((rows, tok, 128))],
        out_shape=[
            jax.ShapeDtypeStruct(wide, BF),
            jax.ShapeDtypeStruct(wide, F32),
            jax.ShapeDtypeStruct(wide, BF),
            jax.ShapeDtypeStruct((rows, tok, 128), F32),
        ],
        scratch_shapes=[pltpu.VMEM((slots // KEYS, heads * tok, KEYS), F32)],
        compiler_params=kernel_params(),
        cost_estimate=pl.CostEstimate(
            flops=flops, bytes_accessed=16 * 1024 * 1024, transcendentals=rows * tok * heads * slots
        ),
        name="attend_forward",
    )(lens, lat, qup, cosine, sine, kv)


def attend_backward(
    heads, scale, lens, query, kv, branch, oq, low, lat, attend, stats, cosine, sine
):
    rows, tok, width = query.shape
    model = branch.shape[2]
    slots = kv.shape[1]
    return pl.pallas_call(
        functools.partial(attend_back_kernel, heads, scale),
        grid=(rows,),
        in_specs=[pl.BlockSpec(memory_space=pltpu.SMEM)]
        + [row_block(v.shape) for v in (query, kv, branch)]
        + [pl.BlockSpec((width, model), lambda i: (0, 0), pipeline_mode=pl.Buffered(1))]
        + [
            pl.BlockSpec(v.shape, lambda i: (0, 0, 0), pipeline_mode=pl.Buffered(1))
            for v in (branch, low, lat)
        ]
        + [row_block(v.shape) for v in (attend, stats, cosine, sine)],
        out_specs=[row_block(query.shape), row_block(kv.shape)]
        + [pl.BlockSpec(oq.shape, lambda i: (0, 0), pipeline_mode=pl.Buffered(1))],
        out_shape=[
            jax.ShapeDtypeStruct(query.shape, BF),
            jax.ShapeDtypeStruct(kv.shape, BF),
            jax.ShapeDtypeStruct(oq.shape, BF),
        ],
        scratch_shapes=[pltpu.VMEM(query.shape, BF)],
        compiler_params=kernel_params(),
        cost_estimate=pl.CostEstimate(
            flops=rows * tok * 10 * slots * width,
            bytes_accessed=100_000_000,
            transcendentals=rows * tok * heads * slots,
        ),
        name="attend_backward",
    )(lens, query, kv, branch, oq, branch, low, lat, attend, stats, cosine, sine)


MESH = pl.DeviceIdType.MESH


def partners():
    row, seq = lax.axis_index("row"), lax.axis_index("seq")
    return {1: (row + 1 - 2 * (row % 2), seq), 2: ((row + 2) % 4, seq), 3: (3 - row, seq)}


def chip_partners(chips):
    row, seq = lax.axis_index("row"), lax.axis_index("seq")
    later = [(row, (seq + 2 * i) % (2 * chips)) for i in range(1, chips)]
    return later, (row, seq + 1 - 2 * (seq % 2))


def greet(devices):
    barrier = pltpu.get_barrier_semaphore()
    for device in devices:
        pl.semaphore_signal(barrier, inc=1, device_id=device, device_id_type=MESH)
    pl.semaphore_wait(barrier, len(devices))


def send(source, target, sems, at, device):
    copy = pltpu.make_async_remote_copy(
        src_ref=source,
        dst_ref=target,
        send_sem=sems[0].at[at],
        recv_sem=sems[1].at[at],
        device_id=device,
        device_id_type=MESH,
    )
    copy.start()
    return copy


TILE = 512


def reduce_rows(product, near, parts, kept, landed, sems, ready=None):
    half = parts.shape[2]
    tiles = half // TILE

    def compute(k, side, store):
        if ready is not None:
            ready(k, side)

        def tile(t, carry):
            local = pl.ds(pl.multiple_of(t * TILE, TILE), TILE)
            columns = pl.ds(pl.multiple_of(side * half + t * TILE, TILE), TILE)
            store(local, columns, product(k, columns))
            return carry

        lax.fori_loop(0, tiles, tile, 0)

    def into_parts(at):
        def store(local, columns, value):
            parts[at, :, local] = value.astype(BF)

        return store

    def into_kept(at):
        def store(local, columns, value):
            kept[at, :, columns] = value

        return store

    copies = []

    def begin():
        for at, (k, side, to) in enumerate([(3, 0, 1), (3, 1, 2), (1, 0, 1), (2, 1, 2)]):
            compute(k, side, into_parts(at))
            copies.append(send(parts.at[at], landed.at[at], sems, at, near[to]))
        compute(2, 0, into_kept(1))
        compute(1, 1, into_kept(1))

    def pass_on():
        copies[0].wait_recv()
        parts[4] = (kept[1, :, :half] + landed[0].astype(F32)).astype(BF)
        copies.append(send(parts.at[4], landed.at[4], sems, 4, near[2]))
        copies[1].wait_recv()
        parts[5] = (kept[1, :, half:] + landed[1].astype(F32)).astype(BF)
        copies.append(send(parts.at[5], landed.at[5], sems, 5, near[1]))

    def finish():
        compute(0, 0, into_kept(0))
        compute(0, 1, into_kept(0))
        copies[2].wait_recv()
        copies[3].wait_recv()
        kept[0, :, :half] = kept[0, :, :half] + landed[2].astype(F32)
        kept[0, :, half:] = kept[0, :, half:] + landed[3].astype(F32)
        copies[4].wait_recv()
        copies[5].wait_recv()
        kept[0, :, :half] = kept[0, :, :half] + landed[4].astype(F32)
        kept[0, :, half:] = kept[0, :, half:] + landed[5].astype(F32)
        for copy in copies:
            copy.wait_send()

    return begin, pass_on, finish


def gather_rows(mine, out, near, sems, local_sem, meanwhile=None):
    tok = mine.shape[0]
    low, high = pl.ds(0, tok // 2), pl.ds(tok // 2, tok // 2)
    own = pltpu.make_async_copy(mine, out.at[0], local_sem)
    own.start()
    first = send(mine.at[low], out.at[1, low], sems, 0, near[1])
    second = send(mine.at[high], out.at[2, high], sems, 1, near[2])
    third = send(mine.at[high], out.at[1, high], sems, 2, near[1])
    fourth = send(mine.at[low], out.at[2, low], sems, 3, near[2])
    if meanwhile is not None:
        meanwhile()
    first.wait_recv()
    fifth = send(out.at[1, low], out.at[3, low], sems, 4, near[2])
    second.wait_recv()
    sixth = send(out.at[2, high], out.at[3, high], sems, 5, near[1])
    for copy in (third, fourth, fifth, sixth):
        copy.wait_recv()
    for copy in (first, second, third, fourth, fifth, sixth):
        copy.wait_send()
    own.wait()


def exchange_scratch(tok, model):
    return [
        pltpu.VMEM((6, tok, model // 2), BF),
        pltpu.VMEM((6, tok, model // 2), BF),
        pltpu.VMEM((2, tok, model), F32),
        pltpu.VMEM((tok, model), BF),
        pltpu.SemaphoreType.DMA((6,)),
        pltpu.SemaphoreType.DMA((6,)),
        pltpu.SemaphoreType.DMA((6,)),
        pltpu.SemaphoreType.DMA((6,)),
        pltpu.SemaphoreType.DMA(()),
    ]


def branch_kernel(
    attend_ref, out_proj_ref, hidden_ref, gain_ref, middle_ref, second_ref, parts, landed, kept, mine, s1, r1, s2, r2, own
):
    near = partners()
    greet([near[1], near[2]])

    def product(k, columns):
        return mm(attend_ref[k], out_proj_ref[:, columns])

    for phase in reduce_rows(product, near, parts, kept, landed, (s1, r1)):
        phase()
    middle = hidden_ref[...].astype(F32) + kept[0]
    middle_ref[...] = middle
    mine[...] = rms_forward(middle, gain_ref[...])[0].astype(BF)
    gather_rows(mine, second_ref, near, (s2, r2), own)


def second_back_kernel(
    both_hbm, ffn_hbm, act_hbm, down_hbm, middle_ref, cot_ref, gain_ref, order_ref, grad_ref, gain_grad_ref, branch_ref, layer_ref, parts, landed, kept, mine, s1, r1, s2, r2, own, both_ref, ffn_ref, act_ref, down_ref, load_sems
):
    del order_ref
    half = ffn_ref.shape[0] // 2
    loads = {}

    def load(name, source, target):
        loads[name] = pltpu.make_async_copy(source, target, load_sems.at[len(loads)])
        loads[name].start()

    load(("both", 3), both_hbm.at[3], both_ref.at[3])
    for side in (0, 1):
        rows = pl.ds(side * half, half)
        load(("ffn", side), ffn_hbm.at[rows], ffn_ref.at[rows])
    for k in (1, 2, 0):
        load(("both", k), both_hbm.at[k], both_ref.at[k])
    load("act", act_hbm, act_ref)
    load("down", down_hbm, down_ref)
    waited = set()

    def loaded(*names):
        for name in names:
            if name not in waited:
                waited.add(name)
                loads[name].wait()

    def ready(k, side):
        loaded(("both", k), ("ffn", side))

    near = partners()
    greet([near[1], near[2]])

    def product(k, columns):
        return mm_nt(both_ref[k], ffn_ref[columns, :])

    begin, pass_on, finish = reduce_rows(product, near, parts, kept, landed, (s1, r1), ready)
    begin()
    pass_on()
    loaded("act", "down")
    for k in range(act_ref.shape[0]):

        def tile(t, carry, k=k):
            columns = pl.ds(pl.multiple_of(t * TILE, TILE), TILE)
            layer_ref[k, :, columns] = mm(act_ref[k], down_ref[:, columns]).astype(BF)
            return carry

        lax.fori_loop(0, down_ref.shape[1] // TILE, tile, 0)
    finish()
    grad_second = kept[0]
    gain = gain_ref[...]
    _, unit, inv = rms_forward(middle_ref[...], gain)
    gain_grad_ref[...] = jnp.sum(grad_second * unit, axis=0, keepdims=True)
    grad_middle = cot_ref[...].astype(F32) + rms_backward(grad_second, unit, inv, gain)
    grad_ref[...] = grad_middle
    mine[...] = grad_middle.astype(BF)
    gather_rows(mine, branch_ref, near, (s2, r2), own)


VMEM_SPEC = pl.BlockSpec(memory_space=pltpu.VMEM)
ANY_SPEC = pl.BlockSpec(memory_space=pl.ANY)


def remote_params(collective_id):
    return pltpu.CompilerParams(
        collective_id=collective_id, has_side_effects=True, vmem_limit_bytes=VMEM_BYTES
    )


def branch_exchange(attend, out_proj, hidden, gain):
    rows, tok, width = attend.shape
    model = hidden.shape[1]
    return pl.pallas_call(
        branch_kernel,
        in_specs=[VMEM_SPEC] * 4,
        out_specs=[VMEM_SPEC, ANY_SPEC],
        out_shape=[
            jax.ShapeDtypeStruct((tok, model), F32),
            jax.ShapeDtypeStruct((rows, tok, model), BF),
        ],
        scratch_shapes=exchange_scratch(tok, model),
        compiler_params=remote_params(1),
        cost_estimate=pl.CostEstimate(
            flops=2 * rows * tok * width * model, bytes_accessed=190_000_000, transcendentals=0
        ),
        name="branch_exchange",
    )(attend, out_proj, hidden, gain)


def second_exchange(both, ffn, act, down, middle, cotangent, gain, order):
    rows, tok, units = both.shape
    model = ffn.shape[0]
    return pl.pallas_call(
        second_back_kernel,
        in_specs=[ANY_SPEC] * 4 + [VMEM_SPEC] * 3 + [ANY_SPEC],
        out_specs=[VMEM_SPEC, VMEM_SPEC, ANY_SPEC, VMEM_SPEC],
        out_shape=[
            jax.ShapeDtypeStruct((tok, model), F32),
            jax.ShapeDtypeStruct((1, model), F32),
            jax.ShapeDtypeStruct((rows, tok, model), BF),
            jax.ShapeDtypeStruct((rows, tok, model), BF),
        ],
        scratch_shapes=exchange_scratch(tok, model)
        + [pltpu.VMEM(v.shape, BF) for v in (both, ffn, act, down)]
        + [pltpu.SemaphoreType.DMA((8,))],
        compiler_params=remote_params(2),
        cost_estimate=pl.CostEstimate(
            flops=2 * rows * tok * units * model, bytes_accessed=190_000_000, transcendentals=0
        ),
        name="second_exchange",
    )(both, ffn, act, down, middle, cotangent, gain, order)


def tail_kernel(
    dq_ref, qup_ref, dkv_ref, latent_ref, lgain_ref, cos_ref, sin_ref, first_ref, hidden_ref, again_ref, grads_ref, lgain_part_ref, again_part_ref, ours, theirs, kv_landed, z_landed, parts, landed, kept, pieces, grads, sc, rc, sk, rk, sz, rz, sl, rl, sg, rg, own_sem
):
    rows, chips, tok, wide = ours.shape
    head = wide // 2
    lat = latent_ref.shape[1]
    width = pieces.shape[2]
    row, seq = lax.axis_index("row"), lax.axis_index("seq")
    core, chip = seq % 2, seq // 2
    near = partners()
    later, twin = chip_partners(chips)
    greet([near[1], near[2], near[3]] + later + [twin])

    swap = send(dkv_ref.at[:, :, 1 - core], theirs, (sc, rc), 0, twin)
    load = pltpu.make_async_copy(dkv_ref.at[:, :, core], ours, own_sem)
    load.start()
    left, right = slice(0, head), slice(head, wide)

    def latent_product(k, columns):
        return mm_nt(dq_ref[k], qup_ref[columns, :])

    begin, pass_on, finish = reduce_rows(latent_product, near, parts, kept, landed, (sl, rl))
    load.wait()
    swap.wait_recv()

    def add(at, side, other):
        ours[at, :, :, side] = (ours[at, :, :, side].astype(F32) + other.astype(F32)).astype(BF)

    copies = []
    for at, (k, side, to) in enumerate([(3, left, 1), (3, right, 2), (1, left, 1), (2, right, 2)]):
        add(k, side, theirs[k, :, :, side])
        copies.append(send(ours.at[k, :, :, side], kv_landed.at[at], (sk, rk), at, near[to]))
    add(2, left, theirs[2, :, :, left])
    add(1, right, theirs[1, :, :, right])
    add(0, left, theirs[0, :, :, left])
    add(0, right, theirs[0, :, :, right])
    begin()
    copies[0].wait_recv()
    add(2, left, kv_landed[0])
    copies.append(send(ours.at[2, :, :, left], kv_landed.at[4], (sk, rk), 4, near[2]))
    copies[1].wait_recv()
    add(1, right, kv_landed[1])
    copies.append(send(ours.at[1, :, :, right], kv_landed.at[5], (sk, rk), 5, near[1]))
    pass_on()
    for at, side in ((2, left), (3, right), (4, left), (5, right)):
        copies[at].wait_recv()
        add(0, side, kv_landed[at])
    along = [
        send(ours.at[0, (chip + i) % chips], z_landed.at[i - 1], (sz, rz), i - 1, later[i - 1])
        for i in range(1, chips)
    ]
    finish()
    grad_latent_norm = kept[0]
    lgain = lgain_ref[...]
    _, unit, inv = rms_forward(latent_ref[...], lgain)
    lgain_part_ref[...] = jnp.sum(grad_latent_norm * unit, axis=0, keepdims=True)
    grad_latent = rms_backward(grad_latent_norm, unit, inv, lgain)
    total = ours[0, chip].astype(F32)
    for i in range(1, chips):
        along[i - 1].wait_recv()
        total = total + z_landed[i - 1].astype(F32)
    grad_key = rotate_back(total[:, :head], cos_ref[...], sin_ref[...])
    joined = jnp.concatenate([grad_latent, grad_key, total[:, head:]], axis=1).astype(BF)
    for j in range(rows):
        pieces[j] = joined[:, j * width : (j + 1) * width]
    last = [
        send(pieces.at[near[k][0]], grads.at[k], (sg, rg), k - 1, near[k]) for k in range(1, rows)
    ]
    grads[0] = pieces[row]
    tiles = again_ref.shape[1] // TILE
    again_part_ref[...] = jnp.zeros_like(again_part_ref)
    for k in range(rows):
        if k:
            last[k - 1].wait_recv()
        grads_ref[k] = grads[k]
        values = hidden_ref[k].astype(F32)
        scale = lax.rsqrt(jnp.mean(values * values, axis=-1, keepdims=True) + epsilon)

        def tile(t, carry):
            columns = pl.ds(pl.multiple_of(t * TILE, TILE), TILE)
            part = mm_nt(grads[k], first_ref[columns, :width])
            part = part * (hidden_ref[k, :, columns].astype(F32) * scale)
            again_part_ref[:, columns] = again_part_ref[:, columns] + jnp.sum(
                part, axis=0, keepdims=True
            )
            return carry

        lax.fori_loop(0, tiles, tile, 0)
    for copy in [swap] + copies + along + last:
        copy.wait_send()


def tail_exchange(
    dq, qup, dkv, latent, lgain, cosine, sine, first_set, hidden_all, again, width
):
    rows, chips, _, tok, wide = dkv.shape
    lat = latent.shape[1]
    model = again.shape[1]
    dma = pltpu.SemaphoreType.DMA
    return pl.pallas_call(
        tail_kernel,
        in_specs=[VMEM_SPEC] * 2 + [ANY_SPEC] + [VMEM_SPEC] * 7,
        out_specs=[VMEM_SPEC] * 3,
        out_shape=[
            jax.ShapeDtypeStruct((rows, tok, width), BF),
            jax.ShapeDtypeStruct((1, lat), F32),
            jax.ShapeDtypeStruct((1, model), F32),
        ],
        scratch_shapes=[
            pltpu.VMEM((rows, chips, tok, wide), BF),
            pltpu.VMEM((rows, chips, tok, wide), BF),
            pltpu.VMEM((6, chips, tok, wide // 2), BF),
            pltpu.VMEM((chips - 1, tok, wide), BF),
            pltpu.VMEM((6, tok, lat // 2), BF),
            pltpu.VMEM((6, tok, lat // 2), BF),
            pltpu.VMEM((2, tok, lat), F32),
            pltpu.VMEM((rows, tok, width), BF),
            pltpu.VMEM((rows, tok, width), BF),
        ]
        + [dma((n,)) for n in (1, 6, chips - 1, 6, 3) for _ in range(2)]
        + [dma(())],
        compiler_params=remote_params(4),
        cost_estimate=pl.CostEstimate(
            flops=2 * rows * tok * lat * qup.shape[1] + 2 * rows * tok * width * model,
            bytes_accessed=230_000_000,
            transcendentals=0,
        ),
        name="tail_exchange",
    )(dq, qup, dkv, latent, lgain, cosine, sine, first_set, hidden_all, again)


def hidden_back_kernel(
    grads_ref, first_ref, hidden_ref, again_ref, middle_ref, term_ref, ffn_ref, out_ref, grad_ref, gain_ref, ffn_back, parts, landed, kept, ours, theirs, z_landed, total, back, s1, r1, sc, rc, sz, rz, sb, rb, sg, rg, own, own_ffn
):
    rows, chips = ours.shape[:2]
    width = grads_ref.shape[2]
    row, seq = lax.axis_index("row"), lax.axis_index("seq")
    core, chip = seq % 2, seq // 2
    near = partners()
    later, twin = chip_partners(chips)
    greet([near[1], near[2], near[3]] + later + [twin])
    swap = send(term_ref.at[:, :, 1 - core], theirs, (sc, rc), 0, twin)
    load = pltpu.make_async_copy(term_ref.at[:, :, core], ours, own)
    load.start()

    def product(k, columns):
        return mm_nt(grads_ref[k], first_ref[columns, :width])

    begin, pass_on, finish = reduce_rows(product, near, parts, kept, landed, (s1, r1))
    keep = pltpu.make_async_copy(ffn_ref.at[row], ffn_back.at[row], own_ffn)
    keep.start()
    begin()
    load.wait()
    swap.wait_recv()
    ours[...] = (ours[...].astype(F32) + theirs[...].astype(F32)).astype(BF)
    pass_on()
    along = [
        send(ours.at[:, (chip + i) % chips], z_landed.at[i - 1], (sz, rz), i - 1, later[i - 1])
        for i in range(1, chips)
    ]
    slices = [
        send(ffn_ref.at[near[k][0]], ffn_back.at[row], (sg, rg), k - 1, near[k])
        for k in range(1, rows)
    ]
    finish()
    again = again_ref[...]
    _, unit, inv = rms_forward(hidden_ref[...].astype(F32), again)
    out_ref[...] = middle_ref[...] + rms_backward(kept[0], unit, inv, again)
    sums = ours[:, chip].astype(F32)
    for i in range(1, chips):
        along[i - 1].wait_recv()
        sums = sums + z_landed[i - 1].astype(F32)
    total[...] = sums.astype(BF)
    last = [
        send(total.at[near[k][0]], back.at[row], (sb, rb), k - 1, near[k]) for k in range(1, rows)
    ]
    back[row] = total[row]
    for copy in last:
        copy.wait_recv()
    gain_ref[...] = jnp.zeros_like(gain_ref)
    for j in range(rows):
        grad_ref[:, j * width : (j + 1) * width] = back[j, :, :width].astype(F32)
        gain_ref[...] = gain_ref[...] + back[j, :, width:].astype(F32)
    keep.wait()
    for copy in slices:
        copy.wait_recv()
    for copy in [swap] + along + last + slices:
        copy.wait_send()


def hidden_exchange(grads, first_set, hidden, again, grad_middle, term, ffn):
    rows, tok, width = grads.shape
    model = again.shape[1]
    _, chips, _, own, wide = term.shape
    dma = pltpu.SemaphoreType.DMA
    return pl.pallas_call(
        hidden_back_kernel,
        in_specs=[VMEM_SPEC] * 5 + [ANY_SPEC] * 2,
        out_specs=[VMEM_SPEC] * 3 + [ANY_SPEC],
        out_shape=[
            jax.ShapeDtypeStruct((tok, model), F32),
            jax.ShapeDtypeStruct((own, rows * width), F32),
            jax.ShapeDtypeStruct((own, wide - width), F32),
            jax.ShapeDtypeStruct(ffn.shape, BF),
        ],
        scratch_shapes=exchange_scratch(tok, model)[:3]
        + [
            pltpu.VMEM((rows, chips, own, wide), BF),
            pltpu.VMEM((rows, chips, own, wide), BF),
            pltpu.VMEM((chips - 1, rows, own, wide), BF),
            pltpu.VMEM((rows, own, wide), BF),
            pltpu.VMEM((rows, own, wide), BF),
        ]
        + [dma((n,)) for n in (6, 1, chips - 1, 3, 3) for _ in range(2)]
        + [dma(()), dma(())],
        compiler_params=remote_params(5),
        cost_estimate=pl.CostEstimate(
            flops=2 * rows * tok * width * model, bytes_accessed=110_000_000, transcendentals=0
        ),
        name="hidden_exchange",
    )(grads, first_set, hidden, again, grad_middle, term, ffn)


def last_kernel(oq_ref, back, s1, r1, own):
    rows, _, wide = back.shape
    row = lax.axis_index("row")
    columns = pl.ds(oq_ref.shape[2] - wide, wide)
    near = partners()
    greet([near[1], near[2], near[3]])
    copies = [
        send(oq_ref.at[near[k][0], :, columns], back.at[row], (s1, r1), k - 1, near[k])
        for k in range(1, rows)
    ]
    copies.append(pltpu.make_async_copy(oq_ref.at[row, :, columns], back.at[row], own))
    copies[-1].start()
    for copy in copies:
        copy.wait()


def last_exchange(oq, model):
    rows, own, total = oq.shape
    dma = pltpu.SemaphoreType.DMA
    return pl.pallas_call(
        last_kernel,
        in_specs=[VMEM_SPEC],
        out_specs=VMEM_SPEC,
        out_shape=jax.ShapeDtypeStruct((rows, own, total - model), BF),
        scratch_shapes=[dma((3,)), dma((3,)), dma(())],
        compiler_params=remote_params(8),
        cost_estimate=pl.CostEstimate(flops=0, bytes_accessed=10_000_000, transcendentals=0),
        name="last_exchange",
    )(oq)


def start_kernel(
    hidden_ref, gate_ref, up_ref, cut_ref, all_ref, ffn_ref, first_ref, s1, r1, sg, rg, sz, rz, sc, rc, own, own_ffn, own_cut
):
    row = lax.axis_index("row")
    rows = all_ref.shape[0]
    units = ffn_ref.shape[2] // 2
    chips = first_ref.shape[1]
    seq = lax.axis_index("seq")
    core, chip = seq % 2, seq // 2
    near = partners()
    later, twin = chip_partners(chips)
    greet([near[1], near[2], near[3]] + later + [twin])
    place = first_ref.at[:, chip, core]
    keep = pltpu.make_async_copy(cut_ref, place, own_cut)
    keep.start()
    along = [send(cut_ref, place, (sz, rz), i - 1, later[i - 1]) for i in range(1, chips)]
    shared = [send(cut_ref, place, (sc, rc), 0, twin)]
    cut = []

    def slices():
        for at, source_ref in ((0, gate_ref), (1, up_ref)):
            for k in range(rows):
                to = row if k == 0 else near[k][0]
                source = source_ref.at[:, pl.ds(pl.multiple_of(to * units, 128), units)]
                target = ffn_ref.at[row, :, pl.ds(at * units, units)]
                if k == 0:
                    copy = pltpu.make_async_copy(source, target, own_ffn.at[at])
                    copy.start()
                else:
                    copy = send(source, target, (sg, rg), 3 * at + k - 1, near[k])
                cut.append(copy)

    gather_rows(hidden_ref, all_ref, near, (s1, r1), own, slices)
    for i in range(1, chips):
        along[i - 1].wait_recv()
        block = first_ref.at[:, (chip + chips - i) % chips, core]
        shared.append(send(block, block, (sc, rc), i, twin))
    keep.wait()
    for copy in cut:
        copy.wait()
    for copy in shared:
        copy.wait_recv()
    for copy in along + shared:
        copy.wait_send()


def start_exchange(hidden, gate, up, first_cut, chips):
    rows, own, wide = first_cut.shape
    dma = pltpu.SemaphoreType.DMA
    return pl.pallas_call(
        start_kernel,
        in_specs=[ANY_SPEC] * 4,
        out_specs=[ANY_SPEC] * 3,
        out_shape=[
            jax.ShapeDtypeStruct((rows,) + hidden.shape, BF),
            jax.ShapeDtypeStruct((rows, gate.shape[0], 2 * gate.shape[1] // rows), BF),
            jax.ShapeDtypeStruct((rows, chips, 2, own, wide), BF),
        ],
        scratch_shapes=[dma((n,)) for n in (6, 6, chips - 1, chips) for _ in range(2)]
        + [dma(()), dma((2,)), dma(())],
        compiler_params=remote_params(6),
        cost_estimate=pl.CostEstimate(flops=0, bytes_accessed=120_000_000, transcendentals=0),
        name="start_exchange",
    )(hidden, gate, up, first_cut)


def front_kernel(
    hidden_ref, first_ref, again_ref, lgain_ref, cos_ref, sin_ref, latent_ref, lat_all_ref, kv_ref, first_low, pieces, landed, lat_mine, kv_mine, sa, ra, sl, rl, sz, rz, sr, rr, sf, rf, sc, rc, own_sem
):
    rows, tok, model = hidden_ref.shape
    chips = kv_ref.shape[1]
    width = pieces.shape[2]
    lat = latent_ref.shape[1]
    head = kv_ref.shape[4] // 2
    row, seq = lax.axis_index("row"), lax.axis_index("seq")
    core, chip = seq % 2, seq // 2
    near = partners()
    later, twin = chip_partners(chips)
    greet([near[1], near[2], near[3]] + later + [twin])

    again = again_ref[...]
    copies = []
    for k in (3, 2, 1, 0):
        first_low[...] = rms_forward(hidden_ref[k].astype(F32), again)[0].astype(BF)
        piece = mm(first_low[...], first_ref[:, :width]).astype(BF)
        if k:
            pieces[k] = piece
            copies.append(send(pieces.at[k], landed.at[row], (sa, ra), k - 1, near[k]))
        else:
            landed[row] = piece
    for copy in copies:
        copy.wait_recv()
    joined = jnp.concatenate([landed[j] for j in range(rows)], axis=1)
    key = rotate(joined[:, lat : lat + head].astype(F32), cos_ref[...], sin_ref[...])
    kv_mine[:, :head] = key.astype(BF)
    kv_mine[:, head:] = joined[:, lat + head :]

    own = pltpu.make_async_copy(kv_mine, kv_ref.at[0, chip, core], own_sem.at[0])
    own.start()
    along = [
        send(kv_mine, kv_ref.at[0, chip, core], (sz, rz), i - 1, later[i - 1])
        for i in range(1, chips)
    ]
    low, high = pl.ds(0, tok // 2), pl.ds(tok // 2, tok // 2)
    across, passed = [], []

    def block(i):
        return (chip + chips - i) % chips

    def spread(i):
        source = kv_mine if i == 0 else kv_ref.at[0, block(i), core]
        for k in (1, 2):
            across.append(
                send(source, kv_ref.at[k, block(i), core], (sr, rr), 2 * i + k - 1, near[k])
            )

    def pass_on(i):
        across[2 * i].wait_recv()
        source = kv_ref.at[1, block(i), core, low]
        passed.append(send(source, kv_ref.at[3, block(i), core, low], (sf, rf), 2 * i, near[2]))
        across[2 * i + 1].wait_recv()
        source = kv_ref.at[2, block(i), core, high]
        passed.append(
            send(source, kv_ref.at[3, block(i), core, high], (sf, rf), 2 * i + 1, near[1])
        )

    spread(0)
    latent = joined[:, :lat].astype(F32)
    latent_ref[...] = latent
    lat_mine[...] = rms_forward(latent, lgain_ref[...])[0].astype(BF)
    lat_own = pltpu.make_async_copy(lat_mine, lat_all_ref.at[0], own_sem.at[1])
    lat_own.start()
    lat_copies = [
        send(lat_mine, lat_all_ref.at[k], (sl, rl), k - 1, near[k]) for k in range(1, rows)
    ]
    for i in range(1, chips):
        along[i - 1].wait_recv()
        spread(i)
        pass_on(i - 1)
    own.wait()
    shared = [send(kv_ref.at[0, :, core], kv_ref.at[0, :, core], (sc, rc), 0, twin)]
    pass_on(chips - 1)
    for k in (1, 2):
        shared.append(send(kv_ref.at[k, :, core], kv_ref.at[k, :, core], (sc, rc), k, twin))
    for copy in passed:
        copy.wait_recv()
    shared.append(send(kv_ref.at[3, :, core], kv_ref.at[3, :, core], (sc, rc), 3, twin))
    for copy in lat_copies + shared:
        copy.wait_recv()
    for copy in copies + along + across + passed + lat_copies + shared:
        copy.wait_send()
    lat_own.wait()


def front_exchange(hidden_all, first_set, again, lgain, cosine, sine, chips, width, head):
    rows, tok, model = hidden_all.shape
    lat = lgain.shape[1]
    dma = pltpu.SemaphoreType.DMA
    pairs = [3, 3, chips - 1, 2 * chips, 2 * chips, 4]
    return pl.pallas_call(
        front_kernel,
        in_specs=[VMEM_SPEC] * 6,
        out_specs=[VMEM_SPEC, ANY_SPEC, ANY_SPEC],
        out_shape=[
            jax.ShapeDtypeStruct((tok, lat), F32),
            jax.ShapeDtypeStruct((rows, tok, lat), BF),
            jax.ShapeDtypeStruct((rows, chips, 2, tok, 2 * head), BF),
        ],
        scratch_shapes=[
            pltpu.VMEM((tok, model), BF),
            pltpu.VMEM((rows, tok, width), BF),
            pltpu.VMEM((rows, tok, width), BF),
            pltpu.VMEM((tok, lat), BF),
            pltpu.VMEM((tok, 2 * head), BF),
        ]
        + [dma((n,)) for n in pairs for _ in range(2)]
        + [dma((2,))],
        compiler_params=remote_params(3),
        cost_estimate=pl.CostEstimate(
            flops=2 * rows * tok * model * width, bytes_accessed=230_000_000, transcendentals=0
        ),
        name="front_exchange",
    )(hidden_all, first_set, again, lgain, cosine, sine)


def deal_kernel(first_ref, qup_ref, lens_ref, cut_ref, qup_cut_ref, lens_all, sf, rf, sq, rq, sl, rl, own):
    row = lax.axis_index("row")
    rows, _, wide = cut_ref.shape
    units = qup_cut_ref.shape[2]
    near = partners()
    greet([near[1], near[2], near[3]])
    copies = []
    for k in (3, 1, 2, 0):
        to = row if k == 0 else near[k][0]
        moves = [
            (first_ref.at[to], cut_ref.at[row], (sf, rf)),
            (
                qup_ref.at[:, pl.ds(pl.multiple_of(to * units, 128), units)],
                qup_cut_ref.at[row],
                (sq, rq),
            ),
            (lens_ref, lens_all.at[k], (sl, rl)),
        ]
        for at, (source, target, sems) in enumerate(moves):
            if k:
                copies.append(send(source, target, sems, k - 1, near[k]))
            else:
                copies.append(pltpu.make_async_copy(source, target, own.at[at]))
                copies[-1].start()
    for copy in copies:
        copy.wait()


def deal_exchange(first, qup, lens):
    rows = first.shape[0]
    dma = pltpu.SemaphoreType.DMA
    return pl.pallas_call(
        deal_kernel,
        in_specs=[VMEM_SPEC] * 3,
        out_specs=[VMEM_SPEC] * 3,
        out_shape=[
            jax.ShapeDtypeStruct(first.shape, BF),
            jax.ShapeDtypeStruct((rows, qup.shape[0], qup.shape[1] // rows), BF),
            jax.ShapeDtypeStruct((rows,) + lens.shape, lens.dtype),
        ],
        scratch_shapes=[dma((3,))] * 6 + [dma((3,))],
        compiler_params=remote_params(7),
        cost_estimate=pl.CostEstimate(flops=0, bytes_accessed=10_000_000, transcendentals=0),
        name="deal_exchange",
    )(first, qup, lens)


def move_row(value, k, rows):
    return lax.ppermute(value, "row", [(i, i ^ k) for i in range(rows)])


def join_columns(blocks):
    rows, n, width = blocks.shape
    return blocks.transpose(1, 0, 2).reshape(n, rows * width)


def scatter_seq(v, axis=0):
    return lax.psum_scatter(v.astype(BF), "seq", scatter_dimension=axis, tiled=True)


def on_device(
    hidden,
    cotangent,
    lengths,
    attn_gain,
    query_down,
    latent_gain,
    query_up,
    key_proj,
    value_proj,
    out_proj,
    ffn_gain,
    gate_proj,
    up_proj,
    down_proj,
):
    tok = hidden.shape[1]
    model = hidden.shape[2]
    rows = lax.axis_size("row")
    spread = lax.axis_size("seq")
    row_index = lax.axis_index("row")
    seq_index = lax.axis_index("seq")
    first_slot = seq_index * tok
    head = key_proj.shape[1]
    lat = query_down.shape[1]
    heads = query_up.shape[1] // head // rows
    units = down_proj.shape[0] * spread
    scale = head ** (-0.5)
    own = query_down.shape[0]
    lat_own = latent_gain.shape[0]

    first_own = jnp.concatenate([query_down, key_proj, value_proj], axis=1)
    first_width = first_own.shape[1] // rows
    gain_own = jnp.stack([attn_gain, ffn_gain, jnp.pad(latent_gain, (0, own - lat_own))], axis=1)
    gain_own = jnp.pad(gain_own, ((0, 0), (0, 125)))
    first_own = jnp.stack(
        [
            jnp.concatenate([first_own[:, j * first_width : (j + 1) * first_width], gain_own], axis=1)
            for j in range(rows)
        ]
    )
    docs = lengths.shape[1]
    first_cut, qup_cut, lens = deal_exchange(
        first_own, query_up, jnp.pad(lengths, ((0, 0), (0, 128 - docs)))
    )
    lens = lens[:, 0, :docs]
    oq_own = jnp.concatenate([out_proj, qup_cut.reshape(out_proj.shape[0], -1)], axis=1)
    full_oq = lax.all_gather(oq_own, "seq", axis=0, tiled=True)
    hidden_all, ffn_cut, first_set = start_exchange(
        hidden[0], gate_proj, up_proj, first_cut, spread // 2
    )
    first_set = first_set.reshape(model, -1)
    full_ffn = lax.all_gather(ffn_cut, "seq", axis=1, tiled=True).reshape(model, -1)
    full_down = lax.all_gather(down_proj, "seq", axis=0, tiled=True)
    full_gains = first_set[:, first_width:].astype(F32)
    full_again = full_gains[:, 0]
    full_fgain = full_gains[:, 1]
    full_lgain = full_gains[:, 2].reshape(rows * spread, own)[:, :lat_own].reshape(lat)
    full_qup = full_oq[:, model:].reshape(spread, rows, lat_own, -1).transpose(1, 0, 2, 3)
    full_qup = full_qup.reshape(lat, heads * head)
    position = document_positions(lens, first_slot + jnp.arange(tok, dtype=jnp.int32))
    cosine, sine = rope_tables(position, head)

    residual_all = hidden_all.astype(F32)
    first_low = rms_forward(residual_all, full_again)[0].astype(BF).reshape(rows * tok, model)
    latent, latent_all, key_value = front_exchange(
        hidden_all,
        first_set,
        full_again[None],
        full_lgain[None],
        cosine[0],
        sine[0],
        spread // 2,
        first_width,
        head,
    )
    key_value = key_value.reshape(rows, spread * tok, 2 * head)
    grad_own, latent_all = lax.optimization_barrier((cotangent[0], latent_all))
    grad_pieces = [move_row(grad_own, k, rows) for k in range(1, rows)]
    query_low, attend, attend_low, stats = attend_forward(
        heads, scale, lens, latent_all, full_qup, cosine, sine, key_value
    )
    middle, second_all = branch_exchange(attend_low, full_oq, hidden[0], full_fgain[None])
    grad_pieces, second_all = lax.optimization_barrier((grad_pieces, second_all))
    grad_all = jnp.stack([cotangent[0]] + grad_pieces).reshape(rows * tok, model)
    second_all = second_all.reshape(rows * tok, model)
    both = mm(second_all, full_ffn)
    gate_pre, upward = both[:, :units], both[:, units:]
    gate_sig = jax.nn.sigmoid(gate_pre)
    gate_act = gate_pre * gate_sig
    act_low = (gate_act * upward).astype(BF)
    down_part = mm_tn(act_low, grad_all).astype(BF)
    down_grad = scatter_seq(down_part)
    full_down, down_order = lax.optimization_barrier((full_down, down_part))
    grad_act = mm_nt(grad_all, full_down)
    slope = gate_sig * (1.0 + gate_pre * (1.0 - gate_sig))
    grad_both = jnp.concatenate([grad_act * upward * slope, grad_act * gate_act], axis=1).astype(BF)
    ffn_term = mm_tn(second_all, grad_both).astype(BF).reshape(rows, model // rows, -1)
    ffn_part = scatter_seq(ffn_term, 1)

    grad_both, ffn_term = lax.optimization_barrier((grad_both, ffn_term))
    grad_middle, ffn_gain_part, branch_all, layer_part = second_exchange(
        grad_both.reshape(rows, tok, 2 * units),
        full_ffn,
        act_low.reshape(rows, tok, units),
        full_down,
        middle,
        cotangent[0],
        full_fgain[None],
        down_order,
    )
    ffn_gain_part = ffn_gain_part[0]
    layer_pieces = [move_row(layer_part[k], k, rows) for k in range(1, rows)]
    grad_query, kv_part, oq_part = attend_backward(
        heads,
        scale,
        lens,
        query_low,
        key_value,
        branch_all,
        full_oq,
        attend_low,
        latent_all,
        attend,
        stats,
        cosine,
        sine,
    )
    grad_query, oq_part, down_grad, layer_pieces = lax.optimization_barrier(
        (grad_query, oq_part, down_grad, layer_pieces)
    )
    oq_part = scatter_seq(oq_part)
    layer_sum = middle + layer_part[0].astype(F32)
    for piece in layer_pieces:
        layer_sum = layer_sum + piece.astype(F32)
    layer_out = layer_sum.astype(BF)
    grad_first_all, latent_gain_part, attn_gain_part = tail_exchange(
        grad_query,
        full_qup,
        kv_part.reshape(rows, spread // 2, 2, tok, 2 * head),
        latent,
        full_lgain[None],
        cosine[0],
        sine[0],
        first_set,
        hidden_all,
        full_again[None],
        first_width,
    )
    lgain_part = jnp.pad(
        latent_gain_part.reshape(rows * spread, lat_own), ((0, 0), (0, own - lat_own))
    ).reshape(model)
    gain_parts = jnp.stack([attn_gain_part[0], ffn_gain_part, lgain_part], axis=1)
    first_term = mm_tn(first_low, grad_first_all.reshape(rows * tok, first_width))
    first_term = jnp.concatenate(
        [first_term, jnp.pad(gain_parts, ((0, 0), (0, 125)))], axis=1
    ).astype(BF)
    hidden_grad, first_grad, gain_grad, ffn_back = hidden_exchange(
        grad_first_all,
        first_set,
        hidden[0],
        full_again[None],
        grad_middle,
        first_term.reshape(rows, spread // 2, 2, own, -1),
        ffn_part,
    )
    hidden_grad, oq_part = lax.optimization_barrier((hidden_grad, oq_part))
    query_up_grad = last_exchange(oq_part.reshape(rows, lat_own, -1), model)
    query_up_grad = join_columns(query_up_grad).astype(F32)
    out_grad = oq_part[:, :model].astype(F32)
    gate_grad = join_columns(ffn_back[:, :, :units]).astype(F32)
    up_grad = join_columns(ffn_back[:, :, units:]).astype(F32)
    return (
        layer_out[None],
        hidden_grad[None],
        gain_grad[:, 0],
        first_grad[:, :lat],
        gain_grad[:lat_own, 2],
        query_up_grad,
        first_grad[:, lat : lat + head],
        first_grad[:, lat + head :],
        out_grad,
        gain_grad[:, 1],
        gate_grad,
        up_grad,
        down_grad.astype(F32),
    )


def solution(mesh):
    token = P("row", "seq", None)
    vector = P(("row", "seq"))
    matrix = P(("row", "seq"), None)
    return jax.shard_map(
        on_device,
        mesh=mesh,
        in_specs=(token, token, P("row", None), vector, matrix, vector)
        + (matrix,) * 4
        + (vector,)
        + (matrix,) * 3,
        out_specs=(token, token, vector, matrix, vector)
        + (matrix,) * 4
        + (vector,)
        + (matrix,) * 3,
        check_vma=False,
    )
```

```python
import functools
import math

import jax
import jax.numpy as jnp
from jax import lax
from jax.experimental import pallas as pl
from jax.experimental.pallas import tpu as pltpu
from jax.sharding import PartitionSpec as P

epsilon = 1e-06
masked_value = -1e30
BF = jnp.bfloat16
F32 = jnp.float32
VMEM_BYTES = 60 * 1024 * 1024


def rms_forward(values, gain):
    inv_rms = lax.rsqrt(jnp.mean(values * values, axis=-1, keepdims=True) + epsilon)
    normed = values * inv_rms
    return (normed * gain, normed, inv_rms)


def rms_backward(incoming, normed, inv_rms, gain):
    grad_normed = incoming * gain
    inner = jnp.mean(grad_normed * normed, axis=-1, keepdims=True)
    return inv_rms * (grad_normed - normed * inner)


def document_positions(lengths, slots):
    ends = jnp.cumsum(lengths, axis=1)
    is_past = slots[None, :, None] >= ends[:, None, :]
    begin = jnp.sum(jnp.where(is_past, lengths[:, None, :], 0), axis=2)
    return slots[None, :] - begin


def rope_tables(position, head_size):
    half_dim = head_size // 2
    frequency = jnp.exp(jnp.arange(half_dim, dtype=F32) * (-2.0 * math.log(10000.0) / head_size))
    angles = position.astype(F32)[..., None] * frequency
    return (jnp.cos(angles), jnp.sin(angles))


def rotate(values, cosine, sine_table):
    half = values.shape[-1] // 2
    front, behind = values[..., :half], values[..., half:]
    return jnp.concatenate(
        [front * cosine - behind * sine_table, behind * cosine + front * sine_table], axis=-1
    )


def rotate_back(grads, cosine, sine_table):
    half = grads.shape[-1] // 2
    front, behind = grads[..., :half], grads[..., half:]
    return jnp.concatenate(
        [front * cosine + behind * sine_table, behind * cosine - front * sine_table], axis=-1
    )


def dot(a, b, dims):
    return lax.dot_general(a, b, (dims, ((), ())), preferred_element_type=F32)


def mm(a, b):
    return dot(a, b, ((1,), (0,)))


def mm_nt(a, b):
    return dot(a, b, ((1,), (1,)))


def mm_tn(a, b):
    return dot(a, b, ((0,), (0,)))


KEYS = 256


def visible(lens_ref, row, first_slot, tok):
    slot = first_slot + lax.broadcasted_iota(jnp.int32, (tok, 1), 0)
    low = jnp.zeros((tok, 1), jnp.int32)
    first_low = jnp.int32(0)
    end = jnp.int32(0)
    docs = lens_ref.shape[1]
    for doc in range(docs):
        end = end + lens_ref[row, doc]
        if doc < docs - 1:
            low = jnp.where(slot >= end, end, low)
            first_low = jnp.where(first_slot >= end, end, first_low)
        else:
            low = jnp.where(slot >= end, slot, low)
            first_low = jnp.where(first_slot >= end, first_slot, first_low)
    first_step = first_low // KEYS
    last_step = (first_slot + tok + KEYS - 1) // KEYS
    return (slot, low, first_step, last_step)


def stack_heads(ref_or_value, heads, head):
    return jnp.concatenate(
        [ref_or_value[:, h * head : (h + 1) * head] for h in range(heads)], axis=0
    )


def attend_kernel(
    heads, scale, lens_ref, lat_ref, qup_ref, cos_ref, sin_ref, kv_ref, q_ref, out_ref, low_ref, stats_ref, score_ref
):
    row = pl.program_id(0)
    tok = lat_ref.shape[1]
    head = kv_ref.shape[2] // 2
    first_slot = lax.axis_index("seq") * tok
    slot, low, first_step, last_step = visible(lens_ref, row, first_slot, tok)
    slot = jnp.concatenate([slot] * heads, axis=0)
    low = jnp.concatenate([low] * heads, axis=0)
    queries = mm(lat_ref[0], qup_ref[...])
    cosine, sine = cos_ref[0], sin_ref[0]
    for h in range(heads):
        q_ref[0, :, h * head : (h + 1) * head] = rotate(
            queries[:, h * head : (h + 1) * head], cosine, sine
        ).astype(BF)
    query = stack_heads(q_ref[0], heads, head)

    def keys_of(step):
        return pl.ds(pl.multiple_of(step * KEYS, KEYS), KEYS)

    def score_step(step, row_max):
        score = mm_nt(query, kv_ref[0, keys_of(step), :head]) * scale
        key_slot = step * KEYS + lax.broadcasted_iota(jnp.int32, (1, KEYS), 1)
        score = jnp.where((key_slot >= low) & (key_slot <= slot), score, masked_value)
        score_ref[step] = score
        return jnp.maximum(row_max, jnp.max(score, axis=1, keepdims=True))

    row_max = lax.fori_loop(
        first_step, last_step, score_step, jnp.full((heads * tok, 1), masked_value, F32)
    )

    def value_step(step, carry):
        row_total, weighted = carry
        weight = jnp.exp(score_ref[step] - row_max)
        row_total = row_total + jnp.sum(weight, axis=1, keepdims=True)
        weighted = weighted + mm(weight.astype(BF), kv_ref[0, keys_of(step), head:])
        return (row_total, weighted)

    row_total, weighted = lax.fori_loop(
        first_step,
        last_step,
        value_step,
        (jnp.zeros((heads * tok, 1), F32), jnp.zeros((heads * tok, head), F32)),
    )
    attend = weighted / row_total
    lane = lax.broadcasted_iota(jnp.int32, (tok, 128), 1)
    stats = jnp.zeros((tok, 128), F32)
    for h in range(heads):
        rows = slice(h * tok, (h + 1) * tok)
        out_ref[0, :, h * head : (h + 1) * head] = attend[rows]
        low_ref[0, :, h * head : (h + 1) * head] = attend[rows].astype(BF)
        stats = jnp.where(lane == h, row_max[rows], stats)
        stats = jnp.where(lane == heads + h, row_total[rows], stats)
    stats_ref[0] = stats


def attend_back_kernel(
    heads, scale, lens_ref, q_ref, kv_ref, branch_ref, proj_ref, branch_all_ref, low_ref, lat_ref, out_ref, stats_ref, cos_ref, sin_ref, dq_ref, dkv_ref, oq_ref, dq_all
):
    row = pl.program_id(0)
    tok = q_ref.shape[1]
    head = kv_ref.shape[2] // 2
    first_slot = lax.axis_index("seq") * tok
    slot, low, first_step, last_step = visible(lens_ref, row, first_slot, tok)
    slot = jnp.concatenate([slot] * heads, axis=0)
    low = jnp.concatenate([low] * heads, axis=0)
    query = stack_heads(q_ref[0], heads, head)
    branch = branch_ref[0]
    grad = jnp.concatenate(
        [mm_nt(branch, proj_ref[h * head : (h + 1) * head, :]) for h in range(heads)], axis=0
    )
    attend = stack_heads(out_ref[0], heads, head)
    stats = stats_ref[0]
    row_max = jnp.concatenate([stats[:, h : h + 1] for h in range(heads)], axis=0)
    row_total = jnp.concatenate(
        [stats[:, heads + h : heads + h + 1] for h in range(heads)], axis=0
    )
    grad_weighted = (grad / row_total).astype(BF)
    delta = jnp.sum(grad * attend, axis=1, keepdims=True) / row_total
    dkv_ref[...] = jnp.zeros_like(dkv_ref)

    def step_back(step, grad_query):
        keys = pl.ds(pl.multiple_of(step * KEYS, KEYS), KEYS)
        key, value = kv_ref[0, keys, :head], kv_ref[0, keys, head:]
        score = mm_nt(query, key) * scale
        key_slot = step * KEYS + lax.broadcasted_iota(jnp.int32, (1, KEYS), 1)
        allowed = (key_slot >= low) & (key_slot <= slot)
        weight = jnp.exp(jnp.where(allowed, score - row_max, masked_value))
        grad_weight = mm_nt(grad_weighted, value)
        grad_score = (weight * (grad_weight - delta)).astype(BF)
        dkv_ref[0, keys, :head] = (mm_tn(grad_score, query) * scale).astype(BF)
        dkv_ref[0, keys, head:] = mm_tn(weight.astype(BF), grad_weighted).astype(BF)
        return grad_query + mm(grad_score, key)

    grad_query = lax.fori_loop(
        first_step, last_step, step_back, jnp.zeros((heads * tok, head), F32)
    )
    cosine, sine = cos_ref[0], sin_ref[0]
    for h in range(heads):
        dq_ref[0, :, h * head : (h + 1) * head] = rotate_back(
            grad_query[h * tok : (h + 1) * tok] * scale, cosine, sine
        ).astype(BF)
        dq_all[row, :, h * head : (h + 1) * head] = dq_ref[0, :, h * head : (h + 1) * head]

    @pl.when(row == pl.num_programs(0) - 1)
    def _():
        weight_grads(low_ref, branch_all_ref, lat_ref, dq_all, oq_ref)


def weight_grads(low_ref, branch_ref, lat_ref, dq_ref, oq_ref):
    model, width = branch_ref.shape[2], dq_ref.shape[2]
    lat = lat_ref.shape[2]
    rows, spread = lax.axis_size("row"), lax.axis_size("seq")
    own = lat // rows // spread
    right = branch_ref[...].reshape(-1, model)
    tile = 256

    def out_tile(t, carry):
        at = pl.ds(pl.multiple_of(t * tile, tile), tile)
        left = low_ref[:, :, at].reshape(-1, tile)
        oq_ref[at, :model] = mm_tn(left, right).astype(BF)
        return carry

    lax.fori_loop(0, low_ref.shape[2] // tile, out_tile, 0)
    right_lat = dq_ref[...].reshape(-1, width)
    block = lat // rows
    if own % 16 == 0:
        for r in range(rows):
            left = lat_ref[:, :, r * block : (r + 1) * block].reshape(-1, block)
            product = mm_tn(left, right_lat).astype(BF)
            for seq in range(spread):
                at = (seq * rows + r) * own
                oq_ref[at : at + own, model:] = product[seq * own : (seq + 1) * own]
    else:
        product = mm_tn(lat_ref[...].reshape(-1, lat), right_lat)
        for seq in range(spread):
            pieces = [
                product[(r * spread + seq) * own : (r * spread + seq + 1) * own] for r in range(rows)
            ]
            oq_ref[seq * rows * own : (seq + 1) * rows * own, model:] = jnp.concatenate(
                pieces, axis=0
            ).astype(BF)


def row_block(shape):
    return pl.BlockSpec((1,) + shape[1:], lambda i: (i, 0, 0))


def whole_block(shape):
    return pl.BlockSpec(shape, lambda i: (0,) * len(shape))


def kernel_params():
    return pltpu.CompilerParams(
        dimension_semantics=("arbitrary",), vmem_limit_bytes=VMEM_BYTES
    )


def attend_forward(heads, scale, lens, lat, qup, cosine, sine, kv):
    rows, tok, _ = lat.shape
    slots = kv.shape[1]
    wide = (rows, tok, qup.shape[1])
    flops = rows * tok * (2 * lat.shape[2] * qup.shape[1] + 4 * slots * qup.shape[1])
    return pl.pallas_call(
        functools.partial(attend_kernel, heads, scale),
        grid=(rows,),
        in_specs=[pl.BlockSpec(memory_space=pltpu.SMEM)]
        + [row_block(lat.shape), whole_block(qup.shape)]
        + [row_block(cosine.shape), row_block(sine.shape), row_block(kv.shape)],
        out_specs=[row_block(wide), row_block(wide), row_block(wide), row_block((rows, tok, 128))],
        out_shape=[
            jax.ShapeDtypeStruct(wide, BF),
            jax.ShapeDtypeStruct(wide, F32),
            jax.ShapeDtypeStruct(wide, BF),
            jax.ShapeDtypeStruct((rows, tok, 128), F32),
        ],
        scratch_shapes=[pltpu.VMEM((slots // KEYS, heads * tok, KEYS), F32)],
        compiler_params=kernel_params(),
        cost_estimate=pl.CostEstimate(
            flops=flops, bytes_accessed=16 * 1024 * 1024, transcendentals=rows * tok * heads * slots
        ),
        name="attend_forward",
    )(lens, lat, qup, cosine, sine, kv)


def attend_backward(
    heads, scale, lens, query, kv, branch, oq, low, lat, attend, stats, cosine, sine
):
    rows, tok, width = query.shape
    model = branch.shape[2]
    slots = kv.shape[1]
    return pl.pallas_call(
        functools.partial(attend_back_kernel, heads, scale),
        grid=(rows,),
        in_specs=[pl.BlockSpec(memory_space=pltpu.SMEM)]
        + [row_block(v.shape) for v in (query, kv, branch)]
        + [pl.BlockSpec((width, model), lambda i: (0, 0), pipeline_mode=pl.Buffered(1))]
        + [
            pl.BlockSpec(v.shape, lambda i: (0, 0, 0), pipeline_mode=pl.Buffered(1))
            for v in (branch, low, lat)
        ]
        + [row_block(v.shape) for v in (attend, stats, cosine, sine)],
        out_specs=[row_block(query.shape), row_block(kv.shape)]
        + [pl.BlockSpec(oq.shape, lambda i: (0, 0), pipeline_mode=pl.Buffered(1))],
        out_shape=[
            jax.ShapeDtypeStruct(query.shape, BF),
            jax.ShapeDtypeStruct(kv.shape, BF),
            jax.ShapeDtypeStruct(oq.shape, BF),
        ],
        scratch_shapes=[pltpu.VMEM(query.shape, BF)],
        compiler_params=kernel_params(),
        cost_estimate=pl.CostEstimate(
            flops=rows * tok * 10 * slots * width,
            bytes_accessed=100_000_000,
            transcendentals=rows * tok * heads * slots,
        ),
        name="attend_backward",
    )(lens, query, kv, branch, oq, branch, low, lat, attend, stats, cosine, sine)


MESH = pl.DeviceIdType.MESH


def partners():
    row, seq = lax.axis_index("row"), lax.axis_index("seq")
    return {1: (row + 1 - 2 * (row % 2), seq), 2: ((row + 2) % 4, seq), 3: (3 - row, seq)}


def chip_partners(chips):
    row, seq = lax.axis_index("row"), lax.axis_index("seq")
    later = [(row, (seq + 2 * i) % (2 * chips)) for i in range(1, chips)]
    return later, (row, seq + 1 - 2 * (seq % 2))


def greet(devices):
    barrier = pltpu.get_barrier_semaphore()
    for device in devices:
        pl.semaphore_signal(barrier, inc=1, device_id=device, device_id_type=MESH)
    pl.semaphore_wait(barrier, len(devices))


def send(source, target, sems, at, device):
    copy = pltpu.make_async_remote_copy(
        src_ref=source,
        dst_ref=target,
        send_sem=sems[0].at[at],
        recv_sem=sems[1].at[at],
        device_id=device,
        device_id_type=MESH,
    )
    copy.start()
    return copy


TILE = 512


def reduce_rows(product, near, parts, kept, landed, sems, ready=None):
    half = parts.shape[2]
    tiles = half // TILE

    def compute(k, side, store):
        if ready is not None:
            ready(k, side)

        def tile(t, carry):
            local = pl.ds(pl.multiple_of(t * TILE, TILE), TILE)
            columns = pl.ds(pl.multiple_of(side * half + t * TILE, TILE), TILE)
            store(local, columns, product(k, columns))
            return carry

        lax.fori_loop(0, tiles, tile, 0)

    def into_parts(at):
        def store(local, columns, value):
            parts[at, :, local] = value.astype(BF)

        return store

    def into_kept(at):
        def store(local, columns, value):
            kept[at, :, columns] = value

        return store

    copies = []

    def begin():
        for at, (k, side, to) in enumerate([(3, 0, 1), (3, 1, 2), (1, 0, 1), (2, 1, 2)]):
            compute(k, side, into_parts(at))
            copies.append(send(parts.at[at], landed.at[at], sems, at, near[to]))
        compute(2, 0, into_kept(1))
        compute(1, 1, into_kept(1))

    def pass_on():
        copies[0].wait_recv()
        parts[4] = (kept[1, :, :half] + landed[0].astype(F32)).astype(BF)
        copies.append(send(parts.at[4], landed.at[4], sems, 4, near[2]))
        copies[1].wait_recv()
        parts[5] = (kept[1, :, half:] + landed[1].astype(F32)).astype(BF)
        copies.append(send(parts.at[5], landed.at[5], sems, 5, near[1]))

    def finish():
        compute(0, 0, into_kept(0))
        compute(0, 1, into_kept(0))
        copies[2].wait_recv()
        copies[3].wait_recv()
        kept[0, :, :half] = kept[0, :, :half] + landed[2].astype(F32)
        kept[0, :, half:] = kept[0, :, half:] + landed[3].astype(F32)
        copies[4].wait_recv()
        copies[5].wait_recv()
        kept[0, :, :half] = kept[0, :, :half] + landed[4].astype(F32)
        kept[0, :, half:] = kept[0, :, half:] + landed[5].astype(F32)
        for copy in copies:
            copy.wait_send()

    return begin, pass_on, finish


def gather_rows(mine, out, near, sems, local_sem, meanwhile=None):
    tok = mine.shape[0]
    low, high = pl.ds(0, tok // 2), pl.ds(tok // 2, tok // 2)
    own = pltpu.make_async_copy(mine, out.at[0], local_sem)
    own.start()
    first = send(mine.at[low], out.at[1, low], sems, 0, near[1])
    second = send(mine.at[high], out.at[2, high], sems, 1, near[2])
    third = send(mine.at[high], out.at[1, high], sems, 2, near[1])
    fourth = send(mine.at[low], out.at[2, low], sems, 3, near[2])
    if meanwhile is not None:
        meanwhile()
    first.wait_recv()
    fifth = send(out.at[1, low], out.at[3, low], sems, 4, near[2])
    second.wait_recv()
    sixth = send(out.at[2, high], out.at[3, high], sems, 5, near[1])
    for copy in (third, fourth, fifth, sixth):
        copy.wait_recv()
    for copy in (first, second, third, fourth, fifth, sixth):
        copy.wait_send()
    own.wait()


def exchange_scratch(tok, model):
    return [
        pltpu.VMEM((6, tok, model // 2), BF),
        pltpu.VMEM((6, tok, model // 2), BF),
        pltpu.VMEM((2, tok, model), F32),
        pltpu.VMEM((tok, model), BF),
        pltpu.SemaphoreType.DMA((6,)),
        pltpu.SemaphoreType.DMA((6,)),
        pltpu.SemaphoreType.DMA((6,)),
        pltpu.SemaphoreType.DMA((6,)),
        pltpu.SemaphoreType.DMA(()),
    ]


def branch_kernel(
    attend_ref, out_proj_ref, hidden_ref, gain_ref, middle_ref, second_ref, parts, landed, kept, mine, s1, r1, s2, r2, own
):
    near = partners()
    greet([near[1], near[2]])

    def product(k, columns):
        return mm(attend_ref[k], out_proj_ref[:, columns])

    for phase in reduce_rows(product, near, parts, kept, landed, (s1, r1)):
        phase()
    middle = hidden_ref[...].astype(F32) + kept[0]
    middle_ref[...] = middle
    mine[...] = rms_forward(middle, gain_ref[...])[0].astype(BF)
    gather_rows(mine, second_ref, near, (s2, r2), own)


def second_back_kernel(
    gate_hbm, up_hbm, ffn_hbm, act_hbm, down_hbm, middle_ref, cot_ref, gain_ref, order_ref, grad_ref, gain_grad_ref, branch_ref, layer_ref, parts, landed, kept, mine, s1, r1, s2, r2, own, both_ref, ffn_ref, act_ref, down_ref, load_sems
):
    del order_ref
    half = ffn_ref.shape[0] // 2
    loads = {}

    def load(name, source, target):
        loads[name] = pltpu.make_async_copy(source, target, load_sems.at[len(loads)])
        loads[name].start()

    units = gate_hbm.shape[2]

    def load_both(k):
        load(("gate", k), gate_hbm.at[k], both_ref.at[k, :, pl.ds(0, units)])
        load(("up", k), up_hbm.at[k], both_ref.at[k, :, pl.ds(units, units)])

    load_both(3)
    for side in (0, 1):
        rows = pl.ds(side * half, half)
        load(("ffn", side), ffn_hbm.at[rows], ffn_ref.at[rows])
    for k in (1, 2, 0):
        load_both(k)
    load("act", act_hbm, act_ref)
    load("down", down_hbm, down_ref)
    waited = set()

    def loaded(*names):
        for name in names:
            if name not in waited:
                waited.add(name)
                loads[name].wait()

    def ready(k, side):
        loaded(("gate", k), ("up", k), ("ffn", side))

    near = partners()
    greet([near[1], near[2]])

    def product(k, columns):
        return mm_nt(both_ref[k], ffn_ref[columns, :])

    begin, pass_on, finish = reduce_rows(product, near, parts, kept, landed, (s1, r1), ready)
    begin()
    pass_on()
    loaded("act", "down")
    for k in range(act_ref.shape[0]):

        def tile(t, carry, k=k):
            columns = pl.ds(pl.multiple_of(t * TILE, TILE), TILE)
            layer_ref[k, :, columns] = mm(act_ref[k], down_ref[:, columns]).astype(BF)
            return carry

        lax.fori_loop(0, down_ref.shape[1] // TILE, tile, 0)
    finish()
    grad_second = kept[0]
    gain = gain_ref[...]
    _, unit, inv = rms_forward(middle_ref[...], gain)
    gain_grad_ref[...] = jnp.sum(grad_second * unit, axis=0, keepdims=True)
    grad_middle = cot_ref[...].astype(F32) + rms_backward(grad_second, unit, inv, gain)
    grad_ref[...] = grad_middle
    mine[...] = grad_middle.astype(BF)
    gather_rows(mine, branch_ref, near, (s2, r2), own)


VMEM_SPEC = pl.BlockSpec(memory_space=pltpu.VMEM)
ANY_SPEC = pl.BlockSpec(memory_space=pl.ANY)


def remote_params(collective_id):
    return pltpu.CompilerParams(
        collective_id=collective_id, has_side_effects=True, vmem_limit_bytes=VMEM_BYTES
    )


def branch_exchange(attend, out_proj, hidden, gain):
    rows, tok, width = attend.shape
    model = hidden.shape[1]
    return pl.pallas_call(
        branch_kernel,
        in_specs=[VMEM_SPEC] * 4,
        out_specs=[VMEM_SPEC, ANY_SPEC],
        out_shape=[
            jax.ShapeDtypeStruct((tok, model), F32),
            jax.ShapeDtypeStruct((rows, tok, model), BF),
        ],
        scratch_shapes=exchange_scratch(tok, model),
        compiler_params=remote_params(1),
        cost_estimate=pl.CostEstimate(
            flops=2 * rows * tok * width * model, bytes_accessed=190_000_000, transcendentals=0
        ),
        name="branch_exchange",
    )(attend, out_proj, hidden, gain)


def second_exchange(gate, up, ffn, act, down, middle, cotangent, gain, order):
    rows, tok, units = gate.shape
    model = ffn.shape[0]
    return pl.pallas_call(
        second_back_kernel,
        in_specs=[ANY_SPEC] * 5 + [VMEM_SPEC] * 3 + [ANY_SPEC],
        out_specs=[VMEM_SPEC, VMEM_SPEC, ANY_SPEC, VMEM_SPEC],
        out_shape=[
            jax.ShapeDtypeStruct((tok, model), F32),
            jax.ShapeDtypeStruct((1, model), F32),
            jax.ShapeDtypeStruct((rows, tok, model), BF),
            jax.ShapeDtypeStruct((rows, tok, model), BF),
        ],
        scratch_shapes=exchange_scratch(tok, model)
        + [pltpu.VMEM(shape, BF) for shape in ((rows, tok, 2 * units), ffn.shape, act.shape, down.shape)]
        + [pltpu.SemaphoreType.DMA((12,))],
        compiler_params=remote_params(2),
        cost_estimate=pl.CostEstimate(
            flops=6 * rows * tok * units * model, bytes_accessed=190_000_000, transcendentals=0
        ),
        name="second_exchange",
    )(gate, up, ffn, act, down, middle, cotangent, gain, order)


def tail_kernel(
    dq_ref, qup_ref, dkv_ref, latent_ref, lgain_ref, cos_ref, sin_ref, first_ref, hidden_ref, again_ref, grads_ref, lgain_part_ref, again_part_ref, ours, theirs, kv_landed, z_landed, parts, landed, kept, pieces, grads, sc, rc, sk, rk, sz, rz, sl, rl, sg, rg, own_sem
):
    rows, chips, tok, wide = ours.shape
    head = wide // 2
    lat = latent_ref.shape[1]
    width = pieces.shape[2]
    row, seq = lax.axis_index("row"), lax.axis_index("seq")
    core, chip = seq % 2, seq // 2
    near = partners()
    later, twin = chip_partners(chips)
    greet([near[1], near[2], near[3]] + later + [twin])

    swap = send(dkv_ref.at[:, :, 1 - core], theirs, (sc, rc), 0, twin)
    load = pltpu.make_async_copy(dkv_ref.at[:, :, core], ours, own_sem)
    load.start()
    left, right = slice(0, head), slice(head, wide)

    def latent_product(k, columns):
        return mm_nt(dq_ref[k], qup_ref[columns, :])

    begin, pass_on, finish = reduce_rows(latent_product, near, parts, kept, landed, (sl, rl))
    load.wait()
    swap.wait_recv()

    blocks = [(chip + i) % chips for i in range(1, chips)] + [chip]
    steps, along = {}, []

    def add(k, block, side, other):
        value = ours[k, block, :, side].astype(F32) + other.astype(F32)
        ours[k, block, :, side] = value.astype(BF)

    def move(n, at, k, side, to):
        source = ours.at[k, blocks[n], :, side]
        steps[n, at] = send(source, kv_landed.at[at, n], (sk, rk), 6 * n + at, near[to])

    def first(n):
        for at, (k, side, to) in enumerate(
            [(3, left, 1), (3, right, 2), (1, left, 1), (2, right, 2)]
        ):
            add(k, blocks[n], side, theirs[k, blocks[n], :, side])
            move(n, at, k, side, to)
        for k, side in ((2, left), (1, right), (0, left), (0, right)):
            add(k, blocks[n], side, theirs[k, blocks[n], :, side])

    def second(n):
        steps[n, 0].wait_recv()
        add(2, blocks[n], left, kv_landed[0, n])
        move(n, 4, 2, left, 2)
        steps[n, 1].wait_recv()
        add(1, blocks[n], right, kv_landed[1, n])
        move(n, 5, 1, right, 1)

    def third(n):
        for at, side in ((2, left), (3, right), (4, left), (5, right)):
            steps[n, at].wait_recv()
            add(0, blocks[n], side, kv_landed[at, n])
        if n < chips - 1:
            along.append(send(ours.at[0, blocks[n]], z_landed.at[n], (sz, rz), n, later[n]))

    for n in range(chips + 1):
        if n < chips:
            first(n)
        if n >= 1:
            second(n - 1)
        if n >= 2:
            third(n - 2)
    begin()
    third(chips - 1)
    pass_on()
    finish()
    grad_latent_norm = kept[0]
    lgain = lgain_ref[...]
    _, unit, inv = rms_forward(latent_ref[...], lgain)
    lgain_part_ref[...] = jnp.sum(grad_latent_norm * unit, axis=0, keepdims=True)
    grad_latent = rms_backward(grad_latent_norm, unit, inv, lgain)
    total = ours[0, chip].astype(F32)
    for i in range(1, chips):
        along[i - 1].wait_recv()
        total = total + z_landed[i - 1].astype(F32)
    grad_key = rotate_back(total[:, :head], cos_ref[...], sin_ref[...])
    joined = jnp.concatenate([grad_latent, grad_key, total[:, head:]], axis=1).astype(BF)
    for j in range(rows):
        pieces[j] = joined[:, j * width : (j + 1) * width]
    last = [
        send(pieces.at[near[k][0]], grads.at[k], (sg, rg), k - 1, near[k]) for k in range(1, rows)
    ]
    grads[0] = pieces[row]
    tiles = again_ref.shape[1] // TILE
    again_part_ref[...] = jnp.zeros_like(again_part_ref)
    for k in range(rows):
        if k:
            last[k - 1].wait_recv()
        grads_ref[k] = grads[k]
        values = hidden_ref[k].astype(F32)
        scale = lax.rsqrt(jnp.mean(values * values, axis=-1, keepdims=True) + epsilon)

        def tile(t, carry):
            columns = pl.ds(pl.multiple_of(t * TILE, TILE), TILE)
            part = mm_nt(grads[k], first_ref[columns, :width])
            part = part * (hidden_ref[k, :, columns].astype(F32) * scale)
            again_part_ref[:, columns] = again_part_ref[:, columns] + jnp.sum(
                part, axis=0, keepdims=True
            )
            return carry

        lax.fori_loop(0, tiles, tile, 0)
    for copy in [swap] + list(steps.values()) + along + last:
        copy.wait_send()


def tail_exchange(
    dq, qup, dkv, latent, lgain, cosine, sine, first_set, hidden_all, again, width
):
    rows, chips, _, tok, wide = dkv.shape
    lat = latent.shape[1]
    model = again.shape[1]
    dma = pltpu.SemaphoreType.DMA
    return pl.pallas_call(
        tail_kernel,
        in_specs=[VMEM_SPEC] * 2 + [ANY_SPEC] + [VMEM_SPEC] * 7,
        out_specs=[VMEM_SPEC] * 3,
        out_shape=[
            jax.ShapeDtypeStruct((rows, tok, width), BF),
            jax.ShapeDtypeStruct((1, lat), F32),
            jax.ShapeDtypeStruct((1, model), F32),
        ],
        scratch_shapes=[
            pltpu.VMEM((rows, chips, tok, wide), BF),
            pltpu.VMEM((rows, chips, tok, wide), BF),
            pltpu.VMEM((6, chips, tok, wide // 2), BF),
            pltpu.VMEM((chips - 1, tok, wide), BF),
            pltpu.VMEM((6, tok, lat // 2), BF),
            pltpu.VMEM((6, tok, lat // 2), BF),
            pltpu.VMEM((2, tok, lat), F32),
            pltpu.VMEM((rows, tok, width), BF),
            pltpu.VMEM((rows, tok, width), BF),
        ]
        + [dma((n,)) for n in (1, 6 * chips, chips - 1, 6, 3) for _ in range(2)]
        + [dma(())],
        compiler_params=remote_params(4),
        cost_estimate=pl.CostEstimate(
            flops=2 * rows * tok * lat * qup.shape[1] + 2 * rows * tok * width * model,
            bytes_accessed=230_000_000,
            transcendentals=0,
        ),
        name="tail_exchange",
    )(dq, qup, dkv, latent, lgain, cosine, sine, first_set, hidden_all, again)


def hidden_back_kernel(
    grads_ref, first_ref, hidden_ref, again_ref, middle_ref, term_ref, out_ref, grad_ref, gain_ref, parts, landed, kept, ours, theirs, z_landed, total, back, s1, r1, sc, rc, sz, rz, sb, rb, own
):
    rows, chips = ours.shape[:2]
    width = grads_ref.shape[2]
    row, seq = lax.axis_index("row"), lax.axis_index("seq")
    core, chip = seq % 2, seq // 2
    near = partners()
    later, twin = chip_partners(chips)
    greet([near[1], near[2], near[3]] + later + [twin])
    swap = send(term_ref.at[:, :, 1 - core], theirs, (sc, rc), 0, twin)
    load = pltpu.make_async_copy(term_ref.at[:, :, core], ours, own)
    load.start()

    def product(k, columns):
        return mm_nt(grads_ref[k], first_ref[columns, :width])

    begin, pass_on, finish = reduce_rows(product, near, parts, kept, landed, (s1, r1))
    begin()
    load.wait()
    swap.wait_recv()
    ours[...] = (ours[...].astype(F32) + theirs[...].astype(F32)).astype(BF)
    along = [
        send(ours.at[:, (chip + i) % chips], z_landed.at[i - 1], (sz, rz), i - 1, later[i - 1])
        for i in range(1, chips)
    ]
    pass_on()
    finish()
    again = again_ref[...]
    _, unit, inv = rms_forward(hidden_ref[...].astype(F32), again)
    out_ref[...] = middle_ref[...] + rms_backward(kept[0], unit, inv, again)
    sums = ours[:, chip].astype(F32)
    for i in range(1, chips):
        along[i - 1].wait_recv()
        sums = sums + z_landed[i - 1].astype(F32)
    total[...] = sums.astype(BF)
    last = [
        send(total.at[near[k][0]], back.at[row], (sb, rb), k - 1, near[k]) for k in range(1, rows)
    ]
    back[row] = total[row]
    for copy in last:
        copy.wait_recv()
    gain_ref[...] = jnp.zeros_like(gain_ref)
    for j in range(rows):
        grad_ref[:, j * width : (j + 1) * width] = back[j, :, :width].astype(F32)
        gain_ref[...] = gain_ref[...] + back[j, :, width:].astype(F32)
    for copy in [swap] + along + last:
        copy.wait_send()


def hidden_exchange(grads, first_set, hidden, again, grad_middle, term):
    rows, tok, width = grads.shape
    model = again.shape[1]
    _, chips, _, own, wide = term.shape
    dma = pltpu.SemaphoreType.DMA
    return pl.pallas_call(
        hidden_back_kernel,
        in_specs=[VMEM_SPEC] * 5 + [ANY_SPEC],
        out_specs=[VMEM_SPEC] * 3,
        out_shape=[
            jax.ShapeDtypeStruct((tok, model), F32),
            jax.ShapeDtypeStruct((own, rows * width), F32),
            jax.ShapeDtypeStruct((own, wide - width), F32),
        ],
        scratch_shapes=exchange_scratch(tok, model)[:3]
        + [
            pltpu.VMEM((rows, chips, own, wide), BF),
            pltpu.VMEM((rows, chips, own, wide), BF),
            pltpu.VMEM((chips - 1, rows, own, wide), BF),
            pltpu.VMEM((rows, own, wide), BF),
            pltpu.VMEM((rows, own, wide), BF),
        ]
        + [dma((n,)) for n in (6, 1, chips - 1, 3) for _ in range(2)]
        + [dma(())],
        compiler_params=remote_params(5),
        cost_estimate=pl.CostEstimate(
            flops=2 * rows * tok * width * model, bytes_accessed=110_000_000, transcendentals=0
        ),
        name="hidden_exchange",
    )(grads, first_set, hidden, again, grad_middle, term)


def last_kernel(oq_ref, back, s1, r1, own):
    rows, _, wide = back.shape
    row = lax.axis_index("row")
    columns = pl.ds(oq_ref.shape[2] - wide, wide)
    near = partners()
    greet([near[1], near[2], near[3]])
    copies = [
        send(oq_ref.at[near[k][0], :, columns], back.at[row], (s1, r1), k - 1, near[k])
        for k in range(1, rows)
    ]
    copies.append(pltpu.make_async_copy(oq_ref.at[row, :, columns], back.at[row], own))
    copies[-1].start()
    for copy in copies:
        copy.wait()


def last_exchange(oq, model):
    rows, own, total = oq.shape
    dma = pltpu.SemaphoreType.DMA
    return pl.pallas_call(
        last_kernel,
        in_specs=[VMEM_SPEC],
        out_specs=VMEM_SPEC,
        out_shape=jax.ShapeDtypeStruct((rows, own, total - model), BF),
        scratch_shapes=[dma((3,)), dma((3,)), dma(())],
        compiler_params=remote_params(8),
        cost_estimate=pl.CostEstimate(flops=0, bytes_accessed=10_000_000, transcendentals=0),
        name="last_exchange",
    )(oq)


def start_kernel(
    hidden_ref, gate_ref, up_ref, cut_ref, all_ref, ffn_ref, first_ref, s1, r1, sg, rg, sz, rz, sc, rc, own, own_ffn, own_cut
):
    row = lax.axis_index("row")
    rows = all_ref.shape[0]
    units = ffn_ref.shape[2] // 2
    chips = first_ref.shape[1]
    seq = lax.axis_index("seq")
    core, chip = seq % 2, seq // 2
    near = partners()
    later, twin = chip_partners(chips)
    greet([near[1], near[2], near[3]] + later + [twin])
    place = first_ref.at[:, chip, core]
    keep = pltpu.make_async_copy(cut_ref, place, own_cut)
    keep.start()
    along = [send(cut_ref, place, (sz, rz), i - 1, later[i - 1]) for i in range(1, chips)]
    shared = [send(cut_ref, place, (sc, rc), 0, twin)]
    cut = []

    def slices():
        for at, source_ref in ((0, gate_ref), (1, up_ref)):
            for k in range(rows):
                to = row if k == 0 else near[k][0]
                source = source_ref.at[:, pl.ds(pl.multiple_of(to * units, 128), units)]
                target = ffn_ref.at[row, :, pl.ds(at * units, units)]
                if k == 0:
                    copy = pltpu.make_async_copy(source, target, own_ffn.at[at])
                    copy.start()
                else:
                    copy = send(source, target, (sg, rg), 3 * at + k - 1, near[k])
                cut.append(copy)

    gather_rows(hidden_ref, all_ref, near, (s1, r1), own, slices)
    for i in range(1, chips):
        along[i - 1].wait_recv()
        block = first_ref.at[:, (chip + chips - i) % chips, core]
        shared.append(send(block, block, (sc, rc), i, twin))
    keep.wait()
    for copy in cut:
        copy.wait()
    for copy in shared:
        copy.wait_recv()
    for copy in along + shared:
        copy.wait_send()


def start_exchange(hidden, gate, up, first_cut, chips):
    rows, own, wide = first_cut.shape
    dma = pltpu.SemaphoreType.DMA
    return pl.pallas_call(
        start_kernel,
        in_specs=[ANY_SPEC] * 4,
        out_specs=[ANY_SPEC] * 3,
        out_shape=[
            jax.ShapeDtypeStruct((rows,) + hidden.shape, BF),
            jax.ShapeDtypeStruct((rows, gate.shape[0], 2 * gate.shape[1] // rows), BF),
            jax.ShapeDtypeStruct((rows, chips, 2, own, wide), BF),
        ],
        scratch_shapes=[dma((n,)) for n in (6, 6, chips - 1, chips) for _ in range(2)]
        + [dma(()), dma((2,)), dma(())],
        compiler_params=remote_params(6),
        cost_estimate=pl.CostEstimate(flops=0, bytes_accessed=120_000_000, transcendentals=0),
        name="start_exchange",
    )(hidden, gate, up, first_cut)


def front_kernel(
    hidden_ref, first_ref, again_ref, lgain_ref, cos_ref, sin_ref, latent_ref, lat_all_ref, kv_ref, first_low, pieces, landed, lat_mine, kv_mine, sa, ra, sl, rl, sz, rz, sr, rr, sf, rf, sc, rc, own_sem
):
    rows, tok, model = hidden_ref.shape
    chips = kv_ref.shape[1]
    width = pieces.shape[2]
    lat = latent_ref.shape[1]
    head = kv_ref.shape[4] // 2
    row, seq = lax.axis_index("row"), lax.axis_index("seq")
    core, chip = seq % 2, seq // 2
    near = partners()
    later, twin = chip_partners(chips)
    greet([near[1], near[2], near[3]] + later + [twin])

    again = again_ref[...]
    copies = []
    for k in (3, 2, 1, 0):
        first_low[...] = rms_forward(hidden_ref[k].astype(F32), again)[0].astype(BF)
        piece = mm(first_low[...], first_ref[:, :width]).astype(BF)
        if k:
            pieces[k] = piece
            copies.append(send(pieces.at[k], landed.at[row], (sa, ra), k - 1, near[k]))
        else:
            landed[row] = piece
    for copy in copies:
        copy.wait_recv()
    joined = jnp.concatenate([landed[j] for j in range(rows)], axis=1)
    key = rotate(joined[:, lat : lat + head].astype(F32), cos_ref[...], sin_ref[...])
    kv_mine[:, :head] = key.astype(BF)
    kv_mine[:, head:] = joined[:, lat + head :]

    own = pltpu.make_async_copy(kv_mine, kv_ref.at[0, chip, core], own_sem.at[0])
    own.start()
    along = [
        send(kv_mine, kv_ref.at[0, chip, core], (sz, rz), i - 1, later[i - 1])
        for i in range(1, chips)
    ]
    low, high = pl.ds(0, tok // 2), pl.ds(tok // 2, tok // 2)
    across, passed = [], []

    def block(i):
        return (chip + chips - i) % chips

    def spread(i):
        source = kv_mine if i == 0 else kv_ref.at[0, block(i), core]
        for k in (1, 2):
            across.append(
                send(source, kv_ref.at[k, block(i), core], (sr, rr), 2 * i + k - 1, near[k])
            )

    def pass_on(i):
        across[2 * i].wait_recv()
        source = kv_ref.at[1, block(i), core, low]
        passed.append(send(source, kv_ref.at[3, block(i), core, low], (sf, rf), 2 * i, near[2]))
        across[2 * i + 1].wait_recv()
        source = kv_ref.at[2, block(i), core, high]
        passed.append(
            send(source, kv_ref.at[3, block(i), core, high], (sf, rf), 2 * i + 1, near[1])
        )

    spread(0)
    latent = joined[:, :lat].astype(F32)
    latent_ref[...] = latent
    lat_mine[...] = rms_forward(latent, lgain_ref[...])[0].astype(BF)
    lat_own = pltpu.make_async_copy(lat_mine, lat_all_ref.at[0], own_sem.at[1])
    lat_own.start()
    lat_copies = [
        send(lat_mine, lat_all_ref.at[k], (sl, rl), k - 1, near[k]) for k in range(1, rows)
    ]
    for i in range(1, chips):
        along[i - 1].wait_recv()
        spread(i)
        pass_on(i - 1)
    own.wait()
    shared = [send(kv_ref.at[0, :, core], kv_ref.at[0, :, core], (sc, rc), 0, twin)]
    pass_on(chips - 1)
    for k in (1, 2):
        shared.append(send(kv_ref.at[k, :, core], kv_ref.at[k, :, core], (sc, rc), k, twin))
    for copy in passed:
        copy.wait_recv()
    shared.append(send(kv_ref.at[3, :, core], kv_ref.at[3, :, core], (sc, rc), 3, twin))
    for copy in lat_copies + shared:
        copy.wait_recv()
    for copy in copies + along + across + passed + lat_copies + shared:
        copy.wait_send()
    lat_own.wait()


def front_exchange(hidden_all, first_set, again, lgain, cosine, sine, chips, width, head):
    rows, tok, model = hidden_all.shape
    lat = lgain.shape[1]
    dma = pltpu.SemaphoreType.DMA
    pairs = [3, 3, chips - 1, 2 * chips, 2 * chips, 4]
    return pl.pallas_call(
        front_kernel,
        in_specs=[VMEM_SPEC] * 6,
        out_specs=[VMEM_SPEC, ANY_SPEC, ANY_SPEC],
        out_shape=[
            jax.ShapeDtypeStruct((tok, lat), F32),
            jax.ShapeDtypeStruct((rows, tok, lat), BF),
            jax.ShapeDtypeStruct((rows, chips, 2, tok, 2 * head), BF),
        ],
        scratch_shapes=[
            pltpu.VMEM((tok, model), BF),
            pltpu.VMEM((rows, tok, width), BF),
            pltpu.VMEM((rows, tok, width), BF),
            pltpu.VMEM((tok, lat), BF),
            pltpu.VMEM((tok, 2 * head), BF),
        ]
        + [dma((n,)) for n in pairs for _ in range(2)]
        + [dma((2,))],
        compiler_params=remote_params(3),
        cost_estimate=pl.CostEstimate(
            flops=2 * rows * tok * model * width, bytes_accessed=230_000_000, transcendentals=0
        ),
        name="front_exchange",
    )(hidden_all, first_set, again, lgain, cosine, sine)


def deal_kernel(first_ref, qup_ref, lens_ref, cut_ref, qup_cut_ref, lens_all, sf, rf, sq, rq, sl, rl, own):
    row = lax.axis_index("row")
    rows, _, wide = cut_ref.shape
    units = qup_cut_ref.shape[2]
    near = partners()
    greet([near[1], near[2], near[3]])
    copies = []
    for k in (3, 1, 2, 0):
        to = row if k == 0 else near[k][0]
        moves = [
            (first_ref.at[to], cut_ref.at[row], (sf, rf)),
            (
                qup_ref.at[:, pl.ds(pl.multiple_of(to * units, 128), units)],
                qup_cut_ref.at[row],
                (sq, rq),
            ),
            (lens_ref, lens_all.at[k], (sl, rl)),
        ]
        for at, (source, target, sems) in enumerate(moves):
            if k:
                copies.append(send(source, target, sems, k - 1, near[k]))
            else:
                copies.append(pltpu.make_async_copy(source, target, own.at[at]))
                copies[-1].start()
    for copy in copies:
        copy.wait()


def deal_exchange(first, qup, lens):
    rows = first.shape[0]
    dma = pltpu.SemaphoreType.DMA
    return pl.pallas_call(
        deal_kernel,
        in_specs=[VMEM_SPEC] * 3,
        out_specs=[VMEM_SPEC] * 3,
        out_shape=[
            jax.ShapeDtypeStruct(first.shape, BF),
            jax.ShapeDtypeStruct((rows, qup.shape[0], qup.shape[1] // rows), BF),
            jax.ShapeDtypeStruct((rows,) + lens.shape, lens.dtype),
        ],
        scratch_shapes=[dma((3,))] * 6 + [dma((3,))],
        compiler_params=remote_params(7),
        cost_estimate=pl.CostEstimate(flops=0, bytes_accessed=10_000_000, transcendentals=0),
        name="deal_exchange",
    )(first, qup, lens)


def ffn_grad_kernel(second_ref, gate_hbm, up_hbm, out_ref, both, mine, theirs, ss, rs, load_sems, out_sems):
    rows = mine.shape[0]
    units = gate_hbm.shape[1]
    block = second_ref.shape[1] // rows
    row = lax.axis_index("row")
    core = lax.axis_index("seq") % 2
    _, twin = chip_partners(mine.shape[1])
    loads = [
        pltpu.make_async_copy(gate_hbm, both.at[:, pl.ds(0, units)], load_sems.at[0]),
        pltpu.make_async_copy(up_hbm, both.at[:, pl.ds(units, units)], load_sems.at[1]),
    ]
    for copy in loads:
        copy.start()
    greet([twin])
    for copy in loads:
        copy.wait()

    def swap(r):
        return pltpu.make_async_remote_copy(
            src_ref=mine.at[r, :, 1 - core],
            dst_ref=theirs.at[r],
            send_sem=ss.at[r],
            recv_sem=rs.at[r],
            device_id=twin,
            device_id_type=MESH,
        )

    def compute(r, carry):
        owner = 2 * ((row // 2 + r // 2) % 2) + (row + r) % 2
        left = second_ref[:, pl.ds(pl.multiple_of(owner * block, block), block)]
        mine[r] = mm_tn(left, both[...]).astype(BF).reshape(mine.shape[1:])
        swap(r).start()
        return carry

    lax.fori_loop(0, rows, compute, 0)
    outs = []
    for r in range(rows):
        swap(r).wait_recv()
        theirs[r] = (mine[r, :, core].astype(F32) + theirs[r].astype(F32)).astype(BF)
        outs.append(pltpu.make_async_copy(theirs.at[r], out_ref.at[r], out_sems.at[r]))
        outs[-1].start()
    for r in range(rows):
        swap(r).wait_send()
        outs[r].wait()


def ffn_grad(second, gate, up, rows, chips):
    tokens, model = second.shape
    units = gate.shape[1]
    own = model // rows // chips // 2
    dma = pltpu.SemaphoreType.DMA
    return pl.pallas_call(
        ffn_grad_kernel,
        in_specs=[VMEM_SPEC] + [ANY_SPEC] * 2,
        out_specs=ANY_SPEC,
        out_shape=jax.ShapeDtypeStruct((rows, chips, own, 2 * units), BF),
        scratch_shapes=[
            pltpu.VMEM((tokens, 2 * units), BF),
            pltpu.VMEM((rows, chips, 2, own, 2 * units), BF),
            pltpu.VMEM((rows, chips, own, 2 * units), BF),
        ]
        + [dma((rows,)), dma((rows,)), dma((2,)), dma((rows,))],
        compiler_params=remote_params(9),
        cost_estimate=pl.CostEstimate(
            flops=4 * tokens * units * model, bytes_accessed=40_000_000, transcendentals=0
        ),
        name="ffn_grad",
    )(second, gate, up)


def move_row(value, k, rows):
    return lax.ppermute(value, "row", [(i, i ^ k) for i in range(rows)])


def in_row_order(pieces):
    rows, me = lax.axis_size("row"), lax.axis_index("row")
    return jnp.stack(
        [lax.select_n(me, *[pieces[j ^ i] for i in range(rows)]) for j in range(rows)]
    )


def join_columns(blocks):
    rows, n, width = blocks.shape
    return blocks.transpose(1, 0, 2).reshape(n, rows * width)


def scatter_seq(v, axis=0):
    return lax.psum_scatter(v.astype(BF), "seq", scatter_dimension=axis, tiled=True)


def on_device(
    hidden,
    cotangent,
    lengths,
    attn_gain,
    query_down,
    latent_gain,
    query_up,
    key_proj,
    value_proj,
    out_proj,
    ffn_gain,
    gate_proj,
    up_proj,
    down_proj,
):
    tok = hidden.shape[1]
    model = hidden.shape[2]
    rows = lax.axis_size("row")
    spread = lax.axis_size("seq")
    row_index = lax.axis_index("row")
    seq_index = lax.axis_index("seq")
    first_slot = seq_index * tok
    head = key_proj.shape[1]
    lat = query_down.shape[1]
    heads = query_up.shape[1] // head // rows
    units = down_proj.shape[0] * spread
    scale = head ** (-0.5)
    own = query_down.shape[0]
    lat_own = latent_gain.shape[0]

    first_own = jnp.concatenate([query_down, key_proj, value_proj], axis=1)
    first_width = first_own.shape[1] // rows
    gain_own = jnp.stack([attn_gain, ffn_gain, jnp.pad(latent_gain, (0, own - lat_own))], axis=1)
    gain_own = jnp.pad(gain_own, ((0, 0), (0, 125)))
    first_own = jnp.stack(
        [
            jnp.concatenate([first_own[:, j * first_width : (j + 1) * first_width], gain_own], axis=1)
            for j in range(rows)
        ]
    )
    docs = lengths.shape[1]
    first_cut, qup_cut, lens = deal_exchange(
        first_own, query_up, jnp.pad(lengths, ((0, 0), (0, 128 - docs)))
    )
    lens = lens[:, 0, :docs]
    oq_own = jnp.concatenate([out_proj, qup_cut.reshape(out_proj.shape[0], -1)], axis=1)
    full_oq = lax.all_gather(oq_own, "seq", axis=0, tiled=True)
    hidden_all, ffn_cut, first_set = start_exchange(
        hidden[0], gate_proj, up_proj, first_cut, spread // 2
    )
    first_set = first_set.reshape(model, -1)
    full_ffn = lax.all_gather(ffn_cut, "seq", axis=1, tiled=True).reshape(model, -1)
    full_down = lax.all_gather(down_proj, "seq", axis=0, tiled=True)
    full_gains = first_set[:, first_width:].astype(F32)
    full_again = full_gains[:, 0]
    full_fgain = full_gains[:, 1]
    full_lgain = full_gains[:, 2].reshape(rows * spread, own)[:, :lat_own].reshape(lat)
    full_qup = full_oq[:, model:].reshape(spread, rows, lat_own, -1).transpose(1, 0, 2, 3)
    full_qup = full_qup.reshape(lat, heads * head)
    position = document_positions(lens, first_slot + jnp.arange(tok, dtype=jnp.int32))
    cosine, sine = rope_tables(position, head)

    residual_all = hidden_all.astype(F32)
    first_low = rms_forward(residual_all, full_again)[0].astype(BF).reshape(rows * tok, model)
    latent, latent_all, key_value = front_exchange(
        hidden_all,
        first_set,
        full_again[None],
        full_lgain[None],
        cosine[0],
        sine[0],
        spread // 2,
        first_width,
        head,
    )
    key_value = key_value.reshape(rows, spread * tok, 2 * head)
    grad_own, latent_all = lax.optimization_barrier((cotangent[0], latent_all))
    grad_pieces = [move_row(grad_own, k, rows) for k in range(1, rows)]
    query_low, attend, attend_low, stats = attend_forward(
        heads, scale, lens, latent_all, full_qup, cosine, sine, key_value
    )
    middle, second_all = branch_exchange(attend_low, full_oq, hidden[0], full_fgain[None])
    grad_pieces, second_all = lax.optimization_barrier((grad_pieces, second_all))
    grad_all = jnp.stack([cotangent[0]] + grad_pieces).reshape(rows * tok, model)
    second_all = second_all.reshape(rows * tok, model)
    both = mm(second_all, full_ffn)
    gate_pre, upward = both[:, :units], both[:, units:]
    gate_sig = jax.nn.sigmoid(gate_pre)
    gate_act = gate_pre * gate_sig
    act_low = (gate_act * upward).astype(BF)
    down_part = mm_tn(act_low, grad_all).astype(BF)
    down_grad = scatter_seq(down_part)
    full_down, down_order = lax.optimization_barrier((full_down, down_part))
    grad_act = mm_nt(grad_all, full_down)
    slope = gate_sig * (1.0 + gate_pre * (1.0 - gate_sig))
    grad_gate = (grad_act * upward * slope).astype(BF)
    grad_upward = (grad_act * gate_act).astype(BF)
    ffn_term = ffn_grad(second_all, grad_gate, grad_upward, rows, spread // 2)
    ffn_part = lax.psum_scatter(
        ffn_term.reshape(rows, model // rows // 2, -1),
        "seq",
        scatter_dimension=1,
        axis_index_groups=[list(range(core, spread, 2)) for core in range(2)],
        tiled=True,
    )
    grad_gate, ffn_term = lax.optimization_barrier((grad_gate, ffn_term))
    grad_middle, ffn_gain_part, branch_all, layer_part = second_exchange(
        grad_gate.reshape(rows, tok, units),
        grad_upward.reshape(rows, tok, units),
        full_ffn,
        act_low.reshape(rows, tok, units),
        full_down,
        middle,
        cotangent[0],
        full_fgain[None],
        down_order,
    )
    ffn_gain_part = ffn_gain_part[0]
    layer_pieces = [move_row(layer_part[k], k, rows) for k in range(1, rows)]
    grad_query, kv_part, oq_part = attend_backward(
        heads,
        scale,
        lens,
        query_low,
        key_value,
        branch_all,
        full_oq,
        attend_low,
        latent_all,
        attend,
        stats,
        cosine,
        sine,
    )
    grad_query, oq_part, down_grad, layer_pieces = lax.optimization_barrier(
        (grad_query, oq_part, down_grad, layer_pieces)
    )
    oq_part = scatter_seq(oq_part)
    layer_sum = middle + layer_part[0].astype(F32)
    for piece in layer_pieces:
        layer_sum = layer_sum + piece.astype(F32)
    layer_out = layer_sum.astype(BF)
    grad_first_all, latent_gain_part, attn_gain_part = tail_exchange(
        grad_query,
        full_qup,
        kv_part.reshape(rows, spread // 2, 2, tok, 2 * head),
        latent,
        full_lgain[None],
        cosine[0],
        sine[0],
        first_set,
        hidden_all,
        full_again[None],
        first_width,
    )
    lgain_part = jnp.pad(
        latent_gain_part.reshape(rows * spread, lat_own), ((0, 0), (0, own - lat_own))
    ).reshape(model)
    gain_parts = jnp.stack([attn_gain_part[0], ffn_gain_part, lgain_part], axis=1)
    first_term = mm_tn(first_low, grad_first_all.reshape(rows * tok, first_width))
    first_term = jnp.concatenate(
        [first_term, jnp.pad(gain_parts, ((0, 0), (0, 125)))], axis=1
    ).astype(BF)
    grad_first_all, ffn_part = lax.optimization_barrier((grad_first_all, ffn_part))
    ffn_pieces = [ffn_part[0]] + [move_row(ffn_part[k], k, rows) for k in range(1, rows)]
    hidden_grad, first_grad, gain_grad = hidden_exchange(
        grad_first_all,
        first_set,
        hidden[0],
        full_again[None],
        grad_middle,
        first_term.reshape(rows, spread // 2, 2, own, -1),
    )
    hidden_grad, oq_part, ffn_pieces = lax.optimization_barrier((hidden_grad, oq_part, ffn_pieces))
    ffn_back = in_row_order(ffn_pieces)
    query_up_grad = last_exchange(oq_part.reshape(rows, lat_own, -1), model)
    query_up_grad = join_columns(query_up_grad).astype(F32)
    out_grad = oq_part[:, :model].astype(F32)
    gate_grad = join_columns(ffn_back[:, :, :units]).astype(F32)
    up_grad = join_columns(ffn_back[:, :, units:]).astype(F32)
    return (
        layer_out[None],
        hidden_grad[None],
        gain_grad[:, 0],
        first_grad[:, :lat],
        gain_grad[:lat_own, 2],
        query_up_grad,
        first_grad[:, lat : lat + head],
        first_grad[:, lat + head :],
        out_grad,
        gain_grad[:, 1],
        gate_grad,
        up_grad,
        down_grad.astype(F32),
    )


def solution(mesh):
    token = P("row", "seq", None)
    vector = P(("row", "seq"))
    matrix = P(("row", "seq"), None)
    return jax.shard_map(
        on_device,
        mesh=mesh,
        in_specs=(token, token, P("row", None), vector, matrix, vector)
        + (matrix,) * 4
        + (vector,)
        + (matrix,) * 3,
        out_specs=(token, token, vector, matrix, vector)
        + (matrix,) * 4
        + (vector,)
        + (matrix,) * 3,
        check_vma=False,
    )
```

```python
import functools
import math

import jax
import jax.numpy as jnp
from jax import lax
from jax.experimental import pallas as pl
from jax.experimental.pallas import tpu as pltpu
from jax.sharding import PartitionSpec as P

epsilon = 1e-06
masked_value = -1e30
BF = jnp.bfloat16
F32 = jnp.float32
VMEM_BYTES = 60 * 1024 * 1024


def rms_forward(values, gain):
    inv_rms = lax.rsqrt(jnp.mean(values * values, axis=-1, keepdims=True) + epsilon)
    normed = values * inv_rms
    return (normed * gain, normed, inv_rms)


def rms_backward(incoming, normed, inv_rms, gain):
    grad_normed = incoming * gain
    inner = jnp.mean(grad_normed * normed, axis=-1, keepdims=True)
    return inv_rms * (grad_normed - normed * inner)


def document_positions(lengths, slots):
    ends = jnp.cumsum(lengths, axis=1)
    is_past = slots[None, :, None] >= ends[:, None, :]
    begin = jnp.sum(jnp.where(is_past, lengths[:, None, :], 0), axis=2)
    return slots[None, :] - begin


def rope_tables(position, head_size):
    half_dim = head_size // 2
    frequency = jnp.exp(jnp.arange(half_dim, dtype=F32) * (-2.0 * math.log(10000.0) / head_size))
    angles = position.astype(F32)[..., None] * frequency
    return (jnp.cos(angles), jnp.sin(angles))


def rotate(values, cosine, sine_table):
    half = values.shape[-1] // 2
    front, behind = values[..., :half], values[..., half:]
    return jnp.concatenate(
        [front * cosine - behind * sine_table, behind * cosine + front * sine_table], axis=-1
    )


def rotate_back(grads, cosine, sine_table):
    half = grads.shape[-1] // 2
    front, behind = grads[..., :half], grads[..., half:]
    return jnp.concatenate(
        [front * cosine + behind * sine_table, behind * cosine - front * sine_table], axis=-1
    )


def dot(a, b, dims):
    return lax.dot_general(a, b, (dims, ((), ())), preferred_element_type=F32)


def mm(a, b):
    return dot(a, b, ((1,), (0,)))


def mm_nt(a, b):
    return dot(a, b, ((1,), (1,)))


def mm_tn(a, b):
    return dot(a, b, ((0,), (0,)))


KEYS = 256


def visible(lens_ref, row, first_slot, tok):
    slot = first_slot + lax.broadcasted_iota(jnp.int32, (tok, 1), 0)
    low = jnp.zeros((tok, 1), jnp.int32)
    first_low = jnp.int32(0)
    end = jnp.int32(0)
    docs = lens_ref.shape[1]
    for doc in range(docs):
        end = end + lens_ref[row, doc]
        if doc < docs - 1:
            low = jnp.where(slot >= end, end, low)
            first_low = jnp.where(first_slot >= end, end, first_low)
        else:
            low = jnp.where(slot >= end, slot, low)
            first_low = jnp.where(first_slot >= end, first_slot, first_low)
    first_step = first_low // KEYS
    last_step = (first_slot + tok + KEYS - 1) // KEYS
    return (slot, low, first_step, last_step)


def stack_heads(ref_or_value, heads, head):
    return jnp.concatenate(
        [ref_or_value[:, h * head : (h + 1) * head] for h in range(heads)], axis=0
    )


def attend_kernel(
    heads, scale, lens_ref, lat_ref, qup_ref, cos_ref, sin_ref, kv_ref, q_ref, out_ref, low_ref, stats_ref, score_ref
):
    row = pl.program_id(0)
    tok = lat_ref.shape[1]
    head = kv_ref.shape[2] // 2
    first_slot = lax.axis_index("seq") * tok
    slot, low, first_step, last_step = visible(lens_ref, row, first_slot, tok)
    slot = jnp.concatenate([slot] * heads, axis=0)
    low = jnp.concatenate([low] * heads, axis=0)
    queries = mm(lat_ref[0], qup_ref[...])
    cosine, sine = cos_ref[0], sin_ref[0]
    for h in range(heads):
        q_ref[0, :, h * head : (h + 1) * head] = rotate(
            queries[:, h * head : (h + 1) * head], cosine, sine
        ).astype(BF)
    query = stack_heads(q_ref[0], heads, head)

    def keys_of(step):
        return pl.ds(pl.multiple_of(step * KEYS, KEYS), KEYS)

    def score_step(step, row_max):
        score = mm_nt(query, kv_ref[0, keys_of(step), :head]) * scale
        key_slot = step * KEYS + lax.broadcasted_iota(jnp.int32, (1, KEYS), 1)
        score = jnp.where((key_slot >= low) & (key_slot <= slot), score, masked_value)
        score_ref[step] = score
        return jnp.maximum(row_max, jnp.max(score, axis=1, keepdims=True))

    row_max = lax.fori_loop(
        first_step, last_step, score_step, jnp.full((heads * tok, 1), masked_value, F32)
    )

    def value_step(step, carry):
        row_total, weighted = carry
        weight = jnp.exp(score_ref[step] - row_max)
        row_total = row_total + jnp.sum(weight, axis=1, keepdims=True)
        weighted = weighted + mm(weight.astype(BF), kv_ref[0, keys_of(step), head:])
        return (row_total, weighted)

    row_total, weighted = lax.fori_loop(
        first_step,
        last_step,
        value_step,
        (jnp.zeros((heads * tok, 1), F32), jnp.zeros((heads * tok, head), F32)),
    )
    attend = weighted / row_total
    lane = lax.broadcasted_iota(jnp.int32, (tok, 128), 1)
    stats = jnp.zeros((tok, 128), F32)
    for h in range(heads):
        rows = slice(h * tok, (h + 1) * tok)
        out_ref[0, :, h * head : (h + 1) * head] = attend[rows]
        low_ref[0, :, h * head : (h + 1) * head] = attend[rows].astype(BF)
        stats = jnp.where(lane == h, row_max[rows], stats)
        stats = jnp.where(lane == heads + h, row_total[rows], stats)
    stats_ref[0] = stats


def attend_back_kernel(
    heads, scale, lens_ref, q_ref, kv_ref, branch_ref, proj_ref, branch_all_ref, low_ref, lat_ref, out_ref, stats_ref, cos_ref, sin_ref, dq_ref, dkv_ref, oq_ref, dq_all
):
    row = pl.program_id(0)
    tok = q_ref.shape[1]
    head = kv_ref.shape[2] // 2
    first_slot = lax.axis_index("seq") * tok
    slot, low, first_step, last_step = visible(lens_ref, row, first_slot, tok)
    slot = jnp.concatenate([slot] * heads, axis=0)
    low = jnp.concatenate([low] * heads, axis=0)
    query = stack_heads(q_ref[0], heads, head)
    branch = branch_ref[0]
    grad = jnp.concatenate(
        [mm_nt(branch, proj_ref[h * head : (h + 1) * head, :]) for h in range(heads)], axis=0
    )
    attend = stack_heads(out_ref[0], heads, head)
    stats = stats_ref[0]
    row_max = jnp.concatenate([stats[:, h : h + 1] for h in range(heads)], axis=0)
    row_total = jnp.concatenate(
        [stats[:, heads + h : heads + h + 1] for h in range(heads)], axis=0
    )
    grad_weighted = (grad / row_total).astype(BF)
    delta = jnp.sum(grad * attend, axis=1, keepdims=True) / row_total
    dkv_ref[...] = jnp.zeros_like(dkv_ref)

    def step_back(step, grad_query):
        keys = pl.ds(pl.multiple_of(step * KEYS, KEYS), KEYS)
        key, value = kv_ref[0, keys, :head], kv_ref[0, keys, head:]
        score = mm_nt(query, key) * scale
        key_slot = step * KEYS + lax.broadcasted_iota(jnp.int32, (1, KEYS), 1)
        allowed = (key_slot >= low) & (key_slot <= slot)
        weight = jnp.exp(jnp.where(allowed, score - row_max, masked_value))
        grad_weight = mm_nt(grad_weighted, value)
        grad_score = (weight * (grad_weight - delta)).astype(BF)
        dkv_ref[0, keys, :head] = (mm_tn(grad_score, query) * scale).astype(BF)
        dkv_ref[0, keys, head:] = mm_tn(weight.astype(BF), grad_weighted).astype(BF)
        return grad_query + mm(grad_score, key)

    grad_query = lax.fori_loop(
        first_step, last_step, step_back, jnp.zeros((heads * tok, head), F32)
    )
    cosine, sine = cos_ref[0], sin_ref[0]
    for h in range(heads):
        dq_ref[0, :, h * head : (h + 1) * head] = rotate_back(
            grad_query[h * tok : (h + 1) * tok] * scale, cosine, sine
        ).astype(BF)
        dq_all[row, :, h * head : (h + 1) * head] = dq_ref[0, :, h * head : (h + 1) * head]

    @pl.when(row == pl.num_programs(0) - 1)
    def _():
        weight_grads(low_ref, branch_all_ref, lat_ref, dq_all, oq_ref)


def weight_grads(low_ref, branch_ref, lat_ref, dq_ref, oq_ref):
    model, width = branch_ref.shape[2], dq_ref.shape[2]
    lat = lat_ref.shape[2]
    rows, spread = lax.axis_size("row"), lax.axis_size("seq")
    own = lat // rows // spread
    right = branch_ref[...].reshape(-1, model)
    tile = 256

    def out_tile(t, carry):
        at = pl.ds(pl.multiple_of(t * tile, tile), tile)
        left = low_ref[:, :, at].reshape(-1, tile)
        oq_ref[at, :model] = mm_tn(left, right).astype(BF)
        return carry

    lax.fori_loop(0, low_ref.shape[2] // tile, out_tile, 0)
    right_lat = dq_ref[...].reshape(-1, width)
    block = lat // rows
    if own % 16 == 0:
        for r in range(rows):
            left = lat_ref[:, :, r * block : (r + 1) * block].reshape(-1, block)
            product = mm_tn(left, right_lat).astype(BF)
            for seq in range(spread):
                at = (seq * rows + r) * own
                oq_ref[at : at + own, model:] = product[seq * own : (seq + 1) * own]
    else:
        product = mm_tn(lat_ref[...].reshape(-1, lat), right_lat)
        for seq in range(spread):
            pieces = [
                product[(r * spread + seq) * own : (r * spread + seq + 1) * own] for r in range(rows)
            ]
            oq_ref[seq * rows * own : (seq + 1) * rows * own, model:] = jnp.concatenate(
                pieces, axis=0
            ).astype(BF)


def row_block(shape):
    return pl.BlockSpec((1,) + shape[1:], lambda i: (i, 0, 0))


def whole_block(shape):
    return pl.BlockSpec(shape, lambda i: (0,) * len(shape))


def kernel_params():
    return pltpu.CompilerParams(
        dimension_semantics=("arbitrary",), vmem_limit_bytes=VMEM_BYTES
    )


def attend_forward(heads, scale, lens, lat, qup, cosine, sine, kv):
    rows, tok, _ = lat.shape
    slots = kv.shape[1]
    wide = (rows, tok, qup.shape[1])
    flops = rows * tok * (2 * lat.shape[2] * qup.shape[1] + 4 * slots * qup.shape[1])
    return pl.pallas_call(
        functools.partial(attend_kernel, heads, scale),
        grid=(rows,),
        in_specs=[pl.BlockSpec(memory_space=pltpu.SMEM)]
        + [row_block(lat.shape), whole_block(qup.shape)]
        + [row_block(cosine.shape), row_block(sine.shape), row_block(kv.shape)],
        out_specs=[row_block(wide), row_block(wide), row_block(wide), row_block((rows, tok, 128))],
        out_shape=[
            jax.ShapeDtypeStruct(wide, BF),
            jax.ShapeDtypeStruct(wide, F32),
            jax.ShapeDtypeStruct(wide, BF),
            jax.ShapeDtypeStruct((rows, tok, 128), F32),
        ],
        scratch_shapes=[pltpu.VMEM((slots // KEYS, heads * tok, KEYS), F32)],
        compiler_params=kernel_params(),
        cost_estimate=pl.CostEstimate(
            flops=flops, bytes_accessed=16 * 1024 * 1024, transcendentals=rows * tok * heads * slots
        ),
        name="attend_forward",
    )(lens, lat, qup, cosine, sine, kv)


def attend_backward(
    heads, scale, lens, query, kv, branch, oq, low, lat, attend, stats, cosine, sine
):
    rows, tok, width = query.shape
    model = branch.shape[2]
    slots = kv.shape[1]
    return pl.pallas_call(
        functools.partial(attend_back_kernel, heads, scale),
        grid=(rows,),
        in_specs=[pl.BlockSpec(memory_space=pltpu.SMEM)]
        + [row_block(v.shape) for v in (query, kv, branch)]
        + [pl.BlockSpec((width, model), lambda i: (0, 0), pipeline_mode=pl.Buffered(1))]
        + [
            pl.BlockSpec(v.shape, lambda i: (0, 0, 0), pipeline_mode=pl.Buffered(1))
            for v in (branch, low, lat)
        ]
        + [row_block(v.shape) for v in (attend, stats, cosine, sine)],
        out_specs=[row_block(query.shape), row_block(kv.shape)]
        + [pl.BlockSpec(oq.shape, lambda i: (0, 0), pipeline_mode=pl.Buffered(1))],
        out_shape=[
            jax.ShapeDtypeStruct(query.shape, BF),
            jax.ShapeDtypeStruct(kv.shape, BF),
            jax.ShapeDtypeStruct(oq.shape, BF),
        ],
        scratch_shapes=[pltpu.VMEM(query.shape, BF)],
        compiler_params=kernel_params(),
        cost_estimate=pl.CostEstimate(
            flops=rows * tok * 10 * slots * width,
            bytes_accessed=100_000_000,
            transcendentals=rows * tok * heads * slots,
        ),
        name="attend_backward",
    )(lens, query, kv, branch, oq, branch, low, lat, attend, stats, cosine, sine)


MESH = pl.DeviceIdType.MESH


def partners():
    row, seq = lax.axis_index("row"), lax.axis_index("seq")
    return {1: (row + 1 - 2 * (row % 2), seq), 2: ((row + 2) % 4, seq), 3: (3 - row, seq)}


def chip_partners(chips):
    row, seq = lax.axis_index("row"), lax.axis_index("seq")
    later = [(row, (seq + 2 * i) % (2 * chips)) for i in range(1, chips)]
    return later, (row, seq + 1 - 2 * (seq % 2))


def greet(devices):
    barrier = pltpu.get_barrier_semaphore()
    for device in devices:
        pl.semaphore_signal(barrier, inc=1, device_id=device, device_id_type=MESH)
    pl.semaphore_wait(barrier, len(devices))


def send(source, target, sems, at, device):
    copy = pltpu.make_async_remote_copy(
        src_ref=source,
        dst_ref=target,
        send_sem=sems[0].at[at],
        recv_sem=sems[1].at[at],
        device_id=device,
        device_id_type=MESH,
    )
    copy.start()
    return copy


TILE = 512


def reduce_rows(product, near, parts, kept, landed, sems, ready=None):
    half = parts.shape[2]
    tiles = half // TILE

    def compute(k, side, store):
        if ready is not None:
            ready(k, side)

        def tile(t, carry):
            local = pl.ds(pl.multiple_of(t * TILE, TILE), TILE)
            columns = pl.ds(pl.multiple_of(side * half + t * TILE, TILE), TILE)
            store(local, columns, product(k, columns))
            return carry

        lax.fori_loop(0, tiles, tile, 0)

    def into_parts(at):
        def store(local, columns, value):
            parts[at, :, local] = value.astype(BF)

        return store

    def into_kept(at):
        def store(local, columns, value):
            kept[at, :, columns] = value

        return store

    copies = []

    def begin():
        for at, (k, side, to) in enumerate([(3, 0, 1), (3, 1, 2), (1, 0, 1), (2, 1, 2)]):
            compute(k, side, into_parts(at))
            copies.append(send(parts.at[at], landed.at[at], sems, at, near[to]))
        compute(2, 0, into_kept(1))
        compute(1, 1, into_kept(1))

    def pass_on():
        copies[0].wait_recv()
        parts[4] = (kept[1, :, :half] + landed[0].astype(F32)).astype(BF)
        copies.append(send(parts.at[4], landed.at[4], sems, 4, near[2]))
        copies[1].wait_recv()
        parts[5] = (kept[1, :, half:] + landed[1].astype(F32)).astype(BF)
        copies.append(send(parts.at[5], landed.at[5], sems, 5, near[1]))

    def finish():
        compute(0, 0, into_kept(0))
        compute(0, 1, into_kept(0))
        copies[2].wait_recv()
        copies[3].wait_recv()
        kept[0, :, :half] = kept[0, :, :half] + landed[2].astype(F32)
        kept[0, :, half:] = kept[0, :, half:] + landed[3].astype(F32)
        copies[4].wait_recv()
        copies[5].wait_recv()
        kept[0, :, :half] = kept[0, :, :half] + landed[4].astype(F32)
        kept[0, :, half:] = kept[0, :, half:] + landed[5].astype(F32)
        for copy in copies:
            copy.wait_send()

    return begin, pass_on, finish


def gather_rows(mine, out, near, sems, local_sem, meanwhile=None):
    tok = mine.shape[0]
    low, high = pl.ds(0, tok // 2), pl.ds(tok // 2, tok // 2)
    own = pltpu.make_async_copy(mine, out.at[0], local_sem)
    own.start()
    first = send(mine.at[low], out.at[1, low], sems, 0, near[1])
    second = send(mine.at[high], out.at[2, high], sems, 1, near[2])
    third = send(mine.at[high], out.at[1, high], sems, 2, near[1])
    fourth = send(mine.at[low], out.at[2, low], sems, 3, near[2])
    if meanwhile is not None:
        meanwhile()
    first.wait_recv()
    fifth = send(out.at[1, low], out.at[3, low], sems, 4, near[2])
    second.wait_recv()
    sixth = send(out.at[2, high], out.at[3, high], sems, 5, near[1])
    for copy in (third, fourth, fifth, sixth):
        copy.wait_recv()
    for copy in (first, second, third, fourth, fifth, sixth):
        copy.wait_send()
    own.wait()


def exchange_scratch(tok, model):
    return [
        pltpu.VMEM((6, tok, model // 2), BF),
        pltpu.VMEM((6, tok, model // 2), BF),
        pltpu.VMEM((2, tok, model), F32),
        pltpu.VMEM((tok, model), BF),
        pltpu.SemaphoreType.DMA((6,)),
        pltpu.SemaphoreType.DMA((6,)),
        pltpu.SemaphoreType.DMA((6,)),
        pltpu.SemaphoreType.DMA((6,)),
        pltpu.SemaphoreType.DMA(()),
    ]


def branch_kernel(
    attend_ref, out_proj_ref, hidden_ref, gain_ref, middle_ref, second_ref, parts, landed, kept, mine, s1, r1, s2, r2, own
):
    near = partners()
    greet([near[1], near[2]])

    def product(k, columns):
        return mm(attend_ref[k], out_proj_ref[:, columns])

    for phase in reduce_rows(product, near, parts, kept, landed, (s1, r1)):
        phase()
    middle = hidden_ref[...].astype(F32) + kept[0]
    middle_ref[...] = middle
    mine[...] = rms_forward(middle, gain_ref[...])[0].astype(BF)
    gather_rows(mine, second_ref, near, (s2, r2), own)


def second_back_kernel(
    gate_hbm, up_hbm, ffn_hbm, act_hbm, down_hbm, middle_ref, cot_ref, gain_ref, order_ref, grad_ref, gain_grad_ref, branch_ref, layer_ref, parts, landed, kept, mine, s1, r1, s2, r2, own, both_ref, ffn_ref, act_ref, down_ref, load_sems
):
    del order_ref
    half = ffn_ref.shape[0] // 2
    loads = {}

    def load(name, source, target):
        loads[name] = pltpu.make_async_copy(source, target, load_sems.at[len(loads)])
        loads[name].start()

    units = gate_hbm.shape[2]

    def load_both(k):
        load(("gate", k), gate_hbm.at[k], both_ref.at[k, :, pl.ds(0, units)])
        load(("up", k), up_hbm.at[k], both_ref.at[k, :, pl.ds(units, units)])

    load_both(3)
    for side in (0, 1):
        rows = pl.ds(side * half, half)
        load(("ffn", side), ffn_hbm.at[rows], ffn_ref.at[rows])
    for k in (1, 2, 0):
        load_both(k)
    load("act", act_hbm, act_ref)
    load("down", down_hbm, down_ref)
    waited = set()

    def loaded(*names):
        for name in names:
            if name not in waited:
                waited.add(name)
                loads[name].wait()

    def ready(k, side):
        loaded(("gate", k), ("up", k), ("ffn", side))

    near = partners()
    greet([near[1], near[2]])

    def product(k, columns):
        return mm_nt(both_ref[k], ffn_ref[columns, :])

    begin, pass_on, finish = reduce_rows(product, near, parts, kept, landed, (s1, r1), ready)
    begin()
    pass_on()
    loaded("act", "down")
    for k in range(act_ref.shape[0]):

        def tile(t, carry, k=k):
            columns = pl.ds(pl.multiple_of(t * TILE, TILE), TILE)
            layer_ref[k, :, columns] = mm(act_ref[k], down_ref[:, columns]).astype(BF)
            return carry

        lax.fori_loop(0, down_ref.shape[1] // TILE, tile, 0)
    gain = gain_ref[...]
    _, unit, inv = rms_forward(middle_ref[...], gain)
    finish()
    grad_second = kept[0]
    gain_grad_ref[...] = jnp.sum(grad_second * unit, axis=0, keepdims=True)
    grad_middle = cot_ref[...].astype(F32) + rms_backward(grad_second, unit, inv, gain)
    grad_ref[...] = grad_middle
    mine[...] = grad_middle.astype(BF)
    gather_rows(mine, branch_ref, near, (s2, r2), own)


VMEM_SPEC = pl.BlockSpec(memory_space=pltpu.VMEM)
ANY_SPEC = pl.BlockSpec(memory_space=pl.ANY)


def remote_params(collective_id):
    return pltpu.CompilerParams(
        collective_id=collective_id, has_side_effects=True, vmem_limit_bytes=VMEM_BYTES
    )


def branch_exchange(attend, out_proj, hidden, gain):
    rows, tok, width = attend.shape
    model = hidden.shape[1]
    return pl.pallas_call(
        branch_kernel,
        in_specs=[VMEM_SPEC] * 4,
        out_specs=[VMEM_SPEC, ANY_SPEC],
        out_shape=[
            jax.ShapeDtypeStruct((tok, model), F32),
            jax.ShapeDtypeStruct((rows, tok, model), BF),
        ],
        scratch_shapes=exchange_scratch(tok, model),
        compiler_params=remote_params(1),
        cost_estimate=pl.CostEstimate(
            flops=2 * rows * tok * width * model, bytes_accessed=190_000_000, transcendentals=0
        ),
        name="branch_exchange",
    )(attend, out_proj, hidden, gain)


def second_exchange(gate, up, ffn, act, down, middle, cotangent, gain, order):
    rows, tok, units = gate.shape
    model = ffn.shape[0]
    return pl.pallas_call(
        second_back_kernel,
        in_specs=[ANY_SPEC] * 5 + [VMEM_SPEC] * 3 + [ANY_SPEC],
        out_specs=[VMEM_SPEC, VMEM_SPEC, ANY_SPEC, VMEM_SPEC],
        out_shape=[
            jax.ShapeDtypeStruct((tok, model), F32),
            jax.ShapeDtypeStruct((1, model), F32),
            jax.ShapeDtypeStruct((rows, tok, model), BF),
            jax.ShapeDtypeStruct((rows, tok, model), BF),
        ],
        scratch_shapes=exchange_scratch(tok, model)
        + [pltpu.VMEM(shape, BF) for shape in ((rows, tok, 2 * units), ffn.shape, act.shape, down.shape)]
        + [pltpu.SemaphoreType.DMA((12,))],
        compiler_params=remote_params(2),
        cost_estimate=pl.CostEstimate(
            flops=6 * rows * tok * units * model, bytes_accessed=190_000_000, transcendentals=0
        ),
        name="second_exchange",
    )(gate, up, ffn, act, down, middle, cotangent, gain, order)


def tail_kernel(
    dq_ref, qup_ref, dkv_ref, latent_ref, lgain_ref, cos_ref, sin_ref, first_ref, hidden_ref, again_ref, grads_ref, lgain_part_ref, again_part_ref, ours, theirs, kv_landed, z_landed, parts, landed, kept, pieces, grads, sc, rc, sk, rk, sz, rz, sl, rl, sg, rg, own_sem
):
    rows, chips, tok, wide = ours.shape
    head = wide // 2
    lat = latent_ref.shape[1]
    width = pieces.shape[2]
    row, seq = lax.axis_index("row"), lax.axis_index("seq")
    core, chip = seq % 2, seq // 2
    near = partners()
    later, twin = chip_partners(chips)
    greet([near[1], near[2], near[3]] + later + [twin])

    swap = send(dkv_ref.at[:, :, 1 - core], theirs, (sc, rc), 0, twin)
    load = pltpu.make_async_copy(dkv_ref.at[:, :, core], ours, own_sem)
    load.start()
    left, right = slice(0, head), slice(head, wide)

    def latent_product(k, columns):
        return mm_nt(dq_ref[k], qup_ref[columns, :])

    begin, pass_on, finish = reduce_rows(latent_product, near, parts, kept, landed, (sl, rl))
    load.wait()
    swap.wait_recv()

    blocks = [(chip + i) % chips for i in range(1, chips)] + [chip]
    steps, along = {}, []

    def add(k, block, side, other):
        value = ours[k, block, :, side].astype(F32) + other.astype(F32)
        ours[k, block, :, side] = value.astype(BF)

    def move(n, at, k, side, to):
        source = ours.at[k, blocks[n], :, side]
        steps[n, at] = send(source, kv_landed.at[at, n], (sk, rk), 6 * n + at, near[to])

    def first(n):
        for at, (k, side, to) in enumerate(
            [(3, left, 1), (3, right, 2), (1, left, 1), (2, right, 2)]
        ):
            add(k, blocks[n], side, theirs[k, blocks[n], :, side])
            move(n, at, k, side, to)
        for k, side in ((2, left), (1, right), (0, left), (0, right)):
            add(k, blocks[n], side, theirs[k, blocks[n], :, side])

    def second(n):
        steps[n, 0].wait_recv()
        add(2, blocks[n], left, kv_landed[0, n])
        move(n, 4, 2, left, 2)
        steps[n, 1].wait_recv()
        add(1, blocks[n], right, kv_landed[1, n])
        move(n, 5, 1, right, 1)

    def third(n):
        for at, side in ((2, left), (3, right), (4, left), (5, right)):
            steps[n, at].wait_recv()
            add(0, blocks[n], side, kv_landed[at, n])
        if n < chips - 1:
            along.append(send(ours.at[0, blocks[n]], z_landed.at[n], (sz, rz), n, later[n]))

    for n in range(chips + 1):
        if n < chips:
            first(n)
        if n >= 1:
            second(n - 1)
        if n >= 2:
            third(n - 2)
    begin()
    third(chips - 1)
    pass_on()
    lgain = lgain_ref[...]
    _, unit, inv = rms_forward(latent_ref[...], lgain)
    scales = []
    for k in range(rows):
        values = hidden_ref[k].astype(F32)
        scales.append(lax.rsqrt(jnp.mean(values * values, axis=-1, keepdims=True) + epsilon))
    finish()
    grad_latent_norm = kept[0]
    lgain_part_ref[...] = jnp.sum(grad_latent_norm * unit, axis=0, keepdims=True)
    grad_latent = rms_backward(grad_latent_norm, unit, inv, lgain)
    total = ours[0, chip].astype(F32)
    for i in range(1, chips):
        along[i - 1].wait_recv()
        total = total + z_landed[i - 1].astype(F32)
    grad_key = rotate_back(total[:, :head], cos_ref[...], sin_ref[...])
    joined = jnp.concatenate([grad_latent, grad_key, total[:, head:]], axis=1).astype(BF)
    for j in range(rows):
        pieces[j] = joined[:, j * width : (j + 1) * width]
    last = [
        send(pieces.at[near[k][0]], grads.at[k], (sg, rg), k - 1, near[k]) for k in range(1, rows)
    ]
    grads[0] = pieces[row]
    tiles = again_ref.shape[1] // TILE
    again_part_ref[...] = jnp.zeros_like(again_part_ref)
    for k in range(rows):
        if k:
            last[k - 1].wait_recv()
        grads_ref[k] = grads[k]

        def tile(t, carry, k=k, scale=scales[k]):
            columns = pl.ds(pl.multiple_of(t * TILE, TILE), TILE)
            part = mm_nt(grads[k], first_ref[columns, :width])
            part = part * (hidden_ref[k, :, columns].astype(F32) * scale)
            again_part_ref[:, columns] = again_part_ref[:, columns] + jnp.sum(
                part, axis=0, keepdims=True
            )
            return carry

        lax.fori_loop(0, tiles, tile, 0)
    for copy in [swap] + list(steps.values()) + along + last:
        copy.wait_send()


def tail_exchange(
    dq, qup, dkv, latent, lgain, cosine, sine, first_set, hidden_all, again, width
):
    rows, chips, _, tok, wide = dkv.shape
    lat = latent.shape[1]
    model = again.shape[1]
    dma = pltpu.SemaphoreType.DMA
    return pl.pallas_call(
        tail_kernel,
        in_specs=[VMEM_SPEC] * 2 + [ANY_SPEC] + [VMEM_SPEC] * 7,
        out_specs=[VMEM_SPEC] * 3,
        out_shape=[
            jax.ShapeDtypeStruct((rows, tok, width), BF),
            jax.ShapeDtypeStruct((1, lat), F32),
            jax.ShapeDtypeStruct((1, model), F32),
        ],
        scratch_shapes=[
            pltpu.VMEM((rows, chips, tok, wide), BF),
            pltpu.VMEM((rows, chips, tok, wide), BF),
            pltpu.VMEM((6, chips, tok, wide // 2), BF),
            pltpu.VMEM((chips - 1, tok, wide), BF),
            pltpu.VMEM((6, tok, lat // 2), BF),
            pltpu.VMEM((6, tok, lat // 2), BF),
            pltpu.VMEM((2, tok, lat), F32),
            pltpu.VMEM((rows, tok, width), BF),
            pltpu.VMEM((rows, tok, width), BF),
        ]
        + [dma((n,)) for n in (1, 6 * chips, chips - 1, 6, 3) for _ in range(2)]
        + [dma(())],
        compiler_params=remote_params(4),
        cost_estimate=pl.CostEstimate(
            flops=2 * rows * tok * lat * qup.shape[1] + 2 * rows * tok * width * model,
            bytes_accessed=230_000_000,
            transcendentals=0,
        ),
        name="tail_exchange",
    )(dq, qup, dkv, latent, lgain, cosine, sine, first_set, hidden_all, again)


def hidden_back_kernel(
    grads_ref, first_ref, hidden_ref, again_ref, middle_ref, term_ref, again_part_ref, fgain_part_ref, lgain_part_ref, out_ref, grad_ref, gain_ref, parts, landed, kept, ours, theirs, z_landed, total, back, gains, gains_theirs, s1, r1, sc, rc, sz, rz, sb, rb, sg, rg, own
):
    rows, chips = ours.shape[:2]
    width = grads_ref.shape[2]
    row, seq = lax.axis_index("row"), lax.axis_index("seq")
    core, chip = seq % 2, seq // 2
    near = partners()
    later, twin = chip_partners(chips)
    greet([near[1], near[2], near[3]] + later + [twin])
    swap = send(term_ref.at[:, :, 1 - core], theirs, (sc, rc), 0, twin)
    load = pltpu.make_async_copy(
        term_ref.at[:, :, core], ours.at[:, :, :, pl.ds(0, width)], own
    )
    load.start()
    at = lax.broadcasted_iota(jnp.int32, (16, 128), 0)
    unit_columns = jnp.where(at == lax.broadcasted_iota(jnp.int32, (16, 128), 1), 1.0, 0.0)
    at = lax.broadcasted_iota(jnp.int32, (16, again_part_ref.shape[1]), 0)
    vectors = jnp.where(at == 0, again_part_ref[...], 0.0)
    vectors = jnp.where(at == 1, fgain_part_ref[...], vectors)
    vectors = jnp.where(at == 2, lgain_part_ref[...], vectors)
    gains[...] = mm_tn(vectors.astype(BF), unit_columns.astype(BF)).astype(BF).reshape(gains.shape)
    swap_gains = send(gains.at[:, :, 1 - core], gains_theirs, (sg, rg), 0, twin)

    def product(k, columns):
        return mm_nt(grads_ref[k], first_ref[columns, :width])

    begin, pass_on, finish = reduce_rows(product, near, parts, kept, landed, (s1, r1))
    begin()
    load.wait()
    swap.wait_recv()
    swap_gains.wait_recv()
    ours[:, :, :, :width] = (ours[:, :, :, :width].astype(F32) + theirs[...].astype(F32)).astype(BF)
    ours[:, :, :, width:] = (
        gains[:, :, core].astype(F32) + gains_theirs[...].astype(F32)
    ).astype(BF)
    along = [
        send(ours.at[:, (chip + i) % chips], z_landed.at[i - 1], (sz, rz), i - 1, later[i - 1])
        for i in range(1, chips)
    ]
    pass_on()
    again = again_ref[...]
    _, unit, inv = rms_forward(hidden_ref[...].astype(F32), again)
    finish()
    out_ref[...] = middle_ref[...] + rms_backward(kept[0], unit, inv, again)
    sums = ours[:, chip].astype(F32)
    for i in range(1, chips):
        along[i - 1].wait_recv()
        sums = sums + z_landed[i - 1].astype(F32)
    total[...] = sums.astype(BF)
    last = [
        send(total.at[near[k][0]], back.at[row], (sb, rb), k - 1, near[k]) for k in range(1, rows)
    ]
    back[row] = total[row]
    for copy in last:
        copy.wait_recv()
    gain_ref[...] = jnp.zeros_like(gain_ref)
    for j in range(rows):
        grad_ref[:, j * width : (j + 1) * width] = back[j, :, :width].astype(F32)
        gain_ref[...] = gain_ref[...] + back[j, :, width:].astype(F32)
    for copy in [swap, swap_gains] + along + last:
        copy.wait_send()


def hidden_exchange(grads, first_set, hidden, again, grad_middle, term, gain_parts):
    rows, tok, width = grads.shape
    model = again.shape[1]
    _, chips, _, own, _ = term.shape
    wide = width + 128
    dma = pltpu.SemaphoreType.DMA
    return pl.pallas_call(
        hidden_back_kernel,
        in_specs=[VMEM_SPEC] * 5 + [ANY_SPEC] + [VMEM_SPEC] * 3,
        out_specs=[VMEM_SPEC] * 3,
        out_shape=[
            jax.ShapeDtypeStruct((tok, model), F32),
            jax.ShapeDtypeStruct((own, rows * width), F32),
            jax.ShapeDtypeStruct((own, wide - width), F32),
        ],
        scratch_shapes=exchange_scratch(tok, model)[:3]
        + [
            pltpu.VMEM((rows, chips, own, wide), BF),
            pltpu.VMEM((rows, chips, own, width), BF),
            pltpu.VMEM((chips - 1, rows, own, wide), BF),
            pltpu.VMEM((rows, own, wide), BF),
            pltpu.VMEM((rows, own, wide), BF),
            pltpu.VMEM((rows, chips, 2, own, 128), BF),
            pltpu.VMEM((rows, chips, own, 128), BF),
        ]
        + [dma((n,)) for n in (6, 1, chips - 1, 3, 1) for _ in range(2)]
        + [dma(())],
        compiler_params=remote_params(5),
        cost_estimate=pl.CostEstimate(
            flops=2 * rows * tok * width * model, bytes_accessed=110_000_000, transcendentals=0
        ),
        name="hidden_exchange",
    )(grads, first_set, hidden, again, grad_middle, term, *gain_parts)


def last_kernel(oq_ref, back, s1, r1, own):
    rows, _, wide = back.shape
    row = lax.axis_index("row")
    columns = pl.ds(oq_ref.shape[2] - wide, wide)
    near = partners()
    greet([near[1], near[2], near[3]])
    copies = [
        send(oq_ref.at[near[k][0], :, columns], back.at[row], (s1, r1), k - 1, near[k])
        for k in range(1, rows)
    ]
    copies.append(pltpu.make_async_copy(oq_ref.at[row, :, columns], back.at[row], own))
    copies[-1].start()
    for copy in copies:
        copy.wait()


def last_exchange(oq, model):
    rows, own, total = oq.shape
    dma = pltpu.SemaphoreType.DMA
    return pl.pallas_call(
        last_kernel,
        in_specs=[VMEM_SPEC],
        out_specs=VMEM_SPEC,
        out_shape=jax.ShapeDtypeStruct((rows, own, total - model), BF),
        scratch_shapes=[dma((3,)), dma((3,)), dma(())],
        compiler_params=remote_params(8),
        cost_estimate=pl.CostEstimate(flops=0, bytes_accessed=10_000_000, transcendentals=0),
        name="last_exchange",
    )(oq)


def start_kernel(
    hidden_ref, gate_ref, up_ref, cut_ref, all_ref, ffn_ref, first_ref, s1, r1, sg, rg, sz, rz, sc, rc, own, own_ffn, own_cut
):
    row = lax.axis_index("row")
    rows = all_ref.shape[0]
    units = ffn_ref.shape[2] // 2
    chips = first_ref.shape[1]
    seq = lax.axis_index("seq")
    core, chip = seq % 2, seq // 2
    near = partners()
    later, twin = chip_partners(chips)
    greet([near[1], near[2], near[3]] + later + [twin])
    place = first_ref.at[:, chip, core]
    keep = pltpu.make_async_copy(cut_ref, place, own_cut)
    keep.start()
    along = [send(cut_ref, place, (sz, rz), i - 1, later[i - 1]) for i in range(1, chips)]
    shared = [send(cut_ref, place, (sc, rc), 0, twin)]
    cut = []

    def slices():
        for at, source_ref in ((0, gate_ref), (1, up_ref)):
            for k in range(rows):
                to = row if k == 0 else near[k][0]
                source = source_ref.at[:, pl.ds(pl.multiple_of(to * units, 128), units)]
                target = ffn_ref.at[row, :, pl.ds(at * units, units)]
                if k == 0:
                    copy = pltpu.make_async_copy(source, target, own_ffn.at[at])
                    copy.start()
                else:
                    copy = send(source, target, (sg, rg), 3 * at + k - 1, near[k])
                cut.append(copy)

    gather_rows(hidden_ref, all_ref, near, (s1, r1), own, slices)
    for i in range(1, chips):
        along[i - 1].wait_recv()
        block = first_ref.at[:, (chip + chips - i) % chips, core]
        shared.append(send(block, block, (sc, rc), i, twin))
    keep.wait()
    for copy in cut:
        copy.wait()
    for copy in shared:
        copy.wait_recv()
    for copy in along + shared:
        copy.wait_send()


def start_exchange(hidden, gate, up, first_cut, chips):
    rows, own, wide = first_cut.shape
    dma = pltpu.SemaphoreType.DMA
    return pl.pallas_call(
        start_kernel,
        in_specs=[ANY_SPEC] * 4,
        out_specs=[ANY_SPEC] * 3,
        out_shape=[
            jax.ShapeDtypeStruct((rows,) + hidden.shape, BF),
            jax.ShapeDtypeStruct((rows, gate.shape[0], 2 * gate.shape[1] // rows), BF),
            jax.ShapeDtypeStruct((rows, chips, 2, own, wide), BF),
        ],
        scratch_shapes=[dma((n,)) for n in (6, 6, chips - 1, chips) for _ in range(2)]
        + [dma(()), dma((2,)), dma(())],
        compiler_params=remote_params(6),
        cost_estimate=pl.CostEstimate(flops=0, bytes_accessed=120_000_000, transcendentals=0),
        name="start_exchange",
    )(hidden, gate, up, first_cut)


def front_kernel(
    hidden_ref, first_ref, again_ref, lgain_ref, cos_ref, sin_ref, latent_ref, lat_all_ref, kv_ref, first_low, pieces, landed, lat_mine, kv_mine, sa, ra, sl, rl, sz, rz, sr, rr, sf, rf, sc, rc, own_sem
):
    rows, tok, model = hidden_ref.shape
    chips = kv_ref.shape[1]
    width = pieces.shape[2]
    lat = latent_ref.shape[1]
    head = kv_ref.shape[4] // 2
    row, seq = lax.axis_index("row"), lax.axis_index("seq")
    core, chip = seq % 2, seq // 2
    near = partners()
    later, twin = chip_partners(chips)
    greet([near[1], near[2], near[3]] + later + [twin])

    again = again_ref[...]
    copies = []
    for k in (3, 2, 1, 0):
        first_low[...] = rms_forward(hidden_ref[k].astype(F32), again)[0].astype(BF)
        piece = mm(first_low[...], first_ref[:, :width]).astype(BF)
        if k:
            pieces[k] = piece
            copies.append(send(pieces.at[k], landed.at[row], (sa, ra), k - 1, near[k]))
        else:
            landed[row] = piece
    for copy in copies:
        copy.wait_recv()
    joined = jnp.concatenate([landed[j] for j in range(rows)], axis=1)
    key = rotate(joined[:, lat : lat + head].astype(F32), cos_ref[...], sin_ref[...])
    kv_mine[:, :head] = key.astype(BF)
    kv_mine[:, head:] = joined[:, lat + head :]

    own = pltpu.make_async_copy(kv_mine, kv_ref.at[0, chip, core], own_sem.at[0])
    own.start()
    along = [
        send(kv_mine, kv_ref.at[0, chip, core], (sz, rz), i - 1, later[i - 1])
        for i in range(1, chips)
    ]
    low, high = pl.ds(0, tok // 2), pl.ds(tok // 2, tok // 2)
    across, passed = [], []

    def block(i):
        return (chip + chips - i) % chips

    def spread(i):
        source = kv_mine if i == 0 else kv_ref.at[0, block(i), core]
        for k in (1, 2):
            across.append(
                send(source, kv_ref.at[k, block(i), core], (sr, rr), 2 * i + k - 1, near[k])
            )

    def pass_on(i):
        across[2 * i].wait_recv()
        source = kv_ref.at[1, block(i), core, low]
        passed.append(send(source, kv_ref.at[3, block(i), core, low], (sf, rf), 2 * i, near[2]))
        across[2 * i + 1].wait_recv()
        source = kv_ref.at[2, block(i), core, high]
        passed.append(
            send(source, kv_ref.at[3, block(i), core, high], (sf, rf), 2 * i + 1, near[1])
        )

    spread(0)
    latent = joined[:, :lat].astype(F32)
    latent_ref[...] = latent
    lat_mine[...] = rms_forward(latent, lgain_ref[...])[0].astype(BF)
    lat_own = pltpu.make_async_copy(lat_mine, lat_all_ref.at[0], own_sem.at[1])
    lat_own.start()
    lat_copies = [
        send(lat_mine, lat_all_ref.at[k], (sl, rl), k - 1, near[k]) for k in range(1, rows)
    ]
    for i in range(1, chips):
        along[i - 1].wait_recv()
        spread(i)
        pass_on(i - 1)
    own.wait()
    shared = [send(kv_ref.at[0, :, core], kv_ref.at[0, :, core], (sc, rc), 0, twin)]
    pass_on(chips - 1)
    for k in (1, 2):
        shared.append(send(kv_ref.at[k, :, core], kv_ref.at[k, :, core], (sc, rc), k, twin))
    for copy in passed:
        copy.wait_recv()
    shared.append(send(kv_ref.at[3, :, core], kv_ref.at[3, :, core], (sc, rc), 3, twin))
    for copy in lat_copies + shared:
        copy.wait_recv()
    for copy in copies + along + across + passed + lat_copies + shared:
        copy.wait_send()
    lat_own.wait()


def front_exchange(hidden_all, first_set, again, lgain, cosine, sine, chips, width, head):
    rows, tok, model = hidden_all.shape
    lat = lgain.shape[1]
    dma = pltpu.SemaphoreType.DMA
    pairs = [3, 3, chips - 1, 2 * chips, 2 * chips, 4]
    return pl.pallas_call(
        front_kernel,
        in_specs=[VMEM_SPEC] * 6,
        out_specs=[VMEM_SPEC, ANY_SPEC, ANY_SPEC],
        out_shape=[
            jax.ShapeDtypeStruct((tok, lat), F32),
            jax.ShapeDtypeStruct((rows, tok, lat), BF),
            jax.ShapeDtypeStruct((rows, chips, 2, tok, 2 * head), BF),
        ],
        scratch_shapes=[
            pltpu.VMEM((tok, model), BF),
            pltpu.VMEM((rows, tok, width), BF),
            pltpu.VMEM((rows, tok, width), BF),
            pltpu.VMEM((tok, lat), BF),
            pltpu.VMEM((tok, 2 * head), BF),
        ]
        + [dma((n,)) for n in pairs for _ in range(2)]
        + [dma((2,))],
        compiler_params=remote_params(3),
        cost_estimate=pl.CostEstimate(
            flops=2 * rows * tok * model * width, bytes_accessed=230_000_000, transcendentals=0
        ),
        name="front_exchange",
    )(hidden_all, first_set, again, lgain, cosine, sine)


def deal_kernel(first_ref, qup_ref, lens_ref, cut_ref, qup_cut_ref, lens_all, sf, rf, sq, rq, sl, rl, own):
    row = lax.axis_index("row")
    rows, _, wide = cut_ref.shape
    units = qup_cut_ref.shape[2]
    near = partners()
    greet([near[1], near[2], near[3]])
    copies = []
    for k in (3, 1, 2, 0):
        to = row if k == 0 else near[k][0]
        moves = [
            (first_ref.at[to], cut_ref.at[row], (sf, rf)),
            (
                qup_ref.at[:, pl.ds(pl.multiple_of(to * units, 128), units)],
                qup_cut_ref.at[row],
                (sq, rq),
            ),
            (lens_ref, lens_all.at[k], (sl, rl)),
        ]
        for at, (source, target, sems) in enumerate(moves):
            if k:
                copies.append(send(source, target, sems, k - 1, near[k]))
            else:
                copies.append(pltpu.make_async_copy(source, target, own.at[at]))
                copies[-1].start()
    for copy in copies:
        copy.wait()


def deal_exchange(first, qup, lens):
    rows = first.shape[0]
    dma = pltpu.SemaphoreType.DMA
    return pl.pallas_call(
        deal_kernel,
        in_specs=[VMEM_SPEC] * 3,
        out_specs=[VMEM_SPEC] * 3,
        out_shape=[
            jax.ShapeDtypeStruct(first.shape, BF),
            jax.ShapeDtypeStruct((rows, qup.shape[0], qup.shape[1] // rows), BF),
            jax.ShapeDtypeStruct((rows,) + lens.shape, lens.dtype),
        ],
        scratch_shapes=[dma((3,))] * 6 + [dma((3,))],
        compiler_params=remote_params(7),
        cost_estimate=pl.CostEstimate(flops=0, bytes_accessed=10_000_000, transcendentals=0),
        name="deal_exchange",
    )(first, qup, lens)


def ffn_grad_kernel(second_ref, gate_hbm, up_hbm, out_ref, both, mine, theirs, ss, rs, load_sems, out_sems):
    rows = mine.shape[0]
    units = gate_hbm.shape[1]
    block = second_ref.shape[1] // rows
    row = lax.axis_index("row")
    core = lax.axis_index("seq") % 2
    _, twin = chip_partners(mine.shape[1])
    loads = [
        pltpu.make_async_copy(gate_hbm, both.at[:, pl.ds(0, units)], load_sems.at[0]),
        pltpu.make_async_copy(up_hbm, both.at[:, pl.ds(units, units)], load_sems.at[1]),
    ]
    for copy in loads:
        copy.start()
    greet([twin])
    for copy in loads:
        copy.wait()

    def swap(r):
        return pltpu.make_async_remote_copy(
            src_ref=mine.at[r, :, 1 - core],
            dst_ref=theirs.at[r],
            send_sem=ss.at[r],
            recv_sem=rs.at[r],
            device_id=twin,
            device_id_type=MESH,
        )

    def compute(r, carry):
        owner = 2 * ((row // 2 + r // 2) % 2) + (row + r) % 2
        left = second_ref[:, pl.ds(pl.multiple_of(owner * block, block), block)]
        mine[r] = mm_tn(left, both[...]).astype(BF).reshape(mine.shape[1:])
        swap(r).start()
        return carry

    lax.fori_loop(0, rows, compute, 0)
    outs = []
    for r in range(rows):
        swap(r).wait_recv()
        theirs[r] = (mine[r, :, core].astype(F32) + theirs[r].astype(F32)).astype(BF)
        outs.append(pltpu.make_async_copy(theirs.at[r], out_ref.at[r], out_sems.at[r]))
        outs[-1].start()
    for r in range(rows):
        swap(r).wait_send()
        outs[r].wait()


def ffn_grad(second, gate, up, rows, chips):
    tokens, model = second.shape
    units = gate.shape[1]
    own = model // rows // chips // 2
    dma = pltpu.SemaphoreType.DMA
    return pl.pallas_call(
        ffn_grad_kernel,
        in_specs=[VMEM_SPEC] + [ANY_SPEC] * 2,
        out_specs=ANY_SPEC,
        out_shape=jax.ShapeDtypeStruct((rows, chips, own, 2 * units), BF),
        scratch_shapes=[
            pltpu.VMEM((tokens, 2 * units), BF),
            pltpu.VMEM((rows, chips, 2, own, 2 * units), BF),
            pltpu.VMEM((rows, chips, own, 2 * units), BF),
        ]
        + [dma((rows,)), dma((rows,)), dma((2,)), dma((rows,))],
        compiler_params=remote_params(9),
        cost_estimate=pl.CostEstimate(
            flops=4 * tokens * units * model, bytes_accessed=40_000_000, transcendentals=0
        ),
        name="ffn_grad",
    )(second, gate, up)


def move_row(value, k, rows):
    return lax.ppermute(value, "row", [(i, i ^ k) for i in range(rows)])


def in_row_order(pieces):
    rows, me = lax.axis_size("row"), lax.axis_index("row")
    return jnp.stack(
        [lax.select_n(me, *[pieces[j ^ i] for i in range(rows)]) for j in range(rows)]
    )


def join_columns(blocks):
    rows, n, width = blocks.shape
    return blocks.transpose(1, 0, 2).reshape(n, rows * width)


def scatter_seq(v, axis=0):
    return lax.psum_scatter(v.astype(BF), "seq", scatter_dimension=axis, tiled=True)


def on_device(
    hidden,
    cotangent,
    lengths,
    attn_gain,
    query_down,
    latent_gain,
    query_up,
    key_proj,
    value_proj,
    out_proj,
    ffn_gain,
    gate_proj,
    up_proj,
    down_proj,
):
    tok = hidden.shape[1]
    model = hidden.shape[2]
    rows = lax.axis_size("row")
    spread = lax.axis_size("seq")
    row_index = lax.axis_index("row")
    seq_index = lax.axis_index("seq")
    first_slot = seq_index * tok
    head = key_proj.shape[1]
    lat = query_down.shape[1]
    heads = query_up.shape[1] // head // rows
    units = down_proj.shape[0] * spread
    scale = head ** (-0.5)
    own = query_down.shape[0]
    lat_own = latent_gain.shape[0]

    first_own = jnp.concatenate([query_down, key_proj, value_proj], axis=1)
    first_width = first_own.shape[1] // rows
    gain_own = jnp.stack([attn_gain, ffn_gain, jnp.pad(latent_gain, (0, own - lat_own))], axis=1)
    gain_own = jnp.pad(gain_own, ((0, 0), (0, 125)))
    first_own = jnp.stack(
        [
            jnp.concatenate([first_own[:, j * first_width : (j + 1) * first_width], gain_own], axis=1)
            for j in range(rows)
        ]
    )
    docs = lengths.shape[1]
    first_cut, qup_cut, lens = deal_exchange(
        first_own, query_up, jnp.pad(lengths, ((0, 0), (0, 128 - docs)))
    )
    lens = lens[:, 0, :docs]
    oq_own = jnp.concatenate([out_proj, qup_cut.reshape(out_proj.shape[0], -1)], axis=1)
    full_oq = lax.all_gather(oq_own, "seq", axis=0, tiled=True)
    hidden_all, ffn_cut, first_set = start_exchange(
        hidden[0], gate_proj, up_proj, first_cut, spread // 2
    )
    first_set = first_set.reshape(model, -1)
    full_ffn = lax.all_gather(ffn_cut, "seq", axis=1, tiled=True).reshape(model, -1)
    full_down = lax.all_gather(down_proj, "seq", axis=0, tiled=True)
    full_gains = first_set[:, first_width:].astype(F32)
    full_again = full_gains[:, 0]
    full_fgain = full_gains[:, 1]
    full_lgain = full_gains[:, 2].reshape(rows * spread, own)[:, :lat_own].reshape(lat)
    full_qup = full_oq[:, model:].reshape(spread, rows, lat_own, -1).transpose(1, 0, 2, 3)
    full_qup = full_qup.reshape(lat, heads * head)
    position = document_positions(lens, first_slot + jnp.arange(tok, dtype=jnp.int32))
    cosine, sine = rope_tables(position, head)

    residual_all = hidden_all.astype(F32)
    first_low = rms_forward(residual_all, full_again)[0].astype(BF).reshape(rows * tok, model)
    latent, latent_all, key_value = front_exchange(
        hidden_all,
        first_set,
        full_again[None],
        full_lgain[None],
        cosine[0],
        sine[0],
        spread // 2,
        first_width,
        head,
    )
    key_value = key_value.reshape(rows, spread * tok, 2 * head)
    grad_own, latent_all = lax.optimization_barrier((cotangent[0], latent_all))
    grad_pieces = [move_row(grad_own, k, rows) for k in range(1, rows)]
    query_low, attend, attend_low, stats = attend_forward(
        heads, scale, lens, latent_all, full_qup, cosine, sine, key_value
    )
    middle, second_all = branch_exchange(attend_low, full_oq, hidden[0], full_fgain[None])
    grad_pieces, second_all = lax.optimization_barrier((grad_pieces, second_all))
    grad_all = jnp.stack([cotangent[0]] + grad_pieces).reshape(rows * tok, model)
    second_all = second_all.reshape(rows * tok, model)
    both = mm(second_all, full_ffn)
    gate_pre, upward = both[:, :units], both[:, units:]
    gate_sig = jax.nn.sigmoid(gate_pre)
    gate_act = gate_pre * gate_sig
    act_low = (gate_act * upward).astype(BF)
    down_part = mm_tn(act_low, grad_all).astype(BF)
    down_grad = scatter_seq(down_part)
    full_down, down_order = lax.optimization_barrier((full_down, down_part))
    grad_act = mm_nt(grad_all, full_down)
    slope = gate_sig * (1.0 + gate_pre * (1.0 - gate_sig))
    grad_gate = (grad_act * upward * slope).astype(BF)
    grad_upward = (grad_act * gate_act).astype(BF)
    ffn_term = ffn_grad(second_all, grad_gate, grad_upward, rows, spread // 2)
    ffn_part = lax.psum_scatter(
        ffn_term.reshape(rows, model // rows // 2, -1),
        "seq",
        scatter_dimension=1,
        axis_index_groups=[list(range(core, spread, 2)) for core in range(2)],
        tiled=True,
    )
    grad_gate, ffn_term = lax.optimization_barrier((grad_gate, ffn_term))
    grad_middle, ffn_gain_part, branch_all, layer_part = second_exchange(
        grad_gate.reshape(rows, tok, units),
        grad_upward.reshape(rows, tok, units),
        full_ffn,
        act_low.reshape(rows, tok, units),
        full_down,
        middle,
        cotangent[0],
        full_fgain[None],
        down_order,
    )
    layer_pieces = [move_row(layer_part[k], k, rows) for k in range(1, rows)]
    grad_query, kv_part, oq_part = attend_backward(
        heads,
        scale,
        lens,
        query_low,
        key_value,
        branch_all,
        full_oq,
        attend_low,
        latent_all,
        attend,
        stats,
        cosine,
        sine,
    )
    grad_query, oq_part, down_grad, layer_pieces = lax.optimization_barrier(
        (grad_query, oq_part, down_grad, layer_pieces)
    )
    oq_part = scatter_seq(oq_part)
    layer_sum = middle + layer_part[0].astype(F32)
    for piece in layer_pieces:
        layer_sum = layer_sum + piece.astype(F32)
    layer_out = layer_sum.astype(BF)
    grad_first_all, latent_gain_part, attn_gain_part = tail_exchange(
        grad_query,
        full_qup,
        kv_part.reshape(rows, spread // 2, 2, tok, 2 * head),
        latent,
        full_lgain[None],
        cosine[0],
        sine[0],
        first_set,
        hidden_all,
        full_again[None],
        first_width,
    )
    lgain_part = jnp.pad(
        latent_gain_part.reshape(rows * spread, lat_own), ((0, 0), (0, own - lat_own))
    ).reshape(1, model)
    first_term = mm_tn(first_low, grad_first_all.reshape(rows * tok, first_width)).astype(BF)
    grad_first_all, ffn_part = lax.optimization_barrier((grad_first_all, ffn_part))
    ffn_pieces = [ffn_part[0]] + [move_row(ffn_part[k], k, rows) for k in range(1, rows)]
    hidden_grad, first_grad, gain_grad = hidden_exchange(
        grad_first_all,
        first_set,
        hidden[0],
        full_again[None],
        grad_middle,
        first_term.reshape(rows, spread // 2, 2, own, -1),
        (attn_gain_part, ffn_gain_part, lgain_part),
    )
    hidden_grad, oq_part, ffn_pieces = lax.optimization_barrier((hidden_grad, oq_part, ffn_pieces))
    ffn_back = in_row_order(ffn_pieces)
    query_up_grad = last_exchange(oq_part.reshape(rows, lat_own, -1), model)
    query_up_grad = join_columns(query_up_grad).astype(F32)
    out_grad = oq_part[:, :model].astype(F32)
    gate_grad = join_columns(ffn_back[:, :, :units]).astype(F32)
    up_grad = join_columns(ffn_back[:, :, units:]).astype(F32)
    return (
        layer_out[None],
        hidden_grad[None],
        gain_grad[:, 0],
        first_grad[:, :lat],
        gain_grad[:lat_own, 2],
        query_up_grad,
        first_grad[:, lat : lat + head],
        first_grad[:, lat + head :],
        out_grad,
        gain_grad[:, 1],
        gate_grad,
        up_grad,
        down_grad.astype(F32),
    )


def solution(mesh):
    token = P("row", "seq", None)
    vector = P(("row", "seq"))
    matrix = P(("row", "seq"), None)
    return jax.shard_map(
        on_device,
        mesh=mesh,
        in_specs=(token, token, P("row", None), vector, matrix, vector)
        + (matrix,) * 4
        + (vector,)
        + (matrix,) * 3,
        out_specs=(token, token, vector, matrix, vector)
        + (matrix,) * 4
        + (vector,)
        + (matrix,) * 3,
        check_vma=False,
    )
```

```python
import functools
import math

import jax
import jax.numpy as jnp
from jax import lax
from jax.experimental import pallas as pl
from jax.experimental.pallas import tpu as pltpu
from jax.sharding import PartitionSpec as P

epsilon = 1e-06
masked_value = -1e30
BF = jnp.bfloat16
F32 = jnp.float32
VMEM_BYTES = 60 * 1024 * 1024


def rms_forward(values, gain):
    inv_rms = lax.rsqrt(jnp.mean(values * values, axis=-1, keepdims=True) + epsilon)
    normed = values * inv_rms
    return (normed * gain, normed, inv_rms)


def rms_backward(incoming, normed, inv_rms, gain):
    grad_normed = incoming * gain
    inner = jnp.mean(grad_normed * normed, axis=-1, keepdims=True)
    return inv_rms * (grad_normed - normed * inner)


def document_positions(lengths, slots):
    ends = jnp.cumsum(lengths, axis=1)
    is_past = slots[None, :, None] >= ends[:, None, :]
    begin = jnp.sum(jnp.where(is_past, lengths[:, None, :], 0), axis=2)
    return slots[None, :] - begin


def rope_tables(position, head_size):
    half_dim = head_size // 2
    frequency = jnp.exp(jnp.arange(half_dim, dtype=F32) * (-2.0 * math.log(10000.0) / head_size))
    angles = position.astype(F32)[..., None] * frequency
    return (jnp.cos(angles), jnp.sin(angles))


def rotate(values, cosine, sine_table):
    half = values.shape[-1] // 2
    front, behind = values[..., :half], values[..., half:]
    return jnp.concatenate(
        [front * cosine - behind * sine_table, behind * cosine + front * sine_table], axis=-1
    )


def rotate_back(grads, cosine, sine_table):
    half = grads.shape[-1] // 2
    front, behind = grads[..., :half], grads[..., half:]
    return jnp.concatenate(
        [front * cosine + behind * sine_table, behind * cosine - front * sine_table], axis=-1
    )


def dot(a, b, dims):
    return lax.dot_general(a, b, (dims, ((), ())), preferred_element_type=F32)


def mm(a, b):
    return dot(a, b, ((1,), (0,)))


def mm_nt(a, b):
    return dot(a, b, ((1,), (1,)))


def mm_tn(a, b):
    return dot(a, b, ((0,), (0,)))


KEYS = 256


def visible(lens_ref, row, first_slot, tok):
    slot = first_slot + lax.broadcasted_iota(jnp.int32, (tok, 1), 0)
    low = jnp.zeros((tok, 1), jnp.int32)
    first_low = jnp.int32(0)
    end = jnp.int32(0)
    docs = lens_ref.shape[1]
    for doc in range(docs):
        end = end + lens_ref[row, doc]
        if doc < docs - 1:
            low = jnp.where(slot >= end, end, low)
            first_low = jnp.where(first_slot >= end, end, first_low)
        else:
            low = jnp.where(slot >= end, slot, low)
            first_low = jnp.where(first_slot >= end, first_slot, first_low)
    first_step = first_low // KEYS
    last_step = (first_slot + tok + KEYS - 1) // KEYS
    return (slot, low, first_step, last_step)


def stack_heads(ref_or_value, heads, head):
    return jnp.concatenate(
        [ref_or_value[:, h * head : (h + 1) * head] for h in range(heads)], axis=0
    )


def attend_kernel(
    heads, scale, lens_ref, lat_ref, qup_ref, cos_ref, sin_ref, kv_ref, q_ref, out_ref, low_ref, stats_ref, score_ref
):
    row = pl.program_id(0)
    tok = lat_ref.shape[1]
    head = kv_ref.shape[2] // 2
    first_slot = lax.axis_index("seq") * tok
    slot, low, first_step, last_step = visible(lens_ref, row, first_slot, tok)
    slot = jnp.concatenate([slot] * heads, axis=0)
    low = jnp.concatenate([low] * heads, axis=0)
    queries = mm(lat_ref[0], qup_ref[...])
    cosine, sine = cos_ref[0], sin_ref[0]
    for h in range(heads):
        q_ref[0, :, h * head : (h + 1) * head] = rotate(
            queries[:, h * head : (h + 1) * head], cosine, sine
        ).astype(BF)
    query = stack_heads(q_ref[0], heads, head)

    def keys_of(step):
        return pl.ds(pl.multiple_of(step * KEYS, KEYS), KEYS)

    def score_step(step, row_max):
        score = mm_nt(query, kv_ref[0, keys_of(step), :head]) * scale
        key_slot = step * KEYS + lax.broadcasted_iota(jnp.int32, (1, KEYS), 1)
        score = jnp.where((key_slot >= low) & (key_slot <= slot), score, masked_value)
        score_ref[step] = score
        return jnp.maximum(row_max, jnp.max(score, axis=1, keepdims=True))

    row_max = lax.fori_loop(
        first_step, last_step, score_step, jnp.full((heads * tok, 1), masked_value, F32)
    )

    def value_step(step, carry):
        row_total, weighted = carry
        weight = jnp.exp(score_ref[step] - row_max)
        row_total = row_total + jnp.sum(weight, axis=1, keepdims=True)
        weighted = weighted + mm(weight.astype(BF), kv_ref[0, keys_of(step), head:])
        return (row_total, weighted)

    row_total, weighted = lax.fori_loop(
        first_step,
        last_step,
        value_step,
        (jnp.zeros((heads * tok, 1), F32), jnp.zeros((heads * tok, head), F32)),
    )
    attend = weighted / row_total
    lane = lax.broadcasted_iota(jnp.int32, (tok, 128), 1)
    stats = jnp.zeros((tok, 128), F32)
    for h in range(heads):
        rows = slice(h * tok, (h + 1) * tok)
        out_ref[0, :, h * head : (h + 1) * head] = attend[rows]
        low_ref[0, :, h * head : (h + 1) * head] = attend[rows].astype(BF)
        stats = jnp.where(lane == h, row_max[rows], stats)
        stats = jnp.where(lane == heads + h, row_total[rows], stats)
    stats_ref[0] = stats


def attend_back_kernel(
    heads, scale, lens_ref, q_ref, kv_ref, branch_ref, proj_ref, branch_all_ref, low_ref, lat_ref, out_ref, stats_ref, cos_ref, sin_ref, dq_ref, dkv_ref, oq_ref, dq_all
):
    row = pl.program_id(0)
    tok = q_ref.shape[1]
    head = kv_ref.shape[2] // 2
    first_slot = lax.axis_index("seq") * tok
    slot, low, first_step, last_step = visible(lens_ref, row, first_slot, tok)
    slot = jnp.concatenate([slot] * heads, axis=0)
    low = jnp.concatenate([low] * heads, axis=0)
    query = stack_heads(q_ref[0], heads, head)
    branch = branch_ref[0]
    grad = jnp.concatenate(
        [mm_nt(branch, proj_ref[h * head : (h + 1) * head, :]) for h in range(heads)], axis=0
    )
    attend = stack_heads(out_ref[0], heads, head)
    stats = stats_ref[0]
    row_max = jnp.concatenate([stats[:, h : h + 1] for h in range(heads)], axis=0)
    row_total = jnp.concatenate(
        [stats[:, heads + h : heads + h + 1] for h in range(heads)], axis=0
    )
    grad_weighted = (grad / row_total).astype(BF)
    delta = jnp.sum(grad * attend, axis=1, keepdims=True) / row_total
    dkv_ref[...] = jnp.zeros_like(dkv_ref)

    def step_back(step, grad_query):
        keys = pl.ds(pl.multiple_of(step * KEYS, KEYS), KEYS)
        key, value = kv_ref[0, keys, :head], kv_ref[0, keys, head:]
        score = mm_nt(query, key) * scale
        key_slot = step * KEYS + lax.broadcasted_iota(jnp.int32, (1, KEYS), 1)
        allowed = (key_slot >= low) & (key_slot <= slot)
        weight = jnp.exp(jnp.where(allowed, score - row_max, masked_value))
        grad_weight = mm_nt(grad_weighted, value)
        grad_score = (weight * (grad_weight - delta)).astype(BF)
        dkv_ref[0, keys, :head] = (mm_tn(grad_score, query) * scale).astype(BF)
        dkv_ref[0, keys, head:] = mm_tn(weight.astype(BF), grad_weighted).astype(BF)
        return grad_query + mm(grad_score, key)

    grad_query = lax.fori_loop(
        first_step, last_step, step_back, jnp.zeros((heads * tok, head), F32)
    )
    cosine, sine = cos_ref[0], sin_ref[0]
    for h in range(heads):
        dq_ref[0, :, h * head : (h + 1) * head] = rotate_back(
            grad_query[h * tok : (h + 1) * tok] * scale, cosine, sine
        ).astype(BF)
        dq_all[row, :, h * head : (h + 1) * head] = dq_ref[0, :, h * head : (h + 1) * head]

    @pl.when(row == pl.num_programs(0) - 1)
    def _():
        weight_grads(low_ref, branch_all_ref, lat_ref, dq_all, oq_ref)


def weight_grads(low_ref, branch_ref, lat_ref, dq_ref, oq_ref):
    model, width = branch_ref.shape[2], dq_ref.shape[2]
    lat = lat_ref.shape[2]
    rows, spread = lax.axis_size("row"), lax.axis_size("seq")
    own = lat // rows // spread
    right = branch_ref[...].reshape(-1, model)
    tile = 256

    def out_tile(t, carry):
        at = pl.ds(pl.multiple_of(t * tile, tile), tile)
        left = low_ref[:, :, at].reshape(-1, tile)
        oq_ref[at, :model] = mm_tn(left, right).astype(BF)
        return carry

    lax.fori_loop(0, low_ref.shape[2] // tile, out_tile, 0)
    right_lat = dq_ref[...].reshape(-1, width)
    block = lat // rows
    if own % 16 == 0:
        for r in range(rows):
            left = lat_ref[:, :, r * block : (r + 1) * block].reshape(-1, block)
            product = mm_tn(left, right_lat).astype(BF)
            for seq in range(spread):
                at = (seq * rows + r) * own
                oq_ref[at : at + own, model:] = product[seq * own : (seq + 1) * own]
    else:
        product = mm_tn(lat_ref[...].reshape(-1, lat), right_lat)
        for seq in range(spread):
            pieces = [
                product[(r * spread + seq) * own : (r * spread + seq + 1) * own] for r in range(rows)
            ]
            oq_ref[seq * rows * own : (seq + 1) * rows * own, model:] = jnp.concatenate(
                pieces, axis=0
            ).astype(BF)


def row_block(shape):
    return pl.BlockSpec((1,) + shape[1:], lambda i: (i, 0, 0))


def whole_block(shape):
    return pl.BlockSpec(shape, lambda i: (0,) * len(shape))


def kernel_params():
    return pltpu.CompilerParams(
        dimension_semantics=("arbitrary",), vmem_limit_bytes=VMEM_BYTES
    )


def attend_forward(heads, scale, lens, lat, qup, cosine, sine, kv):
    rows, tok, _ = lat.shape
    slots = kv.shape[1]
    wide = (rows, tok, qup.shape[1])
    flops = rows * tok * (2 * lat.shape[2] * qup.shape[1] + 4 * slots * qup.shape[1])
    return pl.pallas_call(
        functools.partial(attend_kernel, heads, scale),
        grid=(rows,),
        in_specs=[pl.BlockSpec(memory_space=pltpu.SMEM)]
        + [row_block(lat.shape), whole_block(qup.shape)]
        + [row_block(cosine.shape), row_block(sine.shape), row_block(kv.shape)],
        out_specs=[row_block(wide), row_block(wide), row_block(wide), row_block((rows, tok, 128))],
        out_shape=[
            jax.ShapeDtypeStruct(wide, BF),
            jax.ShapeDtypeStruct(wide, F32),
            jax.ShapeDtypeStruct(wide, BF),
            jax.ShapeDtypeStruct((rows, tok, 128), F32),
        ],
        scratch_shapes=[pltpu.VMEM((slots // KEYS, heads * tok, KEYS), F32)],
        compiler_params=kernel_params(),
        cost_estimate=pl.CostEstimate(
            flops=flops, bytes_accessed=16 * 1024 * 1024, transcendentals=rows * tok * heads * slots
        ),
        name="attend_forward",
    )(lens, lat, qup, cosine, sine, kv)


def attend_backward(
    heads, scale, lens, query, kv, branch, oq, low, lat, attend, stats, cosine, sine
):
    rows, tok, width = query.shape
    model = branch.shape[2]
    slots = kv.shape[1]
    return pl.pallas_call(
        functools.partial(attend_back_kernel, heads, scale),
        grid=(rows,),
        in_specs=[pl.BlockSpec(memory_space=pltpu.SMEM)]
        + [row_block(v.shape) for v in (query, kv, branch)]
        + [pl.BlockSpec((width, model), lambda i: (0, 0), pipeline_mode=pl.Buffered(1))]
        + [
            pl.BlockSpec(v.shape, lambda i: (0, 0, 0), pipeline_mode=pl.Buffered(1))
            for v in (branch, low, lat)
        ]
        + [row_block(v.shape) for v in (attend, stats, cosine, sine)],
        out_specs=[row_block(query.shape), row_block(kv.shape)]
        + [pl.BlockSpec(oq.shape, lambda i: (0, 0), pipeline_mode=pl.Buffered(1))],
        out_shape=[
            jax.ShapeDtypeStruct(query.shape, BF),
            jax.ShapeDtypeStruct(kv.shape, BF),
            jax.ShapeDtypeStruct(oq.shape, BF),
        ],
        scratch_shapes=[pltpu.VMEM(query.shape, BF)],
        compiler_params=kernel_params(),
        cost_estimate=pl.CostEstimate(
            flops=rows * tok * 10 * slots * width,
            bytes_accessed=100_000_000,
            transcendentals=rows * tok * heads * slots,
        ),
        name="attend_backward",
    )(lens, query, kv, branch, oq, branch, low, lat, attend, stats, cosine, sine)


MESH = pl.DeviceIdType.MESH


def partners():
    row, seq = lax.axis_index("row"), lax.axis_index("seq")
    return {1: (row + 1 - 2 * (row % 2), seq), 2: ((row + 2) % 4, seq), 3: (3 - row, seq)}


def chip_partners(chips):
    row, seq = lax.axis_index("row"), lax.axis_index("seq")
    later = [(row, (seq + 2 * i) % (2 * chips)) for i in range(1, chips)]
    return later, (row, seq + 1 - 2 * (seq % 2))


def greet(devices):
    barrier = pltpu.get_barrier_semaphore()
    for device in devices:
        pl.semaphore_signal(barrier, inc=1, device_id=device, device_id_type=MESH)
    pl.semaphore_wait(barrier, len(devices))


def send(source, target, sems, at, device):
    copy = pltpu.make_async_remote_copy(
        src_ref=source,
        dst_ref=target,
        send_sem=sems[0].at[at],
        recv_sem=sems[1].at[at],
        device_id=device,
        device_id_type=MESH,
    )
    copy.start()
    return copy


TILE = 512


def reduce_rows(product, near, parts, kept, landed, sems, ready=None):
    half = parts.shape[2]
    tiles = half // TILE

    def compute(k, side, store):
        if ready is not None:
            ready(k, side)

        def tile(t, carry):
            local = pl.ds(pl.multiple_of(t * TILE, TILE), TILE)
            columns = pl.ds(pl.multiple_of(side * half + t * TILE, TILE), TILE)
            store(local, columns, product(k, columns))
            return carry

        lax.fori_loop(0, tiles, tile, 0)

    def into_parts(at):
        def store(local, columns, value):
            parts[at, :, local] = value.astype(BF)

        return store

    def into_kept(at):
        def store(local, columns, value):
            kept[at, :, columns] = value

        return store

    tok = parts.shape[1]
    halves = [pl.ds(0, tok // 2), pl.ds(tok // 2, tok // 2)]
    copies = {}

    def move(at, part, to):
        rows = halves[part]
        copies[at, part] = send(
            parts.at[at, rows], landed.at[at, rows], sems, 2 * at + part, near[to]
        )

    def begin():
        for at, (k, side, to) in enumerate([(3, 0, 1), (3, 1, 2), (1, 0, 1), (2, 1, 2)]):
            compute(k, side, into_parts(at))
            for part in (0, 1):
                move(at, part, to)
        compute(2, 0, into_kept(1))
        compute(1, 1, into_kept(1))

    left, right = pl.ds(0, half), pl.ds(half, half)

    def pass_on():
        for part in (0, 1):
            rows = halves[part]
            for at, columns, to in ((0, left, 2), (1, right, 1)):
                copies[at, part].wait_recv()
                parts[4 + at, rows] = (
                    kept[1, rows, columns] + landed[at, rows].astype(F32)
                ).astype(BF)
                move(4 + at, part, to)

    def finish(done=None):
        compute(0, 0, into_kept(0))
        compute(0, 1, into_kept(0))
        for part in (0, 1):
            rows = halves[part]
            for first, then, columns in ((2, 4, left), (3, 5, right)):
                copies[first, part].wait_recv()
                copies[then, part].wait_recv()
                kept[0, rows, columns] = kept[0, rows, columns] + (
                    landed[first, rows].astype(F32) + landed[then, rows].astype(F32)
                )
            if done is not None:
                done(part, rows)
        for copy in copies.values():
            copy.wait_send()

    return begin, pass_on, finish


def gather_rows(mine, out, near, sems, local_sem, meanwhile=None):
    tok = mine.shape[0]
    low, high = pl.ds(0, tok // 2), pl.ds(tok // 2, tok // 2)
    own = pltpu.make_async_copy(mine, out.at[0], local_sem)
    own.start()
    first = send(mine.at[low], out.at[1, low], sems, 0, near[1])
    second = send(mine.at[high], out.at[2, high], sems, 1, near[2])
    third = send(mine.at[high], out.at[1, high], sems, 2, near[1])
    fourth = send(mine.at[low], out.at[2, low], sems, 3, near[2])
    if meanwhile is not None:
        meanwhile()
    first.wait_recv()
    fifth = send(out.at[1, low], out.at[3, low], sems, 4, near[2])
    second.wait_recv()
    sixth = send(out.at[2, high], out.at[3, high], sems, 5, near[1])
    for copy in (third, fourth, fifth, sixth):
        copy.wait_recv()
    for copy in (first, second, third, fourth, fifth, sixth):
        copy.wait_send()
    own.wait()


def gather_halves(mine, out, near, sems, local_sem):
    tok = mine.shape[0]
    halves = [pl.ds(0, tok // 2), pl.ds(tok // 2, tok // 2)]
    copies = {}
    own = pltpu.make_async_copy(mine, out.at[0], local_sem)

    def start(part):
        rows = halves[part]
        for k in (1, 2):
            copies[k, part] = send(
                mine.at[rows], out.at[k, rows], sems, 2 * part + k - 1, near[k]
            )
        if part == 1:
            own.start()

    def complete():
        for k, part in ((1, 0), (2, 1)):
            rows = halves[part]
            copies[k, part].wait_recv()
            copies[3, part] = send(out.at[k, rows], out.at[3, rows], sems, 4 + part, near[3 - k])
        for at in ((1, 1), (2, 0), (3, 0), (3, 1)):
            copies[at].wait_recv()
        for copy in copies.values():
            copy.wait_send()
        own.wait()

    return start, complete


def exchange_scratch(tok, model):
    return [
        pltpu.VMEM((6, tok, model // 2), BF),
        pltpu.VMEM((6, tok, model // 2), BF),
        pltpu.VMEM((2, tok, model), F32),
        pltpu.VMEM((tok, model), BF),
        pltpu.SemaphoreType.DMA((12,)),
        pltpu.SemaphoreType.DMA((12,)),
        pltpu.SemaphoreType.DMA((6,)),
        pltpu.SemaphoreType.DMA((6,)),
        pltpu.SemaphoreType.DMA(()),
    ]


def branch_kernel(
    attend_ref, out_proj_ref, hidden_ref, gain_ref, middle_ref, second_ref, parts, landed, kept, mine, s1, r1, s2, r2, own
):
    near = partners()
    greet([near[1], near[2]])

    def product(k, columns):
        return mm(attend_ref[k], out_proj_ref[:, columns])

    start, complete = gather_halves(mine, second_ref, near, (s2, r2), own)
    begin, pass_on, finish = reduce_rows(product, near, parts, kept, landed, (s1, r1))

    def done(part, rows):
        middle = hidden_ref[rows].astype(F32) + kept[0, rows]
        middle_ref[rows] = middle
        mine[rows] = rms_forward(middle, gain_ref[...])[0].astype(BF)
        start(part)

    begin()
    pass_on()
    finish(done)
    complete()


def second_back_kernel(
    gate_hbm, up_hbm, ffn_hbm, act_hbm, down_hbm, middle_ref, cot_ref, gain_ref, order_ref, grad_ref, gain_grad_ref, branch_ref, layer_ref, parts, landed, kept, mine, s1, r1, s2, r2, own, both_ref, ffn_ref, act_ref, down_ref, load_sems
):
    del order_ref
    half = ffn_ref.shape[0] // 2
    loads = {}

    def load(name, source, target):
        loads[name] = pltpu.make_async_copy(source, target, load_sems.at[len(loads)])
        loads[name].start()

    units = gate_hbm.shape[2]

    def load_both(k):
        load(("gate", k), gate_hbm.at[k], both_ref.at[k, :, pl.ds(0, units)])
        load(("up", k), up_hbm.at[k], both_ref.at[k, :, pl.ds(units, units)])

    load_both(3)
    for side in (0, 1):
        rows = pl.ds(side * half, half)
        load(("ffn", side), ffn_hbm.at[rows], ffn_ref.at[rows])
    for k in (1, 2, 0):
        load_both(k)
    load("act", act_hbm, act_ref)
    load("down", down_hbm, down_ref)
    waited = set()

    def loaded(*names):
        for name in names:
            if name not in waited:
                waited.add(name)
                loads[name].wait()

    def ready(k, side):
        loaded(("gate", k), ("up", k), ("ffn", side))

    near = partners()
    greet([near[1], near[2]])

    def product(k, columns):
        return mm_nt(both_ref[k], ffn_ref[columns, :])

    begin, pass_on, finish = reduce_rows(product, near, parts, kept, landed, (s1, r1), ready)
    begin()
    pass_on()
    loaded("act", "down")
    for k in range(act_ref.shape[0]):

        def tile(t, carry, k=k):
            columns = pl.ds(pl.multiple_of(t * TILE, TILE), TILE)
            layer_ref[k, :, columns] = mm(act_ref[k], down_ref[:, columns]).astype(BF)
            return carry

        lax.fori_loop(0, down_ref.shape[1] // TILE, tile, 0)
    start, complete = gather_halves(mine, branch_ref, near, (s2, r2), own)
    gain = gain_ref[...]
    gain_grad_ref[...] = jnp.zeros_like(gain_grad_ref)

    def done(part, rows):
        grad_second = kept[0, rows]
        _, unit, inv = rms_forward(middle_ref[rows], gain)
        grad_middle = cot_ref[rows].astype(F32) + rms_backward(grad_second, unit, inv, gain)
        mine[rows] = grad_middle.astype(BF)
        start(part)
        grad_ref[rows] = grad_middle
        gain_grad_ref[...] = gain_grad_ref[...] + jnp.sum(grad_second * unit, axis=0, keepdims=True)

    finish(done)
    complete()


VMEM_SPEC = pl.BlockSpec(memory_space=pltpu.VMEM)
ANY_SPEC = pl.BlockSpec(memory_space=pl.ANY)


def remote_params(collective_id):
    return pltpu.CompilerParams(
        collective_id=collective_id, has_side_effects=True, vmem_limit_bytes=VMEM_BYTES
    )


def branch_exchange(attend, out_proj, hidden, gain):
    rows, tok, width = attend.shape
    model = hidden.shape[1]
    return pl.pallas_call(
        branch_kernel,
        in_specs=[VMEM_SPEC] * 4,
        out_specs=[VMEM_SPEC, ANY_SPEC],
        out_shape=[
            jax.ShapeDtypeStruct((tok, model), F32),
            jax.ShapeDtypeStruct((rows, tok, model), BF),
        ],
        scratch_shapes=exchange_scratch(tok, model),
        compiler_params=remote_params(1),
        cost_estimate=pl.CostEstimate(
            flops=2 * rows * tok * width * model, bytes_accessed=190_000_000, transcendentals=0
        ),
        name="branch_exchange",
    )(attend, out_proj, hidden, gain)


def second_exchange(gate, up, ffn, act, down, middle, cotangent, gain, order):
    rows, tok, units = gate.shape
    model = ffn.shape[0]
    return pl.pallas_call(
        second_back_kernel,
        in_specs=[ANY_SPEC] * 5 + [VMEM_SPEC] * 3 + [ANY_SPEC],
        out_specs=[VMEM_SPEC, VMEM_SPEC, ANY_SPEC, VMEM_SPEC],
        out_shape=[
            jax.ShapeDtypeStruct((tok, model), F32),
            jax.ShapeDtypeStruct((1, model), F32),
            jax.ShapeDtypeStruct((rows, tok, model), BF),
            jax.ShapeDtypeStruct((rows, tok, model), BF),
        ],
        scratch_shapes=exchange_scratch(tok, model)
        + [pltpu.VMEM(shape, BF) for shape in ((rows, tok, 2 * units), ffn.shape, act.shape, down.shape)]
        + [pltpu.SemaphoreType.DMA((12,))],
        compiler_params=remote_params(2),
        cost_estimate=pl.CostEstimate(
            flops=6 * rows * tok * units * model, bytes_accessed=190_000_000, transcendentals=0
        ),
        name="second_exchange",
    )(gate, up, ffn, act, down, middle, cotangent, gain, order)


def tail_kernel(
    dq_ref, qup_ref, dkv_ref, latent_ref, lgain_ref, cos_ref, sin_ref, first_ref, hidden_ref, again_ref, grads_ref, lgain_part_ref, again_part_ref, ours, theirs, kv_landed, z_landed, parts, landed, kept, pieces, grads, sc, rc, sk, rk, sz, rz, sl, rl, sg, rg, own_sem
):
    rows, chips, tok, wide = ours.shape
    head = wide // 2
    lat = latent_ref.shape[1]
    width = pieces.shape[2]
    row, seq = lax.axis_index("row"), lax.axis_index("seq")
    core, chip = seq % 2, seq // 2
    near = partners()
    later, twin = chip_partners(chips)
    greet([near[1], near[2], near[3]] + later + [twin])

    swap = send(dkv_ref.at[:, :, 1 - core], theirs, (sc, rc), 0, twin)
    load = pltpu.make_async_copy(dkv_ref.at[:, :, core], ours, own_sem)
    load.start()
    left, right = slice(0, head), slice(head, wide)

    def latent_product(k, columns):
        return mm_nt(dq_ref[k], qup_ref[columns, :])

    begin, pass_on, finish = reduce_rows(latent_product, near, parts, kept, landed, (sl, rl))
    load.wait()
    swap.wait_recv()

    blocks = [(chip + i) % chips for i in range(1, chips)] + [chip]
    steps, along = {}, []

    def add(k, block, side, other):
        value = ours[k, block, :, side].astype(F32) + other.astype(F32)
        ours[k, block, :, side] = value.astype(BF)

    def move(n, at, k, side, to):
        source = ours.at[k, blocks[n], :, side]
        steps[n, at] = send(source, kv_landed.at[at, n], (sk, rk), 6 * n + at, near[to])

    def first(n):
        for at, (k, side, to) in enumerate(
            [(3, left, 1), (3, right, 2), (1, left, 1), (2, right, 2)]
        ):
            add(k, blocks[n], side, theirs[k, blocks[n], :, side])
            move(n, at, k, side, to)
        for k, side in ((2, left), (1, right), (0, left), (0, right)):
            add(k, blocks[n], side, theirs[k, blocks[n], :, side])

    def second(n):
        steps[n, 0].wait_recv()
        add(2, blocks[n], left, kv_landed[0, n])
        move(n, 4, 2, left, 2)
        steps[n, 1].wait_recv()
        add(1, blocks[n], right, kv_landed[1, n])
        move(n, 5, 1, right, 1)

    def third(n):
        for at, side in ((2, left), (3, right), (4, left), (5, right)):
            steps[n, at].wait_recv()
            add(0, blocks[n], side, kv_landed[at, n])
        if n < chips - 1:
            along.append(send(ours.at[0, blocks[n]], z_landed.at[n], (sz, rz), n, later[n]))

    for n in range(chips + 1):
        if n < chips:
            first(n)
        if n >= 1:
            second(n - 1)
        if n >= 2:
            third(n - 2)
    begin()
    third(chips - 1)
    pass_on()
    finish()
    grad_latent_norm = kept[0]
    lgain = lgain_ref[...]
    _, unit, inv = rms_forward(latent_ref[...], lgain)
    lgain_part_ref[...] = jnp.sum(grad_latent_norm * unit, axis=0, keepdims=True)
    grad_latent = rms_backward(grad_latent_norm, unit, inv, lgain)
    total = ours[0, chip].astype(F32)
    for i in range(1, chips):
        along[i - 1].wait_recv()
        total = total + z_landed[i - 1].astype(F32)
    grad_key = rotate_back(total[:, :head], cos_ref[...], sin_ref[...])
    joined = jnp.concatenate([grad_latent, grad_key, total[:, head:]], axis=1).astype(BF)
    for j in range(rows):
        pieces[j] = joined[:, j * width : (j + 1) * width]
    last = [
        send(pieces.at[near[k][0]], grads.at[k], (sg, rg), k - 1, near[k]) for k in range(1, rows)
    ]
    grads[0] = pieces[row]
    tiles = again_ref.shape[1] // TILE
    again_part_ref[...] = jnp.zeros_like(again_part_ref)
    for k in range(rows):
        if k:
            last[k - 1].wait_recv()
        grads_ref[k] = grads[k]
        values = hidden_ref[k].astype(F32)
        scale = lax.rsqrt(jnp.mean(values * values, axis=-1, keepdims=True) + epsilon)

        def tile(t, carry):
            columns = pl.ds(pl.multiple_of(t * TILE, TILE), TILE)
            part = mm_nt(grads[k], first_ref[columns, :width])
            part = part * (hidden_ref[k, :, columns].astype(F32) * scale)
            again_part_ref[:, columns] = again_part_ref[:, columns] + jnp.sum(
                part, axis=0, keepdims=True
            )
            return carry

        lax.fori_loop(0, tiles, tile, 0)
    for copy in [swap] + list(steps.values()) + along + last:
        copy.wait_send()


def tail_exchange(
    dq, qup, dkv, latent, lgain, cosine, sine, first_set, hidden_all, again, width
):
    rows, chips, _, tok, wide = dkv.shape
    lat = latent.shape[1]
    model = again.shape[1]
    dma = pltpu.SemaphoreType.DMA
    return pl.pallas_call(
        tail_kernel,
        in_specs=[VMEM_SPEC] * 2 + [ANY_SPEC] + [VMEM_SPEC] * 7,
        out_specs=[VMEM_SPEC] * 3,
        out_shape=[
            jax.ShapeDtypeStruct((rows, tok, width), BF),
            jax.ShapeDtypeStruct((1, lat), F32),
            jax.ShapeDtypeStruct((1, model), F32),
        ],
        scratch_shapes=[
            pltpu.VMEM((rows, chips, tok, wide), BF),
            pltpu.VMEM((rows, chips, tok, wide), BF),
            pltpu.VMEM((6, chips, tok, wide // 2), BF),
            pltpu.VMEM((chips - 1, tok, wide), BF),
            pltpu.VMEM((6, tok, lat // 2), BF),
            pltpu.VMEM((6, tok, lat // 2), BF),
            pltpu.VMEM((2, tok, lat), F32),
            pltpu.VMEM((rows, tok, width), BF),
            pltpu.VMEM((rows, tok, width), BF),
        ]
        + [dma((n,)) for n in (1, 6 * chips, chips - 1, 12, 3) for _ in range(2)]
        + [dma(())],
        compiler_params=remote_params(4),
        cost_estimate=pl.CostEstimate(
            flops=2 * rows * tok * lat * qup.shape[1] + 2 * rows * tok * width * model,
            bytes_accessed=230_000_000,
            transcendentals=0,
        ),
        name="tail_exchange",
    )(dq, qup, dkv, latent, lgain, cosine, sine, first_set, hidden_all, again)


def hidden_back_kernel(
    grads_ref, first_ref, hidden_ref, again_ref, middle_ref, term_ref, out_ref, grad_ref, gain_ref, parts, landed, kept, ours, theirs, z_landed, total, back, s1, r1, sc, rc, sz, rz, sb, rb, own
):
    rows, chips = ours.shape[:2]
    width = grads_ref.shape[2]
    row, seq = lax.axis_index("row"), lax.axis_index("seq")
    core, chip = seq % 2, seq // 2
    near = partners()
    later, twin = chip_partners(chips)
    greet([near[1], near[2], near[3]] + later + [twin])
    swap = send(term_ref.at[:, :, 1 - core], theirs, (sc, rc), 0, twin)
    load = pltpu.make_async_copy(term_ref.at[:, :, core], ours, own)
    load.start()

    def product(k, columns):
        return mm_nt(grads_ref[k], first_ref[columns, :width])

    begin, pass_on, finish = reduce_rows(product, near, parts, kept, landed, (s1, r1))
    begin()
    load.wait()
    swap.wait_recv()
    ours[...] = (ours[...].astype(F32) + theirs[...].astype(F32)).astype(BF)
    along = [
        send(ours.at[:, (chip + i) % chips], z_landed.at[i - 1], (sz, rz), i - 1, later[i - 1])
        for i in range(1, chips)
    ]
    pass_on()
    finish()
    again = again_ref[...]
    _, unit, inv = rms_forward(hidden_ref[...].astype(F32), again)
    out_ref[...] = middle_ref[...] + rms_backward(kept[0], unit, inv, again)
    sums = ours[:, chip].astype(F32)
    for i in range(1, chips):
        along[i - 1].wait_recv()
        sums = sums + z_landed[i - 1].astype(F32)
    total[...] = sums.astype(BF)
    last = [
        send(total.at[near[k][0]], back.at[row], (sb, rb), k - 1, near[k]) for k in range(1, rows)
    ]
    back[row] = total[row]
    for copy in last:
        copy.wait_recv()
    gain_ref[...] = jnp.zeros_like(gain_ref)
    for j in range(rows):
        grad_ref[:, j * width : (j + 1) * width] = back[j, :, :width].astype(F32)
        gain_ref[...] = gain_ref[...] + back[j, :, width:].astype(F32)
    for copy in [swap] + along + last:
        copy.wait_send()


def hidden_exchange(grads, first_set, hidden, again, grad_middle, term):
    rows, tok, width = grads.shape
    model = again.shape[1]
    _, chips, _, own, wide = term.shape
    dma = pltpu.SemaphoreType.DMA
    return pl.pallas_call(
        hidden_back_kernel,
        in_specs=[VMEM_SPEC] * 5 + [ANY_SPEC],
        out_specs=[VMEM_SPEC] * 3,
        out_shape=[
            jax.ShapeDtypeStruct((tok, model), F32),
            jax.ShapeDtypeStruct((own, rows * width), F32),
            jax.ShapeDtypeStruct((own, wide - width), F32),
        ],
        scratch_shapes=exchange_scratch(tok, model)[:3]
        + [
            pltpu.VMEM((rows, chips, own, wide), BF),
            pltpu.VMEM((rows, chips, own, wide), BF),
            pltpu.VMEM((chips - 1, rows, own, wide), BF),
            pltpu.VMEM((rows, own, wide), BF),
            pltpu.VMEM((rows, own, wide), BF),
        ]
        + [dma((n,)) for n in (12, 1, chips - 1, 3) for _ in range(2)]
        + [dma(())],
        compiler_params=remote_params(5),
        cost_estimate=pl.CostEstimate(
            flops=2 * rows * tok * width * model, bytes_accessed=110_000_000, transcendentals=0
        ),
        name="hidden_exchange",
    )(grads, first_set, hidden, again, grad_middle, term)


def last_kernel(oq_ref, back, s1, r1, own):
    rows, _, wide = back.shape
    row = lax.axis_index("row")
    columns = pl.ds(oq_ref.shape[2] - wide, wide)
    near = partners()
    greet([near[1], near[2], near[3]])
    copies = [
        send(oq_ref.at[near[k][0], :, columns], back.at[row], (s1, r1), k - 1, near[k])
        for k in range(1, rows)
    ]
    copies.append(pltpu.make_async_copy(oq_ref.at[row, :, columns], back.at[row], own))
    copies[-1].start()
    for copy in copies:
        copy.wait()


def last_exchange(oq, model):
    rows, own, total = oq.shape
    dma = pltpu.SemaphoreType.DMA
    return pl.pallas_call(
        last_kernel,
        in_specs=[VMEM_SPEC],
        out_specs=VMEM_SPEC,
        out_shape=jax.ShapeDtypeStruct((rows, own, total - model), BF),
        scratch_shapes=[dma((3,)), dma((3,)), dma(())],
        compiler_params=remote_params(8),
        cost_estimate=pl.CostEstimate(flops=0, bytes_accessed=10_000_000, transcendentals=0),
        name="last_exchange",
    )(oq)


def start_kernel(
    hidden_ref, gate_ref, up_ref, cut_ref, all_ref, ffn_ref, first_ref, s1, r1, sg, rg, sz, rz, sc, rc, own, own_ffn, own_cut
):
    row = lax.axis_index("row")
    rows = all_ref.shape[0]
    units = ffn_ref.shape[2] // 2
    chips = first_ref.shape[1]
    seq = lax.axis_index("seq")
    core, chip = seq % 2, seq // 2
    near = partners()
    later, twin = chip_partners(chips)
    greet([near[1], near[2], near[3]] + later + [twin])
    place = first_ref.at[:, chip, core]
    keep = pltpu.make_async_copy(cut_ref, place, own_cut)
    keep.start()
    along = [send(cut_ref, place, (sz, rz), i - 1, later[i - 1]) for i in range(1, chips)]
    shared = [send(cut_ref, place, (sc, rc), 0, twin)]
    cut = []

    def slices():
        for at, source_ref in ((0, gate_ref), (1, up_ref)):
            for k in range(rows):
                to = row if k == 0 else near[k][0]
                source = source_ref.at[:, pl.ds(pl.multiple_of(to * units, 128), units)]
                target = ffn_ref.at[row, :, pl.ds(at * units, units)]
                if k == 0:
                    copy = pltpu.make_async_copy(source, target, own_ffn.at[at])
                    copy.start()
                else:
                    copy = send(source, target, (sg, rg), 3 * at + k - 1, near[k])
                cut.append(copy)

    gather_rows(hidden_ref, all_ref, near, (s1, r1), own, slices)
    for i in range(1, chips):
        along[i - 1].wait_recv()
        block = first_ref.at[:, (chip + chips - i) % chips, core]
        shared.append(send(block, block, (sc, rc), i, twin))
    keep.wait()
    for copy in cut:
        copy.wait()
    for copy in shared:
        copy.wait_recv()
    for copy in along + shared:
        copy.wait_send()


def start_exchange(hidden, gate, up, first_cut, chips):
    rows, own, wide = first_cut.shape
    dma = pltpu.SemaphoreType.DMA
    return pl.pallas_call(
        start_kernel,
        in_specs=[ANY_SPEC] * 4,
        out_specs=[ANY_SPEC] * 3,
        out_shape=[
            jax.ShapeDtypeStruct((rows,) + hidden.shape, BF),
            jax.ShapeDtypeStruct((rows, gate.shape[0], 2 * gate.shape[1] // rows), BF),
            jax.ShapeDtypeStruct((rows, chips, 2, own, wide), BF),
        ],
        scratch_shapes=[dma((n,)) for n in (6, 6, chips - 1, chips) for _ in range(2)]
        + [dma(()), dma((2,)), dma(())],
        compiler_params=remote_params(6),
        cost_estimate=pl.CostEstimate(flops=0, bytes_accessed=120_000_000, transcendentals=0),
        name="start_exchange",
    )(hidden, gate, up, first_cut)


def front_kernel(
    hidden_ref, first_ref, again_ref, lgain_ref, cos_ref, sin_ref, latent_ref, lat_all_ref, kv_ref, first_low, pieces, landed, lat_mine, kv_mine, sa, ra, sl, rl, sz, rz, sr, rr, sf, rf, sc, rc, own_sem
):
    rows, tok, model = hidden_ref.shape
    chips = kv_ref.shape[1]
    width = pieces.shape[2]
    lat = latent_ref.shape[1]
    head = kv_ref.shape[4] // 2
    row, seq = lax.axis_index("row"), lax.axis_index("seq")
    core, chip = seq % 2, seq // 2
    near = partners()
    later, twin = chip_partners(chips)
    greet([near[1], near[2], near[3]] + later + [twin])

    again = again_ref[...]
    copies = []
    for k in (3, 2, 1, 0):
        first_low[...] = rms_forward(hidden_ref[k].astype(F32), again)[0].astype(BF)
        piece = mm(first_low[...], first_ref[:, :width]).astype(BF)
        if k:
            pieces[k] = piece
            copies.append(send(pieces.at[k], landed.at[row], (sa, ra), k - 1, near[k]))
        else:
            landed[row] = piece
    for copy in copies:
        copy.wait_recv()
    joined = jnp.concatenate([landed[j] for j in range(rows)], axis=1)
    key = rotate(joined[:, lat : lat + head].astype(F32), cos_ref[...], sin_ref[...])
    kv_mine[:, :head] = key.astype(BF)
    kv_mine[:, head:] = joined[:, lat + head :]

    own = pltpu.make_async_copy(kv_mine, kv_ref.at[0, chip, core], own_sem.at[0])
    own.start()
    along = [
        send(kv_mine, kv_ref.at[0, chip, core], (sz, rz), i - 1, later[i - 1])
        for i in range(1, chips)
    ]
    low, high = pl.ds(0, tok // 2), pl.ds(tok // 2, tok // 2)
    across, passed = [], []

    def block(i):
        return (chip + chips - i) % chips

    def spread(i):
        source = kv_mine if i == 0 else kv_ref.at[0, block(i), core]
        for k in (1, 2):
            across.append(
                send(source, kv_ref.at[k, block(i), core], (sr, rr), 2 * i + k - 1, near[k])
            )

    def pass_on(i):
        across[2 * i].wait_recv()
        source = kv_ref.at[1, block(i), core, low]
        passed.append(send(source, kv_ref.at[3, block(i), core, low], (sf, rf), 2 * i, near[2]))
        across[2 * i + 1].wait_recv()
        source = kv_ref.at[2, block(i), core, high]
        passed.append(
            send(source, kv_ref.at[3, block(i), core, high], (sf, rf), 2 * i + 1, near[1])
        )

    spread(0)
    latent = joined[:, :lat].astype(F32)
    latent_ref[...] = latent
    lat_mine[...] = rms_forward(latent, lgain_ref[...])[0].astype(BF)
    lat_own = pltpu.make_async_copy(lat_mine, lat_all_ref.at[0], own_sem.at[1])
    lat_own.start()
    lat_copies = [
        send(lat_mine, lat_all_ref.at[k], (sl, rl), k - 1, near[k]) for k in range(1, rows)
    ]
    for i in range(1, chips):
        along[i - 1].wait_recv()
        spread(i)
        pass_on(i - 1)
    own.wait()
    shared = [send(kv_ref.at[0, :, core], kv_ref.at[0, :, core], (sc, rc), 0, twin)]
    pass_on(chips - 1)
    for k in (1, 2):
        shared.append(send(kv_ref.at[k, :, core], kv_ref.at[k, :, core], (sc, rc), k, twin))
    for copy in passed:
        copy.wait_recv()
    shared.append(send(kv_ref.at[3, :, core], kv_ref.at[3, :, core], (sc, rc), 3, twin))
    for copy in lat_copies + shared:
        copy.wait_recv()
    for copy in copies + along + across + passed + lat_copies + shared:
        copy.wait_send()
    lat_own.wait()


def front_exchange(hidden_all, first_set, again, lgain, cosine, sine, chips, width, head):
    rows, tok, model = hidden_all.shape
    lat = lgain.shape[1]
    dma = pltpu.SemaphoreType.DMA
    pairs = [3, 3, chips - 1, 2 * chips, 2 * chips, 4]
    return pl.pallas_call(
        front_kernel,
        in_specs=[VMEM_SPEC] * 6,
        out_specs=[VMEM_SPEC, ANY_SPEC, ANY_SPEC],
        out_shape=[
            jax.ShapeDtypeStruct((tok, lat), F32),
            jax.ShapeDtypeStruct((rows, tok, lat), BF),
            jax.ShapeDtypeStruct((rows, chips, 2, tok, 2 * head), BF),
        ],
        scratch_shapes=[
            pltpu.VMEM((tok, model), BF),
            pltpu.VMEM((rows, tok, width), BF),
            pltpu.VMEM((rows, tok, width), BF),
            pltpu.VMEM((tok, lat), BF),
            pltpu.VMEM((tok, 2 * head), BF),
        ]
        + [dma((n,)) for n in pairs for _ in range(2)]
        + [dma((2,))],
        compiler_params=remote_params(3),
        cost_estimate=pl.CostEstimate(
            flops=2 * rows * tok * model * width, bytes_accessed=230_000_000, transcendentals=0
        ),
        name="front_exchange",
    )(hidden_all, first_set, again, lgain, cosine, sine)


def deal_kernel(first_ref, qup_ref, lens_ref, cut_ref, qup_cut_ref, lens_all, sf, rf, sq, rq, sl, rl, own):
    row = lax.axis_index("row")
    rows, _, wide = cut_ref.shape
    units = qup_cut_ref.shape[2]
    near = partners()
    greet([near[1], near[2], near[3]])
    copies = []
    for k in (3, 1, 2, 0):
        to = row if k == 0 else near[k][0]
        moves = [
            (first_ref.at[to], cut_ref.at[row], (sf, rf)),
            (
                qup_ref.at[:, pl.ds(pl.multiple_of(to * units, 128), units)],
                qup_cut_ref.at[row],
                (sq, rq),
            ),
            (lens_ref, lens_all.at[k], (sl, rl)),
        ]
        for at, (source, target, sems) in enumerate(moves):
            if k:
                copies.append(send(source, target, sems, k - 1, near[k]))
            else:
                copies.append(pltpu.make_async_copy(source, target, own.at[at]))
                copies[-1].start()
    for copy in copies:
        copy.wait()


def deal_exchange(first, qup, lens):
    rows = first.shape[0]
    dma = pltpu.SemaphoreType.DMA
    return pl.pallas_call(
        deal_kernel,
        in_specs=[VMEM_SPEC] * 3,
        out_specs=[VMEM_SPEC] * 3,
        out_shape=[
            jax.ShapeDtypeStruct(first.shape, BF),
            jax.ShapeDtypeStruct((rows, qup.shape[0], qup.shape[1] // rows), BF),
            jax.ShapeDtypeStruct((rows,) + lens.shape, lens.dtype),
        ],
        scratch_shapes=[dma((3,))] * 6 + [dma((3,))],
        compiler_params=remote_params(7),
        cost_estimate=pl.CostEstimate(flops=0, bytes_accessed=10_000_000, transcendentals=0),
        name="deal_exchange",
    )(first, qup, lens)


def ffn_grad_kernel(second_ref, gate_hbm, up_hbm, out_ref, both, mine, theirs, ss, rs, load_sems, out_sems):
    rows = mine.shape[0]
    units = gate_hbm.shape[1]
    block = second_ref.shape[1] // rows
    row = lax.axis_index("row")
    core = lax.axis_index("seq") % 2
    _, twin = chip_partners(mine.shape[1])
    loads = [
        pltpu.make_async_copy(gate_hbm, both.at[:, pl.ds(0, units)], load_sems.at[0]),
        pltpu.make_async_copy(up_hbm, both.at[:, pl.ds(units, units)], load_sems.at[1]),
    ]
    for copy in loads:
        copy.start()
    greet([twin])
    for copy in loads:
        copy.wait()

    def swap(r):
        return pltpu.make_async_remote_copy(
            src_ref=mine.at[r, :, 1 - core],
            dst_ref=theirs.at[r],
            send_sem=ss.at[r],
            recv_sem=rs.at[r],
            device_id=twin,
            device_id_type=MESH,
        )

    def compute(r, carry):
        owner = 2 * ((row // 2 + r // 2) % 2) + (row + r) % 2
        left = second_ref[:, pl.ds(pl.multiple_of(owner * block, block), block)]
        mine[r] = mm_tn(left, both[...]).astype(BF).reshape(mine.shape[1:])
        swap(r).start()
        return carry

    lax.fori_loop(0, rows, compute, 0)
    outs = []
    for r in range(rows):
        swap(r).wait_recv()
        theirs[r] = (mine[r, :, core].astype(F32) + theirs[r].astype(F32)).astype(BF)
        outs.append(pltpu.make_async_copy(theirs.at[r], out_ref.at[r], out_sems.at[r]))
        outs[-1].start()
    for r in range(rows):
        swap(r).wait_send()
        outs[r].wait()


def ffn_grad(second, gate, up, rows, chips):
    tokens, model = second.shape
    units = gate.shape[1]
    own = model // rows // chips // 2
    dma = pltpu.SemaphoreType.DMA
    return pl.pallas_call(
        ffn_grad_kernel,
        in_specs=[VMEM_SPEC] + [ANY_SPEC] * 2,
        out_specs=ANY_SPEC,
        out_shape=jax.ShapeDtypeStruct((rows, chips, own, 2 * units), BF),
        scratch_shapes=[
            pltpu.VMEM((tokens, 2 * units), BF),
            pltpu.VMEM((rows, chips, 2, own, 2 * units), BF),
            pltpu.VMEM((rows, chips, own, 2 * units), BF),
        ]
        + [dma((rows,)), dma((rows,)), dma((2,)), dma((rows,))],
        compiler_params=remote_params(9),
        cost_estimate=pl.CostEstimate(
            flops=4 * tokens * units * model, bytes_accessed=40_000_000, transcendentals=0
        ),
        name="ffn_grad",
    )(second, gate, up)


def move_row(value, k, rows):
    return lax.ppermute(value, "row", [(i, i ^ k) for i in range(rows)])


def in_row_order(pieces):
    rows, me = lax.axis_size("row"), lax.axis_index("row")
    return jnp.stack(
        [lax.select_n(me, *[pieces[j ^ i] for i in range(rows)]) for j in range(rows)]
    )


def join_columns(blocks):
    rows, n, width = blocks.shape
    return blocks.transpose(1, 0, 2).reshape(n, rows * width)


def scatter_seq(v, axis=0):
    return lax.psum_scatter(v.astype(BF), "seq", scatter_dimension=axis, tiled=True)


def on_device(
    hidden,
    cotangent,
    lengths,
    attn_gain,
    query_down,
    latent_gain,
    query_up,
    key_proj,
    value_proj,
    out_proj,
    ffn_gain,
    gate_proj,
    up_proj,
    down_proj,
):
    tok = hidden.shape[1]
    model = hidden.shape[2]
    rows = lax.axis_size("row")
    spread = lax.axis_size("seq")
    row_index = lax.axis_index("row")
    seq_index = lax.axis_index("seq")
    first_slot = seq_index * tok
    head = key_proj.shape[1]
    lat = query_down.shape[1]
    heads = query_up.shape[1] // head // rows
    units = down_proj.shape[0] * spread
    scale = head ** (-0.5)
    own = query_down.shape[0]
    lat_own = latent_gain.shape[0]

    first_own = jnp.concatenate([query_down, key_proj, value_proj], axis=1)
    first_width = first_own.shape[1] // rows
    gain_own = jnp.stack([attn_gain, ffn_gain, jnp.pad(latent_gain, (0, own - lat_own))], axis=1)
    gain_own = jnp.pad(gain_own, ((0, 0), (0, 125)))
    first_own = jnp.stack(
        [
            jnp.concatenate([first_own[:, j * first_width : (j + 1) * first_width], gain_own], axis=1)
            for j in range(rows)
        ]
    )
    docs = lengths.shape[1]
    first_cut, qup_cut, lens = deal_exchange(
        first_own, query_up, jnp.pad(lengths, ((0, 0), (0, 128 - docs)))
    )
    lens = lens[:, 0, :docs]
    oq_own = jnp.concatenate([out_proj, qup_cut.reshape(out_proj.shape[0], -1)], axis=1)
    full_oq = lax.all_gather(oq_own, "seq", axis=0, tiled=True)
    hidden_all, ffn_cut, first_set = start_exchange(
        hidden[0], gate_proj, up_proj, first_cut, spread // 2
    )
    first_set = first_set.reshape(model, -1)
    full_ffn = lax.all_gather(ffn_cut, "seq", axis=1, tiled=True).reshape(model, -1)
    full_down = lax.all_gather(down_proj, "seq", axis=0, tiled=True)
    full_gains = first_set[:, first_width:].astype(F32)
    full_again = full_gains[:, 0]
    full_fgain = full_gains[:, 1]
    full_lgain = full_gains[:, 2].reshape(rows * spread, own)[:, :lat_own].reshape(lat)
    full_qup = full_oq[:, model:].reshape(spread, rows, lat_own, -1).transpose(1, 0, 2, 3)
    full_qup = full_qup.reshape(lat, heads * head)
    position = document_positions(lens, first_slot + jnp.arange(tok, dtype=jnp.int32))
    cosine, sine = rope_tables(position, head)

    residual_all = hidden_all.astype(F32)
    first_low = rms_forward(residual_all, full_again)[0].astype(BF).reshape(rows * tok, model)
    latent, latent_all, key_value = front_exchange(
        hidden_all,
        first_set,
        full_again[None],
        full_lgain[None],
        cosine[0],
        sine[0],
        spread // 2,
        first_width,
        head,
    )
    key_value = key_value.reshape(rows, spread * tok, 2 * head)
    grad_own, latent_all = lax.optimization_barrier((cotangent[0], latent_all))
    grad_pieces = [move_row(grad_own, k, rows) for k in range(1, rows)]
    query_low, attend, attend_low, stats = attend_forward(
        heads, scale, lens, latent_all, full_qup, cosine, sine, key_value
    )
    middle, second_all = branch_exchange(attend_low, full_oq, hidden[0], full_fgain[None])
    grad_pieces, second_all = lax.optimization_barrier((grad_pieces, second_all))
    grad_all = jnp.stack([cotangent[0]] + grad_pieces).reshape(rows * tok, model)
    second_all = second_all.reshape(rows * tok, model)
    both = mm(second_all, full_ffn)
    gate_pre, upward = both[:, :units], both[:, units:]
    gate_sig = jax.nn.sigmoid(gate_pre)
    gate_act = gate_pre * gate_sig
    act_low = (gate_act * upward).astype(BF)
    down_part = mm_tn(act_low, grad_all).astype(BF)
    down_grad = scatter_seq(down_part)
    full_down, down_order = lax.optimization_barrier((full_down, down_part))
    grad_act = mm_nt(grad_all, full_down)
    slope = gate_sig * (1.0 + gate_pre * (1.0 - gate_sig))
    grad_gate = (grad_act * upward * slope).astype(BF)
    grad_upward = (grad_act * gate_act).astype(BF)
    ffn_term = ffn_grad(second_all, grad_gate, grad_upward, rows, spread // 2)
    ffn_part = lax.psum_scatter(
        ffn_term.reshape(rows, model // rows // 2, -1),
        "seq",
        scatter_dimension=1,
        axis_index_groups=[list(range(core, spread, 2)) for core in range(2)],
        tiled=True,
    )
    grad_gate, ffn_term = lax.optimization_barrier((grad_gate, ffn_term))
    grad_middle, ffn_gain_part, branch_all, layer_part = second_exchange(
        grad_gate.reshape(rows, tok, units),
        grad_upward.reshape(rows, tok, units),
        full_ffn,
        act_low.reshape(rows, tok, units),
        full_down,
        middle,
        cotangent[0],
        full_fgain[None],
        down_order,
    )
    ffn_gain_part = ffn_gain_part[0]
    layer_pieces = [move_row(layer_part[k], k, rows) for k in range(1, rows)]
    grad_query, kv_part, oq_part = attend_backward(
        heads,
        scale,
        lens,
        query_low,
        key_value,
        branch_all,
        full_oq,
        attend_low,
        latent_all,
        attend,
        stats,
        cosine,
        sine,
    )
    grad_query, oq_part, down_grad, layer_pieces = lax.optimization_barrier(
        (grad_query, oq_part, down_grad, layer_pieces)
    )
    oq_part = scatter_seq(oq_part)
    layer_sum = middle + layer_part[0].astype(F32)
    for piece in layer_pieces:
        layer_sum = layer_sum + piece.astype(F32)
    layer_out = layer_sum.astype(BF)
    grad_first_all, latent_gain_part, attn_gain_part = tail_exchange(
        grad_query,
        full_qup,
        kv_part.reshape(rows, spread // 2, 2, tok, 2 * head),
        latent,
        full_lgain[None],
        cosine[0],
        sine[0],
        first_set,
        hidden_all,
        full_again[None],
        first_width,
    )
    lgain_part = jnp.pad(
        latent_gain_part.reshape(rows * spread, lat_own), ((0, 0), (0, own - lat_own))
    ).reshape(model)
    gain_parts = jnp.stack([attn_gain_part[0], ffn_gain_part, lgain_part], axis=1)
    first_term = mm_tn(first_low, grad_first_all.reshape(rows * tok, first_width))
    first_term = jnp.concatenate(
        [first_term, jnp.pad(gain_parts, ((0, 0), (0, 125)))], axis=1
    ).astype(BF)
    grad_first_all, ffn_part = lax.optimization_barrier((grad_first_all, ffn_part))
    ffn_pieces = [ffn_part[0]] + [move_row(ffn_part[k], k, rows) for k in range(1, rows)]
    hidden_grad, first_grad, gain_grad = hidden_exchange(
        grad_first_all,
        first_set,
        hidden[0],
        full_again[None],
        grad_middle,
        first_term.reshape(rows, spread // 2, 2, own, -1),
    )
    hidden_grad, oq_part, ffn_pieces = lax.optimization_barrier((hidden_grad, oq_part, ffn_pieces))
    ffn_back = in_row_order(ffn_pieces)
    query_up_grad = last_exchange(oq_part.reshape(rows, lat_own, -1), model)
    query_up_grad = join_columns(query_up_grad).astype(F32)
    out_grad = oq_part[:, :model].astype(F32)
    gate_grad = join_columns(ffn_back[:, :, :units]).astype(F32)
    up_grad = join_columns(ffn_back[:, :, units:]).astype(F32)
    return (
        layer_out[None],
        hidden_grad[None],
        gain_grad[:, 0],
        first_grad[:, :lat],
        gain_grad[:lat_own, 2],
        query_up_grad,
        first_grad[:, lat : lat + head],
        first_grad[:, lat + head :],
        out_grad,
        gain_grad[:, 1],
        gate_grad,
        up_grad,
        down_grad.astype(F32),
    )


def solution(mesh):
    token = P("row", "seq", None)
    vector = P(("row", "seq"))
    matrix = P(("row", "seq"), None)
    return jax.shard_map(
        on_device,
        mesh=mesh,
        in_specs=(token, token, P("row", None), vector, matrix, vector)
        + (matrix,) * 4
        + (vector,)
        + (matrix,) * 3,
        out_specs=(token, token, vector, matrix, vector)
        + (matrix,) * 4
        + (vector,)
        + (matrix,) * 3,
        check_vma=False,
    )
```
